32 devices in a mesh: probe: 4 (over x, core), tile: 4 (over z), level: 2 (over y).
Axes of the slice: x: 2, y: 2, z: 4, core: 2. Of those that a mesh axis runs over, the one named last changes fastest.
Arguments:
- probe_bits: int32 [4, 64, 32, 256], P('probe', 'level', 'tile'), may hold values from 0 to 1
- kappa_sq: float32 [64, 32, 256], P('level', 'tile'), may hold values from 0.25 to 4
- observed: float32 [64, 32, 256], P('level', 'tile'), may hold values from -0.6 to 0.6
Outputs:
- gradient: float32 [64, 32, 256], P('level', 'tile', 'probe')
The draws below stay inside these ranges and needn't reach their ends.
Inputs may be any that keep to these rules, and one draw needn't show every extreme that they name: `probe_bits`: a probe's sign is 2 times its bit minus 1.
All inputs are finite; a program needn't handle non-finite values.
Results may differ from the reference program's by a relative error of at most 0.0003.
Values sent between devices are 32-bit elements; how exact they have to be, the bound alone decides.
No kernel may reach another device: no remote copies, remote signals or barrier semaphores. Data moves between devices by JAX's collectives and lax.ppermute only.
A program may use at most 64 MiB of HBM per device.

```python
import math
import jax
import jax.numpy as jnp
from jax import lax

NY = 256
ITERS = 4
PROBES = 4
NZ = 64
NX = 32


def plant(entries, own_key, smallest, high):
    dims = entries.shape
    spot = [jax.random.randint(jax.random.fold_in(own_key, axis), (), 0, dims[axis]) for axis in range(len(dims))]
    entries = entries.at[tuple(spot)].set(smallest)
    longest = dims.index(max(dims))
    spot[longest] = (spot[longest] + 1) % dims[longest]
    return entries.at[tuple(spot)].set(high)


def level_of(key, shape, split, smallest, top_value):
    def one(position, parts):
        heights = jax.random.uniform(jax.random.fold_in(jax.random.fold_in(key, 6), position), (parts,), jnp.float32, smallest / len(split), top_value / len(split))
        return jnp.repeat(jnp.exp(heights), shape[position] // parts).reshape((-1,) + (1,) * (len(shape) - position - 1))

    loudness = one(*split[0])
    for cut in split[1:]:
        loudness = loudness * one(*cut)
    return loudness


def noise(key, shape, deviation, most, pieces=(), kind=jnp.bfloat16):
    result = deviation * jax.random.normal(key, shape, jnp.float32)
    if pieces:
        result = result * level_of(key, shape, pieces, -0.22, 0.18)
    return jnp.clip(result, -most, most).astype(kind)


def setup_inputs(seed: int = 0) -> dict:
    keys = jax.random.split(jax.random.key(seed), 4)
    return {
        "probe_bits": plant(jax.random.randint(keys[0], (PROBES, NZ, NX, NY), 0, 2), jax.random.fold_in(keys[0], 1), 0, 1).astype(jnp.int32),
        "kappa_sq": jnp.clip(jnp.exp(math.log(4.0) - 2.7725887 * jax.random.uniform(keys[1], (NZ, NX, NY), jnp.float32) ** level_of(keys[1], (NZ, NX, NY), ((0, 2), (1, 4)), -0.2, 0.2)), 0.25, 4.0),
        "observed": noise(keys[2], (NZ, NX, NY), 0.1, 0.6, ((0, 2), (1, 4)), jnp.float32),
    }


VERTICAL = 2.0


def shift_levels(values, stride, level_dim, fill_value):
    level_count = values.shape[level_dim]
    widths = [(0, 0)] * values.ndim
    if stride > 0:
        widths[level_dim] = (stride, 0)
        padded = jnp.pad(values, widths, constant_values=fill_value)
        return lax.slice_in_dim(padded, 0, level_count, axis=level_dim)
    widths[level_dim] = (0, -stride)
    padded = jnp.pad(values, widths, constant_values=fill_value)
    return lax.slice_in_dim(padded, -stride, level_count - stride, axis=level_dim)


def reduction_tables(kappa_sq):
    level_count = kappa_sq.shape[0]
    level_ids = lax.broadcasted_iota(jnp.int32, kappa_sq.shape, 0)
    diagonal = kappa_sq + (4.0 + 2.0 * VERTICAL)
    lower = jnp.where(level_ids > 0, -VERTICAL, 0.0).astype(jnp.float32)
    upper = jnp.where(level_ids < level_count - 1, -VERTICAL, 0.0).astype(jnp.float32)
    tables = []
    stride = 1
    while stride < level_count:
        lower_ratio = -lower / shift_levels(diagonal, stride, 0, 1.0)
        upper_ratio = -upper / shift_levels(diagonal, -stride, 0, 1.0)
        new_diagonal = diagonal + lower_ratio * shift_levels(upper, stride, 0, 0.0) + upper_ratio * shift_levels(lower, -stride, 0, 0.0)
        new_lower = lower_ratio * shift_levels(lower, stride, 0, 0.0)
        upper = upper_ratio * shift_levels(upper, -stride, 0, 0.0)
        lower = new_lower
        diagonal = new_diagonal
        tables.append((lower_ratio, upper_ratio, stride))
        stride = stride * 2
    return tables, 1.0 / diagonal


def vertical_solve(values, tables, inverse_diagonal):
    for lower_ratio, upper_ratio, stride in tables:
        values = values + lower_ratio * shift_levels(values, stride, 1, 0.0) + upper_ratio * shift_levels(values, -stride, 1, 0.0)
    return values * inverse_diagonal


def stencil(padded, values, kappa_sq):
    beside_x = padded[:, 1:-1, 2:, 1:-1] + padded[:, 1:-1, :-2, 1:-1]
    beside_y = padded[:, 1:-1, 1:-1, 2:] + padded[:, 1:-1, 1:-1, :-2]
    beside_z = padded[:, 2:, 1:-1, 1:-1] + padded[:, :-2, 1:-1, 1:-1]
    return (kappa_sq + (4.0 + 2.0 * VERTICAL)) * values - beside_x - beside_y - VERTICAL * beside_z


def apply_k(values, kappa_sq):
    padded = jnp.pad(values, ((0, 0), (1, 1), (1, 1), (1, 1)))
    return stencil(padded, values, kappa_sq)


def reference(probe_bits, kappa_sq, observed):
    tables, inverse_diagonal = reduction_tables(kappa_sq)

    def apply_m(values):
        return vertical_solve(vertical_solve(values, tables, inverse_diagonal), tables, inverse_diagonal)

    def apply_q(values):
        return apply_k(apply_k(values, kappa_sq), kappa_sq)

    def one_probe(running, probe_row):
        sign_field = (2 * probe_row - 1).astype(jnp.float32)[None]
        solution = jnp.zeros_like(sign_field)
        residual = sign_field
        precond = apply_m(residual)
        rho_now = jnp.sum(residual * precond)
        direction = precond
        for iteration in range(ITERS):
            image_field = apply_q(direction)
            step_size = rho_now / jnp.sum(direction * image_field)
            solution = solution + step_size * direction
            if iteration + 1 < ITERS:
                residual = residual - step_size * image_field
                precond = apply_m(residual)
                rho_next = jnp.sum(residual * precond)
                direction = precond + (rho_next / rho_now) * direction
                rho_now = rho_next
        contribution = solution * apply_k(sign_field, kappa_sq) + apply_k(solution, kappa_sq) * sign_field
        return running + contribution[0], None

    trace_sum, unused = lax.scan(one_probe, jnp.zeros(kappa_sq.shape, jnp.float32), probe_bits)
    k_observed = apply_k(observed[None], kappa_sq)[0]
    return kappa_sq * (trace_sum / PROBES - 2.0 * observed * k_observed)
```

```python
import functools

import jax
import jax.numpy as jnp
from jax import lax
from jax.experimental import pallas as pl
from jax.experimental.pallas import tpu as pltpu
from jax.sharding import PartitionSpec as P

ITERS = 4
VERTICAL = 2.0
LANES = 128
ROWS = 8
EDGE = 8
GROUP = 4
SHIFTS = (1.0, 0.0, -2.0)
PAIRS = [(i, j) for j in range(ITERS) for i in range(j + 1)]
COUNT = len(PAIRS) + ITERS
SLOTS = 16


def two_sum(a, b):
    total = a + b
    part = total - a
    return total, (a - (total - part)) + (b - part)


def two_product(a, b):
    def split(v):
        big = v * 4097.0
        high = big - (big - v)
        return high, v - high

    product = a * b
    a_high, a_low = split(a)
    b_high, b_low = split(b)
    return product, ((a_high * b_high - product) + a_high * b_low + a_low * b_high) + a_low * b_low


def pair_add(first, second):
    total, rest = two_sum(first[0], second[0])
    rest = rest + (first[1] + second[1])
    high = total + rest
    return high, rest - (high - total)


def lane_ids(shape):
    return lax.broadcasted_iota(jnp.int32, shape, len(shape) - 1)


def row_ids(shape):
    return lax.broadcasted_iota(jnp.int32, shape, len(shape) - 2)


def pack_kernel(depth, bits_ref, kappa_ref, observed_ref, up_ref, down_ref, cross_ref):
    level = lax.axis_index("level")
    first = level == 0
    per_tile = LANES // EDGE
    tiles = depth // per_tile
    lanes = lane_ids((ROWS, LANES))

    def write(refs, offset, tile):
        for ref in refs:
            ref[offset] = tile

    for which, source in enumerate((bits_ref, kappa_ref)):
        base = which * (depth + tiles)

        def tile_loop(tile, unused, source=source, base=base, which=which):
            def step(slot, packed):
                z = tile * per_tile + slot
                value = source[z]
                if which == 0:
                    value = (2 * value - 1).astype(jnp.float32)
                low, high = value[:, :LANES], value[:, LANES:]
                same = jnp.where(first, low, high)
                cross = jnp.where(first, high, low)
                write((up_ref, down_ref), base + z, same)
                cross_ref[base + z] = cross
                here = lanes // EDGE == slot
                shift = lax.rem(EDGE * slot + EDGE * level, LANES)
                cross_shift = lax.rem(EDGE * slot + EDGE * (1 - level), LANES)
                return (
                    jnp.where(here, pltpu.roll(cross, shift, 1), packed[0]),
                    jnp.where(here, pltpu.roll(same, cross_shift, 1), packed[1]),
                )

            zero = jnp.zeros((ROWS, LANES), jnp.float32)
            packed = lax.fori_loop(0, per_tile, step, (zero, zero), unroll=4)
            write((up_ref, down_ref), base + depth + tile, packed[0])
            cross_ref[base + depth + tile] = packed[1]
            return unused

        lax.fori_loop(0, tiles, tile_loop, 0)
    base = 2 * (depth + tiles)
    in_low = lax.axis_index("probe") < lax.axis_size("probe") // 2

    def half(value):
        return jnp.where(in_low, value[..., :LANES], value[..., LANES:])

    top = half(observed_ref[:, ROWS - 1, :])
    bottom = half(observed_ref[:, 0, :])
    for tile in range(depth // ROWS):
        up_ref[base + tile] = top[tile * ROWS : (tile + 1) * ROWS]
        down_ref[base + tile] = bottom[tile * ROWS : (tile + 1) * ROWS]
    cross_ref[base] = jnp.where(first, half(observed_ref[depth - 1]), half(observed_ref[0]))


def beside(values):
    rows, columns = values.shape
    return (pltpu.roll(values, 1, 0) + pltpu.roll(values, rows - 1, 0)) + (
        pltpu.roll(values, 1, 1) + pltpu.roll(values, columns - 1, 1)
    )


def basis_kernel(
    depth,
    own_ref,
    own_far_ref,
    left_ref,
    left_far_ref,
    right_ref,
    right_far_ref,
    terms_ref,
    gram_ref,
    signs,
    half_diag,
    lower,
    upper,
    basis,
    forward,
    sides,
    backward,
    k_signs,
    k_basis,
    sums,
):
    levels = 2 * depth
    rows, columns = 3 * ROWS, 2 * LANES
    shape = (rows, columns)
    level = lax.axis_index("level")
    tile = lax.axis_index("tile")
    last_tile = lax.axis_size("tile") - 1
    per_tile = LANES // EDGE
    tiles = depth // per_tile
    lanes, ids = lane_ids(shape), row_ids(shape)
    near = jnp.where(level == 0, LANES, 2 * LANES - EDGE)
    inside = (lanes < LANES) | ((lanes >= near) & (lanes < near + EDGE))
    inside = inside & (ids >= jnp.where(tile > 0, 0, ROWS))
    inside = inside & (ids < jnp.where(tile < last_tile, 3 * ROWS, 2 * ROWS))
    mask = jnp.where(inside, 1.0, 0.0)
    zero = jnp.zeros(shape, jnp.float32)
    own = (slice(ROWS, 2 * ROWS), slice(0, LANES))
    own_zero = jnp.zeros((ROWS, LANES), jnp.float32)

    signs[0] = zero
    signs[levels + 1] = zero
    backward[levels] = zero
    upper[levels] = zero
    basis[levels] = zero
    for far, pieces in enumerate(
        ((left_ref, own_ref, right_ref), (left_far_ref, own_far_ref, right_far_ref))
    ):
        start = depth * (level if far == 0 else 1 - level)

        def unpack(z, unused, pieces=pieces, start=start):
            group = z // per_tile
            shift = lax.rem(2 * LANES - EDGE * lax.rem(z, per_tile) - EDGE * level, LANES)

            def gather(base):
                main = jnp.concatenate([piece[base + z] for piece in pieces], axis=0)
                edge = jnp.concatenate([piece[base + depth + group] for piece in pieces], axis=0)
                return jnp.concatenate([main, pltpu.roll(edge, shift, 1)], axis=1)

            signs[start + z + 1] = gather(0) * mask
            half_diag[start + z] = 0.5 * gather(depth + tiles) + (2.0 + VERTICAL)
            return unused

        lax.fori_loop(0, depth, unpack, 0, unroll=2)

    def start_down(k, carry):
        ratio, value = carry
        ratio = mask / (half_diag[k] - ratio)
        value = ratio * (signs[k + 1] + value)
        lower[k] = ratio
        forward[k] = value
        return ratio, value

    lax.fori_loop(0, levels, start_down, (zero, zero), unroll=GROUP)

    def start_up(step, carry):
        k = levels - 1 - step
        ratio, solved, value = carry
        ratio = mask / (half_diag[k] - ratio)
        solved = forward[k] + lower[k] * solved
        value = ratio * (solved + value)
        upper[k] = ratio
        backward[k] = value
        return ratio, solved, value

    lax.fori_loop(0, levels, start_up, (zero, zero, zero), unroll=GROUP)

    def k_of_signs(k, unused):
        value = signs[k + 1]
        image = half_diag[k] * value - (signs[k] + signs[k + 2]) - 0.5 * beside(value)
        k_signs[k] = image[own]
        return unused

    lax.fori_loop(0, levels, k_of_signs, 0, unroll=GROUP)

    place = 0
    for index in range(ITERS):
        final = index + 1 == ITERS

        def next_basis(k, previous, index=index):
            solved = backward[k] + upper[k] * previous
            if index == 0:
                value = solved
            elif SHIFTS[index - 1] == 0.0:
                value = -solved
            else:
                value = SHIFTS[index - 1] * basis[k] - solved
            return solved, value

        def down(group, carry, index=index, final=final, next_basis=next_basis):
            solved, above, here, value, *totals = carry
            products = []
            for step in range(GROUP):
                k = group * GROUP + step
                solved, below = next_basis(k + 1, solved)
                if not final:
                    basis[k + 1] = below
                side = beside(here)
                image = half_diag[k] * here - (above + below) - 0.5 * side
                if not final:
                    value = lower[k] * (beside(image * mask) + value)
                    forward[k] = value
                    sides[k] = side
                my_sign, my_basis, my_image = signs[k + 1][own], here[own], image[own]
                terms_ref[index, k] = my_basis * k_signs[k] + my_image * my_sign
                if not final:
                    k_basis[index, k] = my_image
                products.append(
                    [k_basis[other, k] * my_image for other in range(index)]
                    + [my_image * my_image, my_basis * my_sign]
                )
                above, here = here, below
            for slot in range(index + 2):
                added = (products[0][slot] + products[1][slot]) + (
                    products[2][slot] + products[3][slot]
                )
                totals[2 * slot], rest = two_sum(totals[2 * slot], added)
                totals[2 * slot + 1] = totals[2 * slot + 1] + rest
            return (solved, above, here, value, *totals)

        solved, here = next_basis(0, zero)
        if not final:
            basis[0] = here
        carry = lax.fori_loop(
            0,
            levels // GROUP,
            down,
            (solved, zero, here, zero) + (own_zero,) * (2 * (index + 2)),
        )
        totals = carry[4:]
        for slot in range(index + 1):
            sums[2 * (place + slot)] = totals[2 * slot]
            sums[2 * (place + slot) + 1] = totals[2 * slot + 1]
        place += index + 1
        sums[2 * (len(PAIRS) + index)] = totals[2 * index + 2]
        sums[2 * (len(PAIRS) + index) + 1] = totals[2 * index + 3]
        if final:
            break

        def up(step, carry):
            k = levels - 1 - step
            solved, value = carry
            solved = forward[k] + lower[k] * solved
            value = upper[k] * ((sides[k] + solved) + value)
            backward[k] = value
            return solved, value

        lax.fori_loop(0, levels, up, (zero, zero), unroll=GROUP)

    ids = row_ids((ROWS, LANES))
    for block in range(SLOTS // ROWS):
        high, low = own_zero, own_zero
        for slot in range(block * ROWS, min((block + 1) * ROWS, COUNT)):
            pair = (sums[2 * slot], sums[2 * slot + 1])
            for axis, shift in ((0, 4), (0, 2), (0, 1), (1, 64), (1, 32), (1, 16), (1, 8), (1, 4), (1, 2), (1, 1)):
                pair = pair_add(pair, tuple(pltpu.roll(part, shift, axis) for part in pair))
            here = ids == slot - block * ROWS
            high, low = jnp.where(here, pair[0], high), jnp.where(here, pair[1], low)
        gram_ref[block * ROWS : (block + 1) * ROWS] = high
        gram_ref[SLOTS + block * ROWS : SLOTS + (block + 1) * ROWS] = low


def solve_small(high, low):
    def entry(index):
        return tuple(jnp.broadcast_to(part[index : index + 1], (ROWS, LANES)) for part in (high, low))

    gram = {}
    for place, (i, j) in enumerate(PAIRS):
        gram[i, j] = gram[j, i] = entry(place)
    right = [entry(len(PAIRS) + j) for j in range(ITERS)]
    work = {key: pair[0] for key, pair in gram.items()}
    ratios, inverses = {}, []
    for i in range(ITERS):
        pivot = work[i, i]
        good = pivot > 1e-7 * gram[i, i][0]
        inverses.append(jnp.where(good, 1.0 / jnp.where(good, pivot, 1.0), 0.0))
        for r in range(i + 1, ITERS):
            ratios[r, i] = work[r, i] * inverses[i]
        for r in range(i + 1, ITERS):
            for c in range(i + 1, r + 1):
                work[r, c] = work[c, r] = work[r, c] - ratios[r, i] * work[c, i]

    def solve(values):
        values = list(values)
        for i in range(ITERS):
            for r in range(i + 1, ITERS):
                values[r] = values[r] - ratios[r, i] * values[i]
        values = [value * inverse for value, inverse in zip(values, inverses)]
        for i in reversed(range(ITERS)):
            for r in range(i):
                values[r] = values[r] - ratios[i, r] * values[i]
        return values

    found = solve([pair[0] for pair in right])
    for unused in range(2):
        rest = []
        for i in range(ITERS):
            total = right[i]
            for j in range(ITERS):
                product, error = two_product(gram[i, j][0], found[j])
                total = pair_add(total, (-product, -(error + gram[i, j][1] * found[j])))
            rest.append(total[0] + total[1])
        found = [a + b for a, b in zip(found, solve(rest))]
    return found


def combine_kernel(depth, terms_ref, *refs):
    gram_refs, (keep_ref, send_ref) = refs[:-2], refs[-2:]
    pairs = []
    for ref in gram_refs:
        for start in range(0, ref.shape[0], 2 * SLOTS):
            pairs.append((ref[start : start + SLOTS], ref[start + SLOTS : start + 2 * SLOTS]))
    while len(pairs) > 1:
        merged = [pair_add(pairs[i], pairs[i + 1]) for i in range(0, len(pairs) - 1, 2)]
        pairs = merged + pairs[2 * len(merged) :]
    found = solve_small(*pairs[0])
    core = lax.rem(lax.axis_index("probe"), 2)
    width = LANES // 2
    lower_lanes = lane_ids((ROWS, LANES)) < width
    pairs_deep = depth // 2

    def step(z, unused):
        for half in range(2):
            def total(k):
                value = found[0] * terms_ref[0, k]
                for j in range(1, ITERS):
                    value = value + found[j] * terms_ref[j, k]
                return value

            one = total(half * depth + z)
            two = total(half * depth + pairs_deep + z)
            low = jnp.where(lower_lanes, one, pltpu.roll(two, width, 1))
            high = jnp.where(lower_lanes, pltpu.roll(one, width, 1), two)
            keep_ref[half, z] = jnp.where(core == 0, low, high)
            send_ref[half, z] = jnp.where(core == 0, high, low)
        return unused

    lax.fori_loop(0, pairs_deep, step, 0, unroll=2)


def gradient_kernel(
    depth, probes, trace_a_ref, trace_b_ref, kappa_ref, observed_ref, left_ref, right_ref, far_ref, out_ref
):
    level = lax.axis_index("level")
    tile = lax.axis_index("tile")
    last_tile = lax.axis_size("tile") - 1
    probe = lax.axis_index("probe")
    in_low = probe < probes // 2
    even = lax.rem(probe, 2) == 0
    width = LANES // 2
    lanes = lane_ids((ROWS, 2 * LANES))
    ids = row_ids((ROWS, LANES))
    base = left_ref.shape[0] - depth // ROWS

    def half(value):
        return jnp.where(in_low, value[..., :LANES], value[..., LANES:])

    def take(value):
        return jnp.where(even, value, pltpu.roll(value, width, 1))[:, :width]

    far_edge = far_ref[far_ref.shape[0] - 1]
    for z in range(depth):
        value = observed_ref[z]
        mine = half(value)
        y_sides = jnp.where(lanes > 0, pltpu.roll(value, 1, 1), 0.0) + jnp.where(
            lanes < 2 * LANES - 1, pltpu.roll(value, 2 * LANES - 1, 1), 0.0
        )
        left = left_ref[base + z // ROWS, z % ROWS : z % ROWS + 1, :]
        right = right_ref[base + z // ROWS, z % ROWS : z % ROWS + 1, :]
        before = jnp.where(ids > 0, pltpu.roll(mine, 1, 0), jnp.where(tile > 0, left, 0.0))
        after = jnp.where(
            ids < ROWS - 1, pltpu.roll(mine, ROWS - 1, 0), jnp.where(tile < last_tile, right, 0.0)
        )
        above = half(observed_ref[z - 1]) if z > 0 else jnp.where(level > 0, far_edge, 0.0)
        below = half(observed_ref[z + 1]) if z < depth - 1 else jnp.where(level == 0, far_edge, 0.0)
        kappa = half(kappa_ref[z])
        k_observed = (
            (kappa + (4.0 + 2.0 * VERTICAL)) * mine
            - (before + after)
            - half(y_sides)
            - VERTICAL * (above + below)
        )
        data_part = take(2.0 * mine * k_observed)
        trace = trace_a_ref[z % (depth // 2)] + trace_b_ref[z % (depth // 2)]
        trace = trace[:, :width] if z < depth // 2 else pltpu.roll(trace, width, 1)[:, :width]
        out_ref[z] = take(kappa) * (trace * (0.5 / probes) - data_part)


def whole(count):
    return [pl.BlockSpec(memory_space=pltpu.VMEM)] * count


def body(probe_bits, kappa_sq, observed):
    probes, tile_count = lax.axis_size("probe"), lax.axis_size("tile")
    unused, depth, rows, columns = probe_bits.shape
    assert probe_bits.shape[0] == 1 and lax.axis_size("level") == 2 and probes == 4
    assert rows == ROWS and columns == 2 * LANES and depth % (LANES // EDGE) == 0
    params = pltpu.CompilerParams(vmem_limit_bytes=48 * 1024 * 1024)
    f32 = jnp.float32
    tiles = depth * EDGE // LANES
    field = 2 * (depth + tiles)
    near_shape = jax.ShapeDtypeStruct((field + depth // ROWS, ROWS, LANES), f32)
    far_shape = jax.ShapeDtypeStruct((field + 1, ROWS, LANES), f32)

    up_block, down_block, cross_block = pl.pallas_call(
        functools.partial(pack_kernel, depth),
        out_shape=(near_shape, near_shape, far_shape),
        in_specs=whole(3),
        out_specs=tuple(whole(3)),
        compiler_params=params,
        name="pack",
    )(probe_bits[0], kappa_sq, observed)

    up_pairs = [(i, i + 1) for i in range(tile_count - 1)]
    down_pairs = [(i + 1, i) for i in range(tile_count - 1)]
    own_far = lax.ppermute(cross_block, "level", [(0, 1), (1, 0)])
    left = lax.ppermute(up_block, "tile", up_pairs)
    right = lax.ppermute(down_block, "tile", down_pairs)
    left_far = lax.ppermute(own_far, "tile", up_pairs)
    right_far = lax.ppermute(
        cross_block,
        ("tile", "level"),
        [(2 * a + level, 2 * b + 1 - level) for a, b in down_pairs for level in range(2)],
    )

    levels = 2 * depth
    padded = pltpu.VMEM((levels + 1, 3 * ROWS, 2 * LANES), f32)
    plain = pltpu.VMEM((levels, 3 * ROWS, 2 * LANES), f32)
    terms, gram = pl.pallas_call(
        functools.partial(basis_kernel, depth),
        out_shape=(
            jax.ShapeDtypeStruct((ITERS, levels, ROWS, LANES), f32),
            jax.ShapeDtypeStruct((2 * SLOTS, LANES), f32),
        ),
        in_specs=whole(6),
        out_specs=tuple(whole(2)),
        scratch_shapes=[
            pltpu.VMEM((levels + 2, 3 * ROWS, 2 * LANES), f32),
            plain,
            plain,
            padded,
            padded,
            plain,
            plain,
            padded,
            pltpu.VMEM((levels, ROWS, LANES), f32),
            pltpu.VMEM((ITERS - 1, levels, ROWS, LANES), f32),
            pltpu.VMEM((2 * SLOTS, ROWS, LANES), f32),
        ],
        compiler_params=params,
        name="basis",
    )(up_block, own_far, left, left_far, right, right_far)

    both = jnp.concatenate([gram, lax.ppermute(gram, "level", [(0, 1), (1, 0)])], axis=0)
    if tile_count <= 4:
        partials = [both] + [
            lax.ppermute(both, "tile", [(i, (i + k) % tile_count) for i in range(tile_count)])
            for k in range(1, tile_count)
        ]
    else:
        partials = [lax.all_gather(both, "tile", axis=0, tiled=True)]
    piece = jax.ShapeDtypeStruct((2, depth // 2, ROWS, LANES), f32)
    keep, send = pl.pallas_call(
        functools.partial(combine_kernel, depth),
        out_shape=(piece, piece),
        in_specs=whole(1 + len(partials)),
        out_specs=tuple(whole(2)),
        compiler_params=params,
        name="combine",
    )(terms, *partials)

    summed = keep + lax.ppermute(send, "probe", [(0, 1), (1, 0), (2, 3), (3, 2)])
    half = lax.axis_index("probe") // 2
    straight = lax.dynamic_index_in_dim(summed, half, 0, keepdims=False)
    turned = lax.dynamic_index_in_dim(summed, 1 - half, 0, keepdims=False)

    def routes(flip):
        pairs = []
        for x in range(2):
            for core in range(2):
                for level in range(2):
                    target = x if not flip else 1 - x
                    pairs.append(((2 * x + core) * 2 + level, (2 * level + core) * 2 + target))
        return pairs

    trace_a = lax.ppermute(straight, ("probe", "level"), routes(False))
    trace_b = lax.ppermute(turned, ("probe", "level"), routes(True))
    return pl.pallas_call(
        functools.partial(gradient_kernel, depth, probes),
        out_shape=jax.ShapeDtypeStruct((depth, ROWS, columns // probes), f32),
        in_specs=whole(7),
        out_specs=pl.BlockSpec(memory_space=pltpu.VMEM),
        compiler_params=params,
        name="gradient",
    )(trace_a, trace_b, kappa_sq, observed, left, right, own_far)


def solution(mesh):
    in_specs = (
        P("probe", "level", "tile", None),
        P("level", "tile", None),
        P("level", "tile", None),
    )
    out_specs = P("level", "tile", "probe")
    return jax.shard_map(body, mesh=mesh, in_specs=in_specs, out_specs=out_specs, check_vma=False)
```

```python
import functools

import jax
import jax.numpy as jnp
from jax import lax
from jax.experimental import pallas as pl
from jax.experimental.pallas import tpu as pltpu
from jax.sharding import PartitionSpec as P

ITERS = 4
VERTICAL = 2.0
LANES = 128
ROWS = 8
EDGE = 8
GROUP = 4
SHIFTS = (1.0, 0.0, -2.0)
PAIRS = [(i, j) for j in range(ITERS) for i in range(j + 1)]
COUNT = len(PAIRS) + ITERS
SLOTS = 16


def two_sum(a, b):
    total = a + b
    part = total - a
    return total, (a - (total - part)) + (b - part)


def two_product(a, b):
    def split(v):
        big = v * 4097.0
        high = big - (big - v)
        return high, v - high

    product = a * b
    a_high, a_low = split(a)
    b_high, b_low = split(b)
    return product, ((a_high * b_high - product) + a_high * b_low + a_low * b_high) + a_low * b_low


def pair_add(first, second):
    total, rest = two_sum(first[0], second[0])
    rest = rest + (first[1] + second[1])
    high = total + rest
    return high, rest - (high - total)


def lane_ids(shape):
    return lax.broadcasted_iota(jnp.int32, shape, len(shape) - 1)


def row_ids(shape):
    return lax.broadcasted_iota(jnp.int32, shape, len(shape) - 2)


def split_three(values):
    high = values.astype(jnp.bfloat16)
    rest = values - high.astype(jnp.float32)
    middle = rest.astype(jnp.bfloat16)
    low = (rest - middle.astype(jnp.float32)).astype(jnp.bfloat16)
    return high, middle, low


def pick(values, chosen):
    high, middle, low = (
        jnp.dot(part, chosen, preferred_element_type=jnp.float32) for part in split_three(values)
    )
    return high + (middle + low)


def columns_of(half):
    shape = (2 * LANES, 2 * LANES)
    ids, lane = row_ids(shape), lane_ids(shape)
    odd = (lane // (LANES // 2)) % 2
    main = LANES * half + 2 * (lane % (LANES // 2)) + odd
    edge = LANES - EDGE * half + 2 * (lane % (EDGE // 2)) + odd
    wanted = jnp.where(lane < LANES, main, edge)
    return jnp.where(ids == wanted, 1.0, 0.0).astype(jnp.bfloat16)


def pack_kernel(
    depth,
    bits_hbm,
    kappa_hbm,
    observed_hbm,
    up_ref,
    down_ref,
    cross_ref,
    bits_ref,
    kappa_ref,
    observed_ref,
    arrived,
):
    copies = [
        pltpu.make_async_copy(source, target, arrived.at[place])
        for place, (source, target) in enumerate(
            ((bits_hbm, bits_ref), (kappa_hbm, kappa_ref), (observed_hbm, observed_ref))
        )
    ]
    for copy in copies:
        copy.start()
    level = lax.axis_index("level")
    first = level == 0
    per_tile = LANES // EDGE
    tiles = depth // per_tile
    slot_ids = (lane_ids((ROWS, LANES)) % (LANES // 2)) // (EDGE // 2)
    same_columns, cross_columns = columns_of(level), columns_of(1 - level)
    for which in range(2):
        base = which * (depth + tiles)
        copies[which].wait()
        for refs, chosen in (((up_ref, down_ref), same_columns), ((cross_ref,), cross_columns)):
            if which == 0:
                values = (2 * bits_ref[...] - 1).astype(jnp.float32).reshape(depth * ROWS, 2 * LANES)
                picked = jnp.dot(
                    values.astype(jnp.bfloat16), chosen, preferred_element_type=jnp.float32
                )
            else:
                picked = pick(kappa_ref[...].reshape(depth * ROWS, 2 * LANES), chosen)
            picked = picked.reshape(depth, ROWS, 2 * LANES)
            for ref in refs:
                ref[base : base + depth] = picked[:, :, :LANES]
            for tile in range(tiles):
                packed = picked[tile * per_tile, :, LANES:]
                for slot in range(1, per_tile):
                    packed = jnp.where(
                        slot_ids == slot, picked[tile * per_tile + slot, :, LANES:], packed
                    )
                for ref in refs:
                    ref[base + depth + tile] = packed
    copies[2].wait()
    base = 2 * (depth + tiles)
    in_low = lax.axis_index("probe") < lax.axis_size("probe") // 2

    def half(value):
        return jnp.where(in_low, value[..., :LANES], value[..., LANES:])

    top = half(observed_ref[:, ROWS - 1, :])
    bottom = half(observed_ref[:, 0, :])
    for tile in range(depth // ROWS):
        up_ref[base + tile] = top[tile * ROWS : (tile + 1) * ROWS]
        down_ref[base + tile] = bottom[tile * ROWS : (tile + 1) * ROWS]
    cross_ref[base] = jnp.where(first, half(observed_ref[depth - 1]), half(observed_ref[0]))


def beside(values):
    rows = values.shape[0]
    even, odd = values[:, :LANES], values[:, LANES:]
    y_sides = jnp.concatenate(
        [odd + pltpu.roll(odd, 1, 1), even + pltpu.roll(even, LANES - 1, 1)], axis=1
    )
    return (pltpu.roll(values, 1, 0) + pltpu.roll(values, rows - 1, 0)) + y_sides


def basis_kernel(
    depth,
    own_ref,
    own_far_ref,
    left_ref,
    left_far_ref,
    right_ref,
    right_far_ref,
    terms_ref,
    gram_ref,
    signs,
    half_diag,
    lower,
    upper,
    basis,
    forward,
    sides,
    backward,
    k_signs,
    k_basis,
    sums,
):
    levels = 2 * depth
    rows, columns = 3 * ROWS, 2 * LANES
    shape = (rows, columns)
    level = lax.axis_index("level")
    tile = lax.axis_index("tile")
    last_tile = lax.axis_size("tile") - 1
    per_tile = LANES // EDGE
    tiles = depth // per_tile
    lanes, ids = lane_ids(shape), row_ids(shape)
    half = LANES // 2
    lanes = lanes % LANES
    near = jnp.where(level == 0, half, LANES - EDGE // 2)
    inside = (lanes < half) | ((lanes >= near) & (lanes < near + EDGE // 2))
    inside = inside & (ids >= jnp.where(tile > 0, 0, ROWS))
    inside = inside & (ids < jnp.where(tile < last_tile, 3 * ROWS, 2 * ROWS))
    mask = jnp.where(inside, 1.0, 0.0)
    zero = jnp.zeros(shape, jnp.float32)
    own = (slice(ROWS, 2 * ROWS), slice(0, 2 * LANES))
    mine = lane_ids((ROWS, LANES)) < half
    own_zero = jnp.zeros((ROWS, LANES), jnp.float32)

    signs[0] = zero
    signs[levels + 1] = zero
    backward[levels] = zero
    upper[levels] = zero
    basis[levels] = zero
    for far, pieces in enumerate(
        ((left_ref, own_ref, right_ref), (left_far_ref, own_far_ref, right_far_ref))
    ):
        start = depth * (level if far == 0 else 1 - level)

        def unpack(z, unused, pieces=pieces, start=start):
            group = z // per_tile
            shift = half + (half - EDGE // 2) * level - (EDGE // 2) * lax.rem(z, per_tile)
            shift = lax.rem(shift + LANES, LANES)

            def gather(base):
                evens, odds = [], []
                for piece in pieces:
                    main = piece[base + z]
                    edge = pltpu.roll(piece[base + depth + group], shift, 1)
                    evens.append(jnp.where(mine, main, edge))
                    odds.append(pltpu.roll(jnp.where(mine, edge, main), half, 1))
                return jnp.concatenate(
                    [jnp.concatenate(evens, axis=0), jnp.concatenate(odds, axis=0)], axis=1
                )

            signs[start + z + 1] = gather(0) * mask
            half_diag[start + z] = 0.5 * gather(depth + tiles) + (2.0 + VERTICAL)
            return unused

        lax.fori_loop(0, depth, unpack, 0, unroll=2)

    def start_down(k, carry):
        ratio, value, from_end = carry
        ratio = mask / (half_diag[k] - ratio)
        here = signs[k + 1]
        value = ratio * (here + value)
        lower[k] = ratio
        forward[k] = value
        other = levels - 1 - k
        from_end = mask / (half_diag[other] - from_end)
        upper[other] = from_end
        image = half_diag[k] * here - (signs[k] + signs[k + 2]) - 0.5 * beside(here)
        k_signs[k] = image[own]
        return ratio, value, from_end

    lax.fori_loop(0, levels, start_down, (zero, zero, zero), unroll=GROUP)

    def start_up(step, carry):
        k = levels - 1 - step
        solved, value = carry
        solved = forward[k] + lower[k] * solved
        value = upper[k] * (solved + value)
        backward[k] = value
        return solved, value

    lax.fori_loop(0, levels, start_up, (zero, zero), unroll=GROUP)

    place = 0
    for index in range(ITERS):
        final = index + 1 == ITERS

        def next_basis(k, previous, index=index):
            solved = backward[k] + upper[k] * previous
            if index == 0:
                value = solved
            elif SHIFTS[index - 1] == 0.0:
                value = -solved
            else:
                value = SHIFTS[index - 1] * basis[k] - solved
            return solved, value

        def down(group, carry, index=index, final=final, next_basis=next_basis):
            solved, above, here, value, *totals = carry
            products = []
            for step in range(GROUP):
                k = group * GROUP + step
                solved, below = next_basis(k + 1, solved)
                if not final:
                    basis[k + 1] = below
                side = beside(here)
                image = half_diag[k] * here - (above + below) - 0.5 * side
                if not final:
                    value = lower[k] * (beside(image * mask) + value)
                    forward[k] = value
                    sides[k] = side
                my_sign, my_basis, my_image = signs[k + 1][own], here[own], image[own]
                term = my_basis * k_signs[k] + my_image * my_sign
                terms_ref[index, k] = jnp.where(
                    mine, term[:, :LANES], pltpu.roll(term[:, LANES:], half, 1)
                )
                if not final:
                    k_basis[index, k] = my_image
                factors = [(k_basis[other, k], my_image) for other in range(index)]
                factors += [(my_image, my_image), (my_basis, my_sign)]
                products.append(
                    [a[:, :LANES] * b[:, :LANES] + a[:, LANES:] * b[:, LANES:] for a, b in factors]
                )
                above, here = here, below
            for slot in range(index + 2):
                added = (products[0][slot] + products[1][slot]) + (
                    products[2][slot] + products[3][slot]
                )
                totals[2 * slot], rest = two_sum(totals[2 * slot], added)
                totals[2 * slot + 1] = totals[2 * slot + 1] + rest
            return (solved, above, here, value, *totals)

        solved, here = next_basis(0, zero)
        if not final:
            basis[0] = here
        carry = lax.fori_loop(
            0,
            levels // GROUP,
            down,
            (solved, zero, here, zero) + (own_zero,) * (2 * (index + 2)),
        )
        totals = [jnp.where(mine, total, 0.0) for total in carry[4:]]
        for slot in range(index + 1):
            sums[2 * (place + slot)] = totals[2 * slot]
            sums[2 * (place + slot) + 1] = totals[2 * slot + 1]
        place += index + 1
        sums[2 * (len(PAIRS) + index)] = totals[2 * index + 2]
        sums[2 * (len(PAIRS) + index) + 1] = totals[2 * index + 3]
        if final:
            break

        def up(step, carry):
            k = levels - 1 - step
            solved, value = carry
            solved = forward[k] + lower[k] * solved
            value = upper[k] * ((sides[k] + solved) + value)
            backward[k] = value
            return solved, value

        lax.fori_loop(0, levels, up, (zero, zero), unroll=GROUP)

    ids = row_ids((ROWS, LANES))
    for block in range(SLOTS // ROWS):
        high, low = own_zero, own_zero
        for slot in range(block * ROWS, min((block + 1) * ROWS, COUNT)):
            pair = (sums[2 * slot], sums[2 * slot + 1])
            for axis, shift in ((0, 4), (0, 2), (0, 1), (1, 64), (1, 32), (1, 16), (1, 8), (1, 4), (1, 2), (1, 1)):
                pair = pair_add(pair, tuple(pltpu.roll(part, shift, axis) for part in pair))
            here = ids == slot - block * ROWS
            high, low = jnp.where(here, pair[0], high), jnp.where(here, pair[1], low)
        gram_ref[block * ROWS : (block + 1) * ROWS] = high
        gram_ref[SLOTS + block * ROWS : SLOTS + (block + 1) * ROWS] = low


def solve_small(high, low):
    def entry(index):
        return tuple(jnp.broadcast_to(part[index : index + 1], (ROWS, LANES)) for part in (high, low))

    gram = {}
    for place, (i, j) in enumerate(PAIRS):
        gram[i, j] = gram[j, i] = entry(place)
    right = [entry(len(PAIRS) + j) for j in range(ITERS)]
    work = {key: pair[0] for key, pair in gram.items()}
    ratios, inverses = {}, []
    for i in range(ITERS):
        pivot = work[i, i]
        good = pivot > 1e-7 * gram[i, i][0]
        inverses.append(jnp.where(good, 1.0 / jnp.where(good, pivot, 1.0), 0.0))
        for r in range(i + 1, ITERS):
            ratios[r, i] = work[r, i] * inverses[i]
        for r in range(i + 1, ITERS):
            for c in range(i + 1, r + 1):
                work[r, c] = work[c, r] = work[r, c] - ratios[r, i] * work[c, i]

    def solve(values):
        values = list(values)
        for i in range(ITERS):
            for r in range(i + 1, ITERS):
                values[r] = values[r] - ratios[r, i] * values[i]
        values = [value * inverse for value, inverse in zip(values, inverses)]
        for i in reversed(range(ITERS)):
            for r in range(i):
                values[r] = values[r] - ratios[i, r] * values[i]
        return values

    found = solve([pair[0] for pair in right])
    for unused in range(2):
        rest = []
        for i in range(ITERS):
            total = right[i]
            for j in range(ITERS):
                product, error = two_product(gram[i, j][0], found[j])
                total = pair_add(total, (-product, -(error + gram[i, j][1] * found[j])))
            rest.append(total[0] + total[1])
        found = [a + b for a, b in zip(found, solve(rest))]
    return found


def combine_kernel(depth, terms_ref, *refs):
    gram_refs, (keep_ref, send_ref) = refs[:-2], refs[-2:]
    pairs = []
    for ref in gram_refs:
        for start in range(0, ref.shape[0], 2 * SLOTS):
            pairs.append((ref[start : start + SLOTS], ref[start + SLOTS : start + 2 * SLOTS]))
    while len(pairs) > 1:
        merged = [pair_add(pairs[i], pairs[i + 1]) for i in range(0, len(pairs) - 1, 2)]
        pairs = merged + pairs[2 * len(merged) :]
    found = solve_small(*pairs[0])
    core = lax.rem(lax.axis_index("probe"), 2)
    width = LANES // 4
    first_lanes = lane_ids((ROWS, LANES)) % (2 * width) < width
    pairs_deep = depth // 2

    def step(z, unused):
        for half in range(2):
            def total(k):
                value = found[0] * terms_ref[0, k]
                for j in range(1, ITERS):
                    value = value + found[j] * terms_ref[j, k]
                return value

            one = total(half * depth + z)
            two = total(half * depth + pairs_deep + z)
            low = jnp.where(first_lanes, one, pltpu.roll(two, width, 1))
            high = jnp.where(first_lanes, pltpu.roll(one, LANES - width, 1), two)
            keep_ref[half, z] = jnp.where(core == 0, low, high)
            send_ref[half, z] = jnp.where(core == 0, high, low)
        return unused

    lax.fori_loop(0, pairs_deep, step, 0, unroll=2)


def gradient_kernel(
    depth, probes, trace_a_ref, trace_b_ref, kappa_ref, observed_ref, left_ref, right_ref, far_ref, out_ref
):
    level = lax.axis_index("level")
    tile = lax.axis_index("tile")
    last_tile = lax.axis_size("tile") - 1
    probe = lax.axis_index("probe")
    in_low = probe < probes // 2
    even = lax.rem(probe, 2) == 0
    width = LANES // 2
    lanes = lane_ids((ROWS, 2 * LANES))
    ids = row_ids((ROWS, LANES))
    base = left_ref.shape[0] - depth // ROWS

    def half(value):
        return jnp.where(in_low, value[..., :LANES], value[..., LANES:])

    def take(value):
        return jnp.where(even, value, pltpu.roll(value, width, 1))[:, :width]

    far_edge = far_ref[far_ref.shape[0] - 1]
    square = (LANES, LANES)
    lane = lane_ids(square)
    source = (width // 2) * (lane // width) + (lane % width) // 2 + width * (lane % 2)
    chosen = jnp.where(row_ids(square) == source, 1.0, 0.0).astype(jnp.bfloat16)
    traces = pick((trace_a_ref[...] + trace_b_ref[...]).reshape(-1, LANES), chosen)
    traces = traces.reshape(depth // 2, ROWS, LANES)
    for z in range(depth):
        value = observed_ref[z]
        mine = half(value)
        y_sides = jnp.where(lanes > 0, pltpu.roll(value, 1, 1), 0.0) + jnp.where(
            lanes < 2 * LANES - 1, pltpu.roll(value, 2 * LANES - 1, 1), 0.0
        )
        left = left_ref[base + z // ROWS, z % ROWS : z % ROWS + 1, :]
        right = right_ref[base + z // ROWS, z % ROWS : z % ROWS + 1, :]
        before = jnp.where(ids > 0, pltpu.roll(mine, 1, 0), jnp.where(tile > 0, left, 0.0))
        after = jnp.where(
            ids < ROWS - 1, pltpu.roll(mine, ROWS - 1, 0), jnp.where(tile < last_tile, right, 0.0)
        )
        above = half(observed_ref[z - 1]) if z > 0 else jnp.where(level > 0, far_edge, 0.0)
        below = half(observed_ref[z + 1]) if z < depth - 1 else jnp.where(level == 0, far_edge, 0.0)
        kappa = half(kappa_ref[z])
        k_observed = (
            (kappa + (4.0 + 2.0 * VERTICAL)) * mine
            - (before + after)
            - half(y_sides)
            - VERTICAL * (above + below)
        )
        data_part = take(2.0 * mine * k_observed)
        trace = traces[z % (depth // 2)]
        trace = trace[:, :width] if z < depth // 2 else pltpu.roll(trace, width, 1)[:, :width]
        out_ref[z] = take(kappa) * (trace * (0.5 / probes) - data_part)


def whole(count):
    return [pl.BlockSpec(memory_space=pltpu.VMEM)] * count


def body(probe_bits, kappa_sq, observed):
    probes, tile_count = lax.axis_size("probe"), lax.axis_size("tile")
    unused, depth, rows, columns = probe_bits.shape
    assert probe_bits.shape[0] == 1 and lax.axis_size("level") == 2 and probes == 4
    assert rows == ROWS and columns == 2 * LANES and depth % (LANES // EDGE) == 0
    params = pltpu.CompilerParams(vmem_limit_bytes=48 * 1024 * 1024)
    f32 = jnp.float32
    tiles = depth * EDGE // LANES
    field = 2 * (depth + tiles)
    near_shape = jax.ShapeDtypeStruct((field + depth // ROWS, ROWS, LANES), f32)
    far_shape = jax.ShapeDtypeStruct((field + 1, ROWS, LANES), f32)

    up_block, down_block, cross_block = pl.pallas_call(
        functools.partial(pack_kernel, depth),
        out_shape=(near_shape, near_shape, far_shape),
        in_specs=[pl.BlockSpec(memory_space=pl.ANY)] * 3,
        out_specs=tuple(whole(3)),
        scratch_shapes=[
            pltpu.VMEM((depth, rows, columns), jnp.int32),
            pltpu.VMEM((depth, rows, columns), f32),
            pltpu.VMEM((depth, rows, columns), f32),
            pltpu.SemaphoreType.DMA((3,)),
        ],
        compiler_params=params,
        name="pack",
    )(probe_bits[0], kappa_sq, observed)

    up_pairs = [(i, i + 1) for i in range(tile_count - 1)]
    down_pairs = [(i + 1, i) for i in range(tile_count - 1)]
    own_far = lax.ppermute(cross_block, "level", [(0, 1), (1, 0)])
    left = lax.ppermute(up_block, "tile", up_pairs)
    right = lax.ppermute(down_block, "tile", down_pairs)
    left_far = lax.ppermute(own_far, "tile", up_pairs)
    right_far = lax.ppermute(
        cross_block,
        ("tile", "level"),
        [(2 * a + level, 2 * b + 1 - level) for a, b in down_pairs for level in range(2)],
    )

    levels = 2 * depth
    padded = pltpu.VMEM((levels + 1, 3 * ROWS, 2 * LANES), f32)
    plain = pltpu.VMEM((levels, 3 * ROWS, 2 * LANES), f32)
    terms, gram = pl.pallas_call(
        functools.partial(basis_kernel, depth),
        out_shape=(
            jax.ShapeDtypeStruct((ITERS, levels, ROWS, LANES), f32),
            jax.ShapeDtypeStruct((2 * SLOTS, LANES), f32),
        ),
        in_specs=whole(6),
        out_specs=tuple(whole(2)),
        scratch_shapes=[
            pltpu.VMEM((levels + 2, 3 * ROWS, 2 * LANES), f32),
            plain,
            plain,
            padded,
            padded,
            plain,
            plain,
            padded,
            pltpu.VMEM((levels, ROWS, 2 * LANES), f32),
            pltpu.VMEM((ITERS - 1, levels, ROWS, 2 * LANES), f32),
            pltpu.VMEM((2 * SLOTS, ROWS, LANES), f32),
        ],
        compiler_params=params,
        name="basis",
    )(up_block, own_far, left, left_far, right, right_far)

    both = jnp.concatenate([gram, lax.ppermute(gram, "level", [(0, 1), (1, 0)])], axis=0)
    if tile_count <= 4:
        partials = [both] + [
            lax.ppermute(both, "tile", [(i, (i + k) % tile_count) for i in range(tile_count)])
            for k in range(1, tile_count)
        ]
    else:
        partials = [lax.all_gather(both, "tile", axis=0, tiled=True)]
    piece = jax.ShapeDtypeStruct((2, depth // 2, ROWS, LANES), f32)
    keep, send = pl.pallas_call(
        functools.partial(combine_kernel, depth),
        out_shape=(piece, piece),
        in_specs=whole(1 + len(partials)),
        out_specs=tuple(whole(2)),
        compiler_params=params,
        name="combine",
    )(terms, *partials)

    summed = keep + lax.ppermute(send, "probe", [(0, 1), (1, 0), (2, 3), (3, 2)])
    half = lax.axis_index("probe") // 2
    straight = lax.dynamic_index_in_dim(summed, half, 0, keepdims=False)
    turned = lax.dynamic_index_in_dim(summed, 1 - half, 0, keepdims=False)

    def routes(flip):
        pairs = []
        for x in range(2):
            for core in range(2):
                for level in range(2):
                    target = x if not flip else 1 - x
                    pairs.append(((2 * x + core) * 2 + level, (2 * level + core) * 2 + target))
        return pairs

    trace_a = lax.ppermute(straight, ("probe", "level"), routes(False))
    trace_b = lax.ppermute(turned, ("probe", "level"), routes(True))
    return pl.pallas_call(
        functools.partial(gradient_kernel, depth, probes),
        out_shape=jax.ShapeDtypeStruct((depth, ROWS, columns // probes), f32),
        in_specs=whole(7),
        out_specs=pl.BlockSpec(memory_space=pltpu.VMEM),
        compiler_params=params,
        name="gradient",
    )(trace_a, trace_b, kappa_sq, observed, left, right, own_far)


def solution(mesh):
    in_specs = (
        P("probe", "level", "tile", None),
        P("level", "tile", None),
        P("level", "tile", None),
    )
    out_specs = P("level", "tile", "probe")
    return jax.shard_map(body, mesh=mesh, in_specs=in_specs, out_specs=out_specs, check_vma=False)
```

```python
import functools

import jax
import jax.numpy as jnp
from jax import lax
from jax.experimental import pallas as pl
from jax.experimental.pallas import tpu as pltpu
from jax.sharding import PartitionSpec as P

ITERS = 4
VERTICAL = 2.0
LANES = 128
ROWS = 8
EDGE = 8
GROUP = 8
SHIFTS = (1.0, 0.0, -2.0)
PAIRS = [(i, j) for j in range(ITERS) for i in range(j + 1)]
COUNT = len(PAIRS) + ITERS
SLOTS = 16


def two_sum(a, b):
    total = a + b
    part = total - a
    return total, (a - (total - part)) + (b - part)


def two_product(a, b):
    def split(v):
        big = v * 4097.0
        high = big - (big - v)
        return high, v - high

    product = a * b
    a_high, a_low = split(a)
    b_high, b_low = split(b)
    return product, ((a_high * b_high - product) + a_high * b_low + a_low * b_high) + a_low * b_low


def pair_add(first, second):
    total, rest = two_sum(first[0], second[0])
    rest = rest + (first[1] + second[1])
    high = total + rest
    return high, rest - (high - total)


def lane_ids(shape):
    return lax.broadcasted_iota(jnp.int32, shape, len(shape) - 1)


def row_ids(shape):
    return lax.broadcasted_iota(jnp.int32, shape, len(shape) - 2)


def split_three(values):
    high = values.astype(jnp.bfloat16)
    rest = values - high.astype(jnp.float32)
    middle = rest.astype(jnp.bfloat16)
    low = (rest - middle.astype(jnp.float32)).astype(jnp.bfloat16)
    return high, middle, low


def pick(values, chosen):
    high, middle, low = (
        jnp.dot(part, chosen, preferred_element_type=jnp.float32) for part in split_three(values)
    )
    return high + (middle + low)


def columns_of(half):
    shape = (2 * LANES, 2 * LANES)
    ids, lane = row_ids(shape), lane_ids(shape)
    odd = (lane // (LANES // 2)) % 2
    main = LANES * half + 2 * (lane % (LANES // 2)) + odd
    edge = LANES - EDGE * half + 2 * (lane % (EDGE // 2)) + odd
    wanted = jnp.where(lane < LANES, main, edge)
    return jnp.where(ids == wanted, 1.0, 0.0).astype(jnp.bfloat16)


def pack_kernel(
    depth,
    bits_hbm,
    kappa_hbm,
    observed_hbm,
    up_ref,
    down_ref,
    cross_ref,
    bits_ref,
    kappa_ref,
    observed_ref,
    arrived,
):
    copies = [
        pltpu.make_async_copy(source, target, arrived.at[place])
        for place, (source, target) in enumerate(
            ((bits_hbm, bits_ref), (kappa_hbm, kappa_ref), (observed_hbm, observed_ref))
        )
    ]
    for copy in copies:
        copy.start()
    level = lax.axis_index("level")
    first = level == 0
    per_tile = LANES // EDGE
    tiles = depth // per_tile
    slot_ids = (lane_ids((ROWS, LANES)) % (LANES // 2)) // (EDGE // 2)
    same_columns, cross_columns = columns_of(level), columns_of(1 - level)
    for which in range(2):
        base = which * (depth + tiles)
        copies[which].wait()
        for refs, chosen in (((up_ref, down_ref), same_columns), ((cross_ref,), cross_columns)):
            if which == 0:
                values = (2 * bits_ref[...] - 1).astype(jnp.float32).reshape(depth * ROWS, 2 * LANES)
                picked = jnp.dot(
                    values.astype(jnp.bfloat16), chosen, preferred_element_type=jnp.float32
                )
            else:
                picked = pick(kappa_ref[...].reshape(depth * ROWS, 2 * LANES), chosen)
            picked = picked.reshape(depth, ROWS, 2 * LANES)
            for ref in refs:
                ref[base : base + depth] = picked[:, :, :LANES]
            for tile in range(tiles):
                packed = picked[tile * per_tile, :, LANES:]
                for slot in range(1, per_tile):
                    packed = jnp.where(
                        slot_ids == slot, picked[tile * per_tile + slot, :, LANES:], packed
                    )
                for ref in refs:
                    ref[base + depth + tile] = packed
    copies[2].wait()
    base = 2 * (depth + tiles)
    in_low = lax.axis_index("probe") < lax.axis_size("probe") // 2

    def half(value):
        return jnp.where(in_low, value[..., :LANES], value[..., LANES:])

    top = half(observed_ref[:, ROWS - 1, :])
    bottom = half(observed_ref[:, 0, :])
    for tile in range(depth // ROWS):
        up_ref[base + tile] = top[tile * ROWS : (tile + 1) * ROWS]
        down_ref[base + tile] = bottom[tile * ROWS : (tile + 1) * ROWS]
    cross_ref[base] = jnp.where(first, half(observed_ref[depth - 1]), half(observed_ref[0]))


def beside(values):
    rows = values.shape[0]
    even, odd = values[:, :LANES], values[:, LANES:]
    y_sides = jnp.concatenate(
        [odd + pltpu.roll(odd, 1, 1), even + pltpu.roll(even, LANES - 1, 1)], axis=1
    )
    return (pltpu.roll(values, 1, 0) + pltpu.roll(values, rows - 1, 0)) + y_sides


def basis_kernel(
    depth,
    own_ref,
    own_far_ref,
    left_ref,
    left_far_ref,
    right_ref,
    right_far_ref,
    terms_ref,
    gram_ref,
    signs,
    half_diag,
    lower,
    upper,
    basis,
    forward,
    sides,
    backward,
    k_signs,
    k_basis,
    sums,
):
    levels = 2 * depth
    rows, columns = 3 * ROWS, 2 * LANES
    shape = (rows, columns)
    level = lax.axis_index("level")
    tile = lax.axis_index("tile")
    last_tile = lax.axis_size("tile") - 1
    per_tile = LANES // EDGE
    tiles = depth // per_tile
    lanes, ids = lane_ids(shape), row_ids(shape)
    half = LANES // 2
    lanes = lanes % LANES
    near = jnp.where(level == 0, half, LANES - EDGE // 2)
    inside = (lanes < half) | ((lanes >= near) & (lanes < near + EDGE // 2))
    inside = inside & (ids >= jnp.where(tile > 0, 0, ROWS))
    inside = inside & (ids < jnp.where(tile < last_tile, 3 * ROWS, 2 * ROWS))
    mask = jnp.where(inside, 1.0, 0.0)
    half_mask = 0.5 * mask
    zero = jnp.zeros(shape, jnp.float32)
    own = (slice(ROWS, 2 * ROWS), slice(0, 2 * LANES))
    mine = lane_ids((ROWS, LANES)) < half
    own_zero = jnp.zeros((ROWS, LANES), jnp.float32)

    signs[0] = zero
    signs[levels + 1] = zero
    backward[levels] = zero
    upper[levels] = zero
    basis[levels] = zero
    for far, pieces in enumerate(
        ((left_ref, own_ref, right_ref), (left_far_ref, own_far_ref, right_far_ref))
    ):
        start = depth * (level if far == 0 else 1 - level)

        def unpack(z, unused, pieces=pieces, start=start):
            group = z // per_tile
            shift = half + (half - EDGE // 2) * level - (EDGE // 2) * lax.rem(z, per_tile)
            shift = lax.rem(shift + LANES, LANES)

            def gather(base):
                evens, odds = [], []
                for piece in pieces:
                    main = piece[base + z]
                    edge = pltpu.roll(piece[base + depth + group], shift, 1)
                    evens.append(jnp.where(mine, main, edge))
                    odds.append(pltpu.roll(jnp.where(mine, edge, main), half, 1))
                return jnp.concatenate(
                    [jnp.concatenate(evens, axis=0), jnp.concatenate(odds, axis=0)], axis=1
                )

            signs[start + z + 1] = gather(0) * mask
            half_diag[start + z] = 0.5 * gather(depth + tiles) + (2.0 + VERTICAL)
            return unused

        lax.fori_loop(0, depth, unpack, 0, unroll=per_tile)

    def start_down(k, carry):
        ratio, value, from_end = carry
        ratio = mask / (half_diag[k] - ratio)
        here = signs[k + 1]
        value = ratio * (here + value)
        lower[k] = ratio
        forward[k] = value
        other = levels - 1 - k
        from_end = mask / (half_diag[other] - from_end)
        upper[other] = from_end
        image = half_diag[k] * here - (signs[k] + signs[k + 2]) - 0.5 * beside(here)
        k_signs[k] = image[own]
        return ratio, value, from_end

    lax.fori_loop(0, levels, start_down, (zero, zero, zero), unroll=GROUP)

    def start_up(step, carry):
        k = levels - 1 - step
        solved, value = carry
        solved = forward[k] + lower[k] * solved
        value = upper[k] * (solved + value)
        backward[k] = value
        return solved, value

    lax.fori_loop(0, levels, start_up, (zero, zero), unroll=GROUP)

    place = 0
    for index in range(ITERS):
        final = index + 1 == ITERS

        def next_basis(k, previous, index=index):
            solved = backward[k] + upper[k] * previous
            if index == 0:
                value = solved
            elif SHIFTS[index - 1] == 0.0:
                value = -solved
            else:
                value = SHIFTS[index - 1] * basis[k] - solved
            return solved, value

        def down(group, carry, index=index, final=final, next_basis=next_basis):
            solved, above, here, value, *totals = carry
            products = []
            for step in range(GROUP):
                k = group * GROUP + step
                solved, below = next_basis(k + 1, solved)
                if not final:
                    basis[k + 1] = below
                side = beside(here)
                image = half_diag[k] * here - (above + below) - half_mask * side
                if not final:
                    value = lower[k] * (beside(image) + value)
                    forward[k] = value
                    sides[k] = side
                my_sign, my_basis, my_image = signs[k + 1][own], here[own], image[own]
                term = my_basis * k_signs[k] + my_image * my_sign
                terms_ref[index, k] = jnp.where(
                    mine, term[:, :LANES], pltpu.roll(term[:, LANES:], half, 1)
                )
                if not final:
                    k_basis[index, k] = my_image
                factors = [(k_basis[other, k], my_image) for other in range(index)]
                factors += [(my_image, my_image), (my_basis, my_sign)]
                products.append(
                    [a[:, :LANES] * b[:, :LANES] + a[:, LANES:] * b[:, LANES:] for a, b in factors]
                )
                above, here = here, below
            for slot in range(index + 2):
                for four in range(0, GROUP, 4):
                    added = (products[four][slot] + products[four + 1][slot]) + (
                        products[four + 2][slot] + products[four + 3][slot]
                    )
                    totals[2 * slot], rest = two_sum(totals[2 * slot], added)
                    totals[2 * slot + 1] = totals[2 * slot + 1] + rest
            return (solved, above, here, value, *totals)

        solved, here = next_basis(0, zero)
        if not final:
            basis[0] = here
        carry = lax.fori_loop(
            0,
            levels // GROUP,
            down,
            (solved, zero, here, zero) + (own_zero,) * (2 * (index + 2)),
        )
        totals = [jnp.where(mine, total, 0.0) for total in carry[4:]]
        for slot in range(index + 1):
            sums[2 * (place + slot)] = totals[2 * slot]
            sums[2 * (place + slot) + 1] = totals[2 * slot + 1]
        place += index + 1
        sums[2 * (len(PAIRS) + index)] = totals[2 * index + 2]
        sums[2 * (len(PAIRS) + index) + 1] = totals[2 * index + 3]
        if final:
            break

        def up(step, carry):
            k = levels - 1 - step
            solved, value = carry
            solved = forward[k] + lower[k] * solved
            value = upper[k] * ((sides[k] + solved) + value)
            backward[k] = value
            return solved, value

        lax.fori_loop(0, levels, up, (zero, zero), unroll=GROUP)

    ids = row_ids((ROWS, LANES))
    for block in range(SLOTS // ROWS):
        high, low = own_zero, own_zero
        for slot in range(block * ROWS, min((block + 1) * ROWS, COUNT)):
            pair = (sums[2 * slot], sums[2 * slot + 1])
            for shift in (4, 2, 1):
                pair = pair_add(pair, tuple(pltpu.roll(part, shift, 0) for part in pair))
            here = ids == slot - block * ROWS
            high, low = jnp.where(here, pair[0], high), jnp.where(here, pair[1], low)
        gram_ref[block * ROWS : (block + 1) * ROWS] = high
        gram_ref[SLOTS + block * ROWS : SLOTS + (block + 1) * ROWS] = low
    ones = jnp.ones((LANES, LANES), jnp.bfloat16)

    def lane_sum(part):
        return jnp.dot(part, ones, preferred_element_type=jnp.float32)

    high, middle, low = (lane_sum(part) for part in split_three(gram_ref[:SLOTS]))
    high, rest = two_sum(high, middle)
    gram_ref[:SLOTS] = high
    gram_ref[SLOTS:] = rest + (low + lane_sum(gram_ref[SLOTS:].astype(jnp.bfloat16)))


def solve_small(high, low):
    def entry(index):
        return tuple(jnp.broadcast_to(part[index : index + 1], (ROWS, LANES)) for part in (high, low))

    gram = {}
    for place, (i, j) in enumerate(PAIRS):
        gram[i, j] = gram[j, i] = entry(place)
    right = [entry(len(PAIRS) + j) for j in range(ITERS)]
    work = {key: pair[0] for key, pair in gram.items()}
    ratios, inverses = {}, []
    for i in range(ITERS):
        pivot = work[i, i]
        good = pivot > 1e-7 * gram[i, i][0]
        inverses.append(jnp.where(good, 1.0 / jnp.where(good, pivot, 1.0), 0.0))
        for r in range(i + 1, ITERS):
            ratios[r, i] = work[r, i] * inverses[i]
        for r in range(i + 1, ITERS):
            for c in range(i + 1, r + 1):
                work[r, c] = work[c, r] = work[r, c] - ratios[r, i] * work[c, i]

    def solve(values):
        values = list(values)
        for i in range(ITERS):
            for r in range(i + 1, ITERS):
                values[r] = values[r] - ratios[r, i] * values[i]
        values = [value * inverse for value, inverse in zip(values, inverses)]
        for i in reversed(range(ITERS)):
            for r in range(i):
                values[r] = values[r] - ratios[i, r] * values[i]
        return values

    found = solve([pair[0] for pair in right])
    for unused in range(2):
        rest = []
        for i in range(ITERS):
            total = right[i]
            for j in range(ITERS):
                product, error = two_product(gram[i, j][0], found[j])
                total = pair_add(total, (-product, -(error + gram[i, j][1] * found[j])))
            rest.append(total[0] + total[1])
        found = [a + b for a, b in zip(found, solve(rest))]
    return found


def combine_kernel(depth, terms_ref, *refs):
    gram_refs, (keep_ref, send_ref) = refs[:-2], refs[-2:]
    pairs = []
    for ref in gram_refs:
        for start in range(0, ref.shape[0], 2 * SLOTS):
            pairs.append((ref[start : start + SLOTS], ref[start + SLOTS : start + 2 * SLOTS]))
    while len(pairs) > 1:
        merged = [pair_add(pairs[i], pairs[i + 1]) for i in range(0, len(pairs) - 1, 2)]
        pairs = merged + pairs[2 * len(merged) :]
    found = solve_small(*pairs[0])
    core = lax.rem(lax.axis_index("probe"), 2)
    width = LANES // 4
    first_lanes = lane_ids((ROWS, LANES)) % (2 * width) < width
    pairs_deep = depth // 2

    def step(z, unused):
        for half in range(2):
            def total(k):
                value = found[0] * terms_ref[0, k]
                for j in range(1, ITERS):
                    value = value + found[j] * terms_ref[j, k]
                return value

            one = total(half * depth + z)
            two = total(half * depth + pairs_deep + z)
            low = jnp.where(first_lanes, one, pltpu.roll(two, width, 1))
            high = jnp.where(first_lanes, pltpu.roll(one, LANES - width, 1), two)
            keep_ref[half, z] = jnp.where(core == 0, low, high)
            send_ref[half, z] = jnp.where(core == 0, high, low)
        return unused

    lax.fori_loop(0, pairs_deep, step, 0, unroll=2)


def observed_kernel(
    depth, probes, kappa_ref, observed_ref, left_ref, right_ref, far_ref, factor_ref, data_ref
):
    level = lax.axis_index("level")
    tile = lax.axis_index("tile")
    last_tile = lax.axis_size("tile") - 1
    probe = lax.axis_index("probe")
    in_low = probe < probes // 2
    even = lax.rem(probe, 2) == 0
    width = LANES // 2
    lanes = lane_ids((ROWS, 2 * LANES))
    ids = row_ids((ROWS, LANES))
    base = left_ref.shape[0] - depth // ROWS

    def half(value):
        return jnp.where(in_low, value[..., :LANES], value[..., LANES:])

    def take(value):
        return jnp.where(even, value, pltpu.roll(value, width, 1))[:, :width]

    far_edge = far_ref[far_ref.shape[0] - 1]
    for z in range(depth):
        value = observed_ref[z]
        mine = half(value)
        y_sides = jnp.where(lanes > 0, pltpu.roll(value, 1, 1), 0.0) + jnp.where(
            lanes < 2 * LANES - 1, pltpu.roll(value, 2 * LANES - 1, 1), 0.0
        )
        left = left_ref[base + z // ROWS, z % ROWS : z % ROWS + 1, :]
        right = right_ref[base + z // ROWS, z % ROWS : z % ROWS + 1, :]
        before = jnp.where(ids > 0, pltpu.roll(mine, 1, 0), jnp.where(tile > 0, left, 0.0))
        after = jnp.where(
            ids < ROWS - 1, pltpu.roll(mine, ROWS - 1, 0), jnp.where(tile < last_tile, right, 0.0)
        )
        above = half(observed_ref[z - 1]) if z > 0 else jnp.where(level > 0, far_edge, 0.0)
        below = half(observed_ref[z + 1]) if z < depth - 1 else jnp.where(level == 0, far_edge, 0.0)
        kappa = half(kappa_ref[z])
        k_observed = (
            (kappa + (4.0 + 2.0 * VERTICAL)) * mine
            - (before + after)
            - half(y_sides)
            - VERTICAL * (above + below)
        )
        factor_ref[z] = take(kappa * (0.5 / probes))
        data_ref[z] = take(kappa * (2.0 * mine * k_observed))


def gradient_kernel(depth, trace_a_ref, trace_b_ref, factor_ref, data_ref, out_ref):
    width = LANES // 2
    square = (LANES, LANES)
    lane = lane_ids(square)
    source = (width // 2) * (lane // width) + (lane % width) // 2 + width * (lane % 2)
    chosen = jnp.where(row_ids(square) == source, 1.0, 0.0).astype(jnp.bfloat16)
    traces = pick((trace_a_ref[...] + trace_b_ref[...]).reshape(-1, LANES), chosen)
    traces = traces.reshape(depth // 2, ROWS, LANES)
    for z in range(depth // 2):
        out_ref[z] = factor_ref[z] * traces[z, :, :width] - data_ref[z]
        later = depth // 2 + z
        second = pltpu.roll(traces[z], width, 1)[:, :width]
        out_ref[later] = factor_ref[later] * second - data_ref[later]


def whole(count):
    return [pl.BlockSpec(memory_space=pltpu.VMEM)] * count


def body(probe_bits, kappa_sq, observed):
    probes, tile_count = lax.axis_size("probe"), lax.axis_size("tile")
    unused, depth, rows, columns = probe_bits.shape
    assert probe_bits.shape[0] == 1 and lax.axis_size("level") == 2 and probes == 4
    assert rows == ROWS and columns == 2 * LANES and depth % (LANES // EDGE) == 0
    params = pltpu.CompilerParams(vmem_limit_bytes=48 * 1024 * 1024)
    f32 = jnp.float32
    tiles = depth * EDGE // LANES
    field = 2 * (depth + tiles)
    near_shape = jax.ShapeDtypeStruct((field + depth // ROWS, ROWS, LANES), f32)
    far_shape = jax.ShapeDtypeStruct((field + 1, ROWS, LANES), f32)

    up_block, down_block, cross_block = pl.pallas_call(
        functools.partial(pack_kernel, depth),
        out_shape=(near_shape, near_shape, far_shape),
        in_specs=[pl.BlockSpec(memory_space=pltpu.HBM)] * 3,
        out_specs=tuple(whole(3)),
        scratch_shapes=[
            pltpu.VMEM((depth, rows, columns), jnp.int32),
            pltpu.VMEM((depth, rows, columns), f32),
            pltpu.VMEM((depth, rows, columns), f32),
            pltpu.SemaphoreType.DMA((3,)),
        ],
        compiler_params=params,
        name="pack",
    )(probe_bits[0], kappa_sq, observed)

    up_pairs = [(i, i + 1) for i in range(tile_count - 1)]
    down_pairs = [(i + 1, i) for i in range(tile_count - 1)]
    own_far = lax.ppermute(cross_block, "level", [(0, 1), (1, 0)])
    left = lax.ppermute(up_block, "tile", up_pairs)
    right = lax.ppermute(down_block, "tile", down_pairs)
    left_far = lax.ppermute(own_far, "tile", up_pairs)
    right_far = lax.ppermute(
        cross_block,
        ("tile", "level"),
        [(2 * a + level, 2 * b + 1 - level) for a, b in down_pairs for level in range(2)],
    )

    quarter = jax.ShapeDtypeStruct((depth, ROWS, columns // probes), f32)
    factor, data = pl.pallas_call(
        functools.partial(observed_kernel, depth, probes),
        out_shape=(quarter, quarter),
        in_specs=whole(5),
        out_specs=tuple(whole(2)),
        compiler_params=params,
        name="observed",
    )(kappa_sq, observed, left, right, own_far)

    levels = 2 * depth
    padded = pltpu.VMEM((levels + 1, 3 * ROWS, 2 * LANES), f32)
    plain = pltpu.VMEM((levels, 3 * ROWS, 2 * LANES), f32)
    terms, gram = pl.pallas_call(
        functools.partial(basis_kernel, depth),
        out_shape=(
            jax.ShapeDtypeStruct((ITERS, levels, ROWS, LANES), f32),
            jax.ShapeDtypeStruct((2 * SLOTS, LANES), f32),
        ),
        in_specs=whole(6),
        out_specs=tuple(whole(2)),
        scratch_shapes=[
            pltpu.VMEM((levels + 2, 3 * ROWS, 2 * LANES), f32),
            plain,
            plain,
            padded,
            padded,
            plain,
            plain,
            padded,
            pltpu.VMEM((levels, ROWS, 2 * LANES), f32),
            pltpu.VMEM((ITERS - 1, levels, ROWS, 2 * LANES), f32),
            pltpu.VMEM((2 * SLOTS, ROWS, LANES), f32),
        ],
        compiler_params=params,
        name="basis",
    )(up_block, own_far, left, left_far, right, right_far)

    both = jnp.concatenate([gram, lax.ppermute(gram, "level", [(0, 1), (1, 0)])], axis=0)
    if tile_count <= 4:
        partials = [both] + [
            lax.ppermute(both, "tile", [(i, (i + k) % tile_count) for i in range(tile_count)])
            for k in range(1, tile_count)
        ]
    else:
        partials = [lax.all_gather(both, "tile", axis=0, tiled=True)]
    piece = jax.ShapeDtypeStruct((2, depth // 2, ROWS, LANES), f32)
    keep, send = pl.pallas_call(
        functools.partial(combine_kernel, depth),
        out_shape=(piece, piece),
        in_specs=whole(1 + len(partials)),
        out_specs=tuple(whole(2)),
        compiler_params=params,
        name="combine",
    )(terms, *partials)

    summed = keep + lax.ppermute(send, "probe", [(0, 1), (1, 0), (2, 3), (3, 2)])
    half = lax.axis_index("probe") // 2
    straight = lax.dynamic_index_in_dim(summed, half, 0, keepdims=False)
    turned = lax.dynamic_index_in_dim(summed, 1 - half, 0, keepdims=False)

    def routes(flip):
        pairs = []
        for x in range(2):
            for core in range(2):
                for level in range(2):
                    target = x if not flip else 1 - x
                    pairs.append(((2 * x + core) * 2 + level, (2 * level + core) * 2 + target))
        return pairs

    trace_a = lax.ppermute(straight, ("probe", "level"), routes(False))
    trace_b = lax.ppermute(turned, ("probe", "level"), routes(True))
    return pl.pallas_call(
        functools.partial(gradient_kernel, depth),
        out_shape=quarter,
        in_specs=whole(4),
        out_specs=pl.BlockSpec(memory_space=pltpu.VMEM),
        compiler_params=params,
        name="gradient",
    )(trace_a, trace_b, factor, data)


def solution(mesh):
    in_specs = (
        P("probe", "level", "tile", None),
        P("level", "tile", None),
        P("level", "tile", None),
    )
    out_specs = P("level", "tile", "probe")
    return jax.shard_map(body, mesh=mesh, in_specs=in_specs, out_specs=out_specs, check_vma=False)
```

```python
import functools

import jax
import jax.numpy as jnp
from jax import lax
from jax.experimental import pallas as pl
from jax.experimental.pallas import tpu as pltpu
from jax.sharding import PartitionSpec as P

ITERS = 4
VERTICAL = 2.0
LANES = 128
ROWS = 8
EDGE = 8
GROUP = 8
SHIFTS = (1.0, 0.0, -2.0)
PAIRS = [(i, j) for j in range(ITERS) for i in range(j + 1)]
COUNT = len(PAIRS) + ITERS
SLOTS = 16


def two_sum(a, b):
    total = a + b
    part = total - a
    return total, (a - (total - part)) + (b - part)


def two_product(a, b):
    def split(v):
        big = v * 4097.0
        high = big - (big - v)
        return high, v - high

    product = a * b
    a_high, a_low = split(a)
    b_high, b_low = split(b)
    return product, ((a_high * b_high - product) + a_high * b_low + a_low * b_high) + a_low * b_low


def pair_add(first, second):
    total, rest = two_sum(first[0], second[0])
    rest = rest + (first[1] + second[1])
    high = total + rest
    return high, rest - (high - total)


def lane_ids(shape):
    return lax.broadcasted_iota(jnp.int32, shape, len(shape) - 1)


def row_ids(shape):
    return lax.broadcasted_iota(jnp.int32, shape, len(shape) - 2)


def split_three(values):
    high = values.astype(jnp.bfloat16)
    rest = values - high.astype(jnp.float32)
    middle = rest.astype(jnp.bfloat16)
    low = (rest - middle.astype(jnp.float32)).astype(jnp.bfloat16)
    return high, middle, low


def pick(values, chosen):
    high, middle, low = (
        jnp.dot(part, chosen, preferred_element_type=jnp.float32) for part in split_three(values)
    )
    return high + (middle + low)


def columns_of(half):
    shape = (2 * LANES, 2 * LANES)
    ids, lane = row_ids(shape), lane_ids(shape)
    odd = (lane // (LANES // 2)) % 2
    main = LANES * half + 2 * (lane % (LANES // 2)) + odd
    edge = LANES - EDGE * half + 2 * (lane % (EDGE // 2)) + odd
    wanted = jnp.where(lane < LANES, main, edge)
    return jnp.where(ids == wanted, 1.0, 0.0).astype(jnp.bfloat16)


def pack_kernel(
    depth,
    bits_hbm,
    kappa_hbm,
    observed_hbm,
    even_ref,
    odd_ref,
    cross_ref,
    bits_ref,
    kappa_ref,
    observed_ref,
    arrived,
):
    copies = [
        pltpu.make_async_copy(source, target, arrived.at[place])
        for place, (source, target) in enumerate(
            ((bits_hbm, bits_ref), (kappa_hbm, kappa_ref), (observed_hbm, observed_ref))
        )
    ]
    for copy in copies:
        copy.start()
    level = lax.axis_index("level")
    first = level == 0
    per_tile = LANES // EDGE
    tiles = depth // per_tile
    slot_ids = (lane_ids((ROWS, LANES)) % (LANES // 2)) // (EDGE // 2)
    same_columns, cross_columns = columns_of(level), columns_of(1 - level)
    for which in range(2):
        base = which * (depth + tiles)
        copies[which].wait()
        for refs, chosen in (((even_ref, odd_ref), same_columns), ((cross_ref,), cross_columns)):
            if which == 0:
                values = (2 * bits_ref[...] - 1).astype(jnp.float32).reshape(depth * ROWS, 2 * LANES)
                picked = jnp.dot(
                    values.astype(jnp.bfloat16), chosen, preferred_element_type=jnp.float32
                )
            else:
                picked = pick(kappa_ref[...].reshape(depth * ROWS, 2 * LANES), chosen)
            picked = picked.reshape(depth, ROWS, 2 * LANES)
            for ref in refs:
                ref[base : base + depth] = picked[:, :, :LANES]
            for tile in range(tiles):
                packed = picked[tile * per_tile, :, LANES:]
                for slot in range(1, per_tile):
                    packed = jnp.where(
                        slot_ids == slot, picked[tile * per_tile + slot, :, LANES:], packed
                    )
                for ref in refs:
                    ref[base + depth + tile] = packed
    copies[2].wait()
    base = 2 * (depth + tiles)
    in_low = lax.axis_index("probe") < lax.axis_size("probe") // 2

    def half(value):
        return jnp.where(in_low, value[..., :LANES], value[..., LANES:])

    top = half(observed_ref[:, ROWS - 1, :])
    bottom = half(observed_ref[:, 0, :])
    goes_up = lax.rem(lax.axis_index("tile"), 2) == 0
    for tile in range(depth // ROWS):
        here = slice(tile * ROWS, (tile + 1) * ROWS)
        even_ref[base + tile] = jnp.where(goes_up, top[here], bottom[here])
        odd_ref[base + tile] = jnp.where(goes_up, bottom[here], top[here])
    cross_ref[base] = jnp.where(first, half(observed_ref[depth - 1]), half(observed_ref[0]))


def beside(values):
    rows = values.shape[0]
    even, odd = values[:, :LANES], values[:, LANES:]
    y_sides = jnp.concatenate(
        [odd + pltpu.roll(odd, 1, 1), even + pltpu.roll(even, LANES - 1, 1)], axis=1
    )
    return (pltpu.roll(values, 1, 0) + pltpu.roll(values, rows - 1, 0)) + y_sides


def basis_kernel(
    depth,
    own_ref,
    own_far_ref,
    even_ref,
    even_far_ref,
    odd_ref,
    odd_far_ref,
    terms_ref,
    gram_ref,
    signs,
    half_diag,
    lower,
    upper,
    basis,
    forward,
    sides,
    backward,
    k_signs,
    k_basis,
    sums,
):
    levels = 2 * depth
    rows, columns = 3 * ROWS, 2 * LANES
    shape = (rows, columns)
    level = lax.axis_index("level")
    tile = lax.axis_index("tile")
    last_tile = lax.axis_size("tile") - 1
    per_tile = LANES // EDGE
    tiles = depth // per_tile
    lanes, ids = lane_ids(shape), row_ids(shape)
    half = LANES // 2
    lanes = lanes % LANES
    near = jnp.where(level == 0, half, LANES - EDGE // 2)
    inside = (lanes < half) | ((lanes >= near) & (lanes < near + EDGE // 2))
    inside = inside & (ids >= jnp.where(tile > 0, 0, ROWS))
    inside = inside & (ids < jnp.where(tile < last_tile, 3 * ROWS, 2 * ROWS))
    mask = jnp.where(inside, 1.0, 0.0)
    half_mask = 0.5 * mask
    zero = jnp.zeros(shape, jnp.float32)
    own = (slice(ROWS, 2 * ROWS), slice(0, 2 * LANES))
    mine = lane_ids((ROWS, LANES)) < half
    own_zero = jnp.zeros((ROWS, LANES), jnp.float32)

    signs[0] = zero
    signs[levels + 1] = zero
    backward[levels] = zero
    upper[levels] = zero
    basis[levels] = zero
    from_even = lax.rem(tile, 2) == 1
    for far, pieces in enumerate(
        ((even_ref, own_ref, odd_ref), (even_far_ref, own_far_ref, odd_far_ref))
    ):
        start = depth * (level if far == 0 else 1 - level)

        def unpack(z, unused, pieces=pieces, start=start):
            group = z // per_tile
            shift = half + (half - EDGE // 2) * level - (EDGE // 2) * lax.rem(z, per_tile)
            shift = lax.rem(shift + LANES, LANES)

            def gather(base):
                evens, odds = [], []
                first, second, third = [
                    (piece[base + z], piece[base + depth + group]) for piece in pieces
                ]
                left = [jnp.where(from_even, a, b) for a, b in zip(first, third)]
                right = [jnp.where(from_even, b, a) for a, b in zip(first, third)]
                for main, edge in (left, second, right):
                    edge = pltpu.roll(edge, shift, 1)
                    evens.append(jnp.where(mine, main, edge))
                    odds.append(pltpu.roll(jnp.where(mine, edge, main), half, 1))
                return jnp.concatenate(
                    [jnp.concatenate(evens, axis=0), jnp.concatenate(odds, axis=0)], axis=1
                )

            signs[start + z + 1] = gather(0) * mask
            half_diag[start + z] = 0.5 * gather(depth + tiles) + (2.0 + VERTICAL)
            return unused

        lax.fori_loop(0, depth, unpack, 0, unroll=per_tile)

    def start_down(k, carry):
        ratio, value, from_end = carry
        ratio = mask / (half_diag[k] - ratio)
        here = signs[k + 1]
        value = ratio * (here + value)
        lower[k] = ratio
        forward[k] = value
        other = levels - 1 - k
        from_end = mask / (half_diag[other] - from_end)
        upper[other] = from_end
        image = half_diag[k] * here - (signs[k] + signs[k + 2]) - 0.5 * beside(here)
        k_signs[k] = image[own]
        return ratio, value, from_end

    lax.fori_loop(0, levels, start_down, (zero, zero, zero), unroll=GROUP)

    def start_up(step, carry):
        k = levels - 1 - step
        solved, value = carry
        solved = forward[k] + lower[k] * solved
        value = upper[k] * (solved + value)
        backward[k] = value
        return solved, value

    lax.fori_loop(0, levels, start_up, (zero, zero), unroll=GROUP)

    place = 0
    for index in range(ITERS):
        final = index + 1 == ITERS

        def next_basis(k, previous, index=index):
            solved = backward[k] + upper[k] * previous
            if index == 0:
                value = solved
            elif SHIFTS[index - 1] == 0.0:
                value = -solved
            else:
                value = SHIFTS[index - 1] * basis[k] - solved
            return solved, value

        def down(group, carry, index=index, final=final, next_basis=next_basis):
            solved, above, here, value, *totals = carry
            products = []
            for step in range(GROUP):
                k = group * GROUP + step
                solved, below = next_basis(k + 1, solved)
                if not final:
                    basis[k + 1] = below
                side = beside(here)
                image = half_diag[k] * here - (above + below) - half_mask * side
                if not final:
                    value = lower[k] * (beside(image) + value)
                    forward[k] = value
                    sides[k] = side
                my_sign, my_basis, my_image = signs[k + 1][own], here[own], image[own]
                term = my_basis * k_signs[k] + my_image * my_sign
                terms_ref[index, k] = jnp.where(
                    mine, term[:, :LANES], pltpu.roll(term[:, LANES:], half, 1)
                )
                if not final:
                    k_basis[index, k] = my_image
                factors = [(k_basis[other, k], my_image) for other in range(index)]
                factors += [(my_image, my_image), (my_basis, my_sign)]
                products.append(
                    [a[:, :LANES] * b[:, :LANES] + a[:, LANES:] * b[:, LANES:] for a, b in factors]
                )
                above, here = here, below
            for slot in range(index + 2):
                for four in range(0, GROUP, 4):
                    added = (products[four][slot] + products[four + 1][slot]) + (
                        products[four + 2][slot] + products[four + 3][slot]
                    )
                    totals[2 * slot], rest = two_sum(totals[2 * slot], added)
                    totals[2 * slot + 1] = totals[2 * slot + 1] + rest
            return (solved, above, here, value, *totals)

        solved, here = next_basis(0, zero)
        if not final:
            basis[0] = here
        carry = lax.fori_loop(
            0,
            levels // GROUP,
            down,
            (solved, zero, here, zero) + (own_zero,) * (2 * (index + 2)),
        )
        totals = [jnp.where(mine, total, 0.0) for total in carry[4:]]
        for slot in range(index + 1):
            sums[2 * (place + slot)] = totals[2 * slot]
            sums[2 * (place + slot) + 1] = totals[2 * slot + 1]
        place += index + 1
        sums[2 * (len(PAIRS) + index)] = totals[2 * index + 2]
        sums[2 * (len(PAIRS) + index) + 1] = totals[2 * index + 3]
        if final:
            break

        def up(step, carry):
            k = levels - 1 - step
            solved, value = carry
            solved = forward[k] + lower[k] * solved
            value = upper[k] * ((sides[k] + solved) + value)
            backward[k] = value
            return solved, value

        lax.fori_loop(0, levels, up, (zero, zero), unroll=GROUP)

    ids = row_ids((ROWS, LANES))
    for block in range(SLOTS // ROWS):
        high, low = own_zero, own_zero
        for slot in range(block * ROWS, min((block + 1) * ROWS, COUNT)):
            pair = (sums[2 * slot], sums[2 * slot + 1])
            for shift in (4, 2, 1):
                pair = pair_add(pair, tuple(pltpu.roll(part, shift, 0) for part in pair))
            here = ids == slot - block * ROWS
            high, low = jnp.where(here, pair[0], high), jnp.where(here, pair[1], low)
        gram_ref[block * ROWS : (block + 1) * ROWS] = high
        gram_ref[SLOTS + block * ROWS : SLOTS + (block + 1) * ROWS] = low
    ones = jnp.ones((LANES, LANES), jnp.bfloat16)

    def lane_sum(part):
        return jnp.dot(part, ones, preferred_element_type=jnp.float32)

    high, middle, low = (lane_sum(part) for part in split_three(gram_ref[:SLOTS]))
    high, rest = two_sum(high, middle)
    gram_ref[:SLOTS] = high
    gram_ref[SLOTS:] = rest + (low + lane_sum(gram_ref[SLOTS:].astype(jnp.bfloat16)))


def solve_small(high, low):
    def entry(index):
        return tuple(jnp.broadcast_to(part[index : index + 1], (ROWS, LANES)) for part in (high, low))

    gram = {}
    for place, (i, j) in enumerate(PAIRS):
        gram[i, j] = gram[j, i] = entry(place)
    right = [entry(len(PAIRS) + j) for j in range(ITERS)]
    work = {key: pair[0] for key, pair in gram.items()}
    ratios, inverses = {}, []
    for i in range(ITERS):
        pivot = work[i, i]
        good = pivot > 1e-7 * gram[i, i][0]
        inverses.append(jnp.where(good, 1.0 / jnp.where(good, pivot, 1.0), 0.0))
        for r in range(i + 1, ITERS):
            ratios[r, i] = work[r, i] * inverses[i]
        for r in range(i + 1, ITERS):
            for c in range(i + 1, r + 1):
                work[r, c] = work[c, r] = work[r, c] - ratios[r, i] * work[c, i]

    def solve(values):
        values = list(values)
        for i in range(ITERS):
            for r in range(i + 1, ITERS):
                values[r] = values[r] - ratios[r, i] * values[i]
        values = [value * inverse for value, inverse in zip(values, inverses)]
        for i in reversed(range(ITERS)):
            for r in range(i):
                values[r] = values[r] - ratios[i, r] * values[i]
        return values

    found = solve([pair[0] for pair in right])
    for unused in range(2):
        rest = []
        for i in range(ITERS):
            total = right[i]
            for j in range(ITERS):
                product, error = two_product(gram[i, j][0], found[j])
                total = pair_add(total, (-product, -(error + gram[i, j][1] * found[j])))
            rest.append(total[0] + total[1])
        found = [a + b for a, b in zip(found, solve(rest))]
    return found


def combine_kernel(depth, terms_ref, *refs):
    gram_refs, (keep_ref, send_ref) = refs[:-2], refs[-2:]
    pairs = []
    for ref in gram_refs:
        for start in range(0, ref.shape[0], 2 * SLOTS):
            pairs.append((ref[start : start + SLOTS], ref[start + SLOTS : start + 2 * SLOTS]))
    while len(pairs) > 1:
        merged = [pair_add(pairs[i], pairs[i + 1]) for i in range(0, len(pairs) - 1, 2)]
        pairs = merged + pairs[2 * len(merged) :]
    found = solve_small(*pairs[0])
    core = lax.rem(lax.axis_index("probe"), 2)
    width = LANES // 4
    first_lanes = lane_ids((ROWS, LANES)) % (2 * width) < width
    pairs_deep = depth // 2

    def step(z, unused):
        for half in range(2):
            def total(k):
                value = found[0] * terms_ref[0, k]
                for j in range(1, ITERS):
                    value = value + found[j] * terms_ref[j, k]
                return value

            one = total(half * depth + z)
            two = total(half * depth + pairs_deep + z)
            low = jnp.where(first_lanes, one, pltpu.roll(two, width, 1))
            high = jnp.where(first_lanes, pltpu.roll(one, LANES - width, 1), two)
            keep_ref[half, z] = jnp.where(core == 0, low, high)
            send_ref[half, z] = jnp.where(core == 0, high, low)
        return unused

    lax.fori_loop(0, pairs_deep, step, 0, unroll=2)


def observed_kernel(
    depth, probes, kappa_ref, observed_ref, even_ref, odd_ref, far_ref, factor_ref, data_ref
):
    level = lax.axis_index("level")
    tile = lax.axis_index("tile")
    last_tile = lax.axis_size("tile") - 1
    probe = lax.axis_index("probe")
    in_low = probe < probes // 2
    even = lax.rem(probe, 2) == 0
    width = LANES // 2
    lanes = lane_ids((ROWS, 2 * LANES))
    ids = row_ids((ROWS, LANES))
    base = even_ref.shape[0] - depth // ROWS
    from_even = lax.rem(tile, 2) == 1

    def half(value):
        return jnp.where(in_low, value[..., :LANES], value[..., LANES:])

    def take(value):
        return jnp.where(even, value, pltpu.roll(value, width, 1))[:, :width]

    far_edge = far_ref[far_ref.shape[0] - 1]
    for z in range(depth):
        value = observed_ref[z]
        mine = half(value)
        y_sides = jnp.where(lanes > 0, pltpu.roll(value, 1, 1), 0.0) + jnp.where(
            lanes < 2 * LANES - 1, pltpu.roll(value, 2 * LANES - 1, 1), 0.0
        )
        first = even_ref[base + z // ROWS, z % ROWS : z % ROWS + 1, :]
        second = odd_ref[base + z // ROWS, z % ROWS : z % ROWS + 1, :]
        left, right = jnp.where(from_even, first, second), jnp.where(from_even, second, first)
        before = jnp.where(ids > 0, pltpu.roll(mine, 1, 0), jnp.where(tile > 0, left, 0.0))
        after = jnp.where(
            ids < ROWS - 1, pltpu.roll(mine, ROWS - 1, 0), jnp.where(tile < last_tile, right, 0.0)
        )
        above = half(observed_ref[z - 1]) if z > 0 else jnp.where(level > 0, far_edge, 0.0)
        below = half(observed_ref[z + 1]) if z < depth - 1 else jnp.where(level == 0, far_edge, 0.0)
        kappa = half(kappa_ref[z])
        k_observed = (
            (kappa + (4.0 + 2.0 * VERTICAL)) * mine
            - (before + after)
            - half(y_sides)
            - VERTICAL * (above + below)
        )
        factor_ref[z] = take(kappa * (0.5 / probes))
        data_ref[z] = take(kappa * (2.0 * mine * k_observed))


def gradient_kernel(depth, trace_a_ref, trace_b_ref, factor_ref, data_ref, out_ref):
    width = LANES // 2
    square = (LANES, LANES)
    lane = lane_ids(square)
    source = (width // 2) * (lane // width) + (lane % width) // 2 + width * (lane % 2)
    chosen = jnp.where(row_ids(square) == source, 1.0, 0.0).astype(jnp.bfloat16)
    traces = pick((trace_a_ref[...] + trace_b_ref[...]).reshape(-1, LANES), chosen)
    traces = traces.reshape(depth // 2, ROWS, LANES)
    for z in range(depth // 2):
        out_ref[z] = factor_ref[z] * traces[z, :, :width] - data_ref[z]
        later = depth // 2 + z
        second = pltpu.roll(traces[z], width, 1)[:, :width]
        out_ref[later] = factor_ref[later] * second - data_ref[later]


def whole(count):
    return [pl.BlockSpec(memory_space=pltpu.VMEM)] * count


def body(probe_bits, kappa_sq, observed):
    probes, tile_count = lax.axis_size("probe"), lax.axis_size("tile")
    unused, depth, rows, columns = probe_bits.shape
    assert probe_bits.shape[0] == 1 and lax.axis_size("level") == 2 and probes == 4
    assert rows == ROWS and columns == 2 * LANES and depth % (LANES // EDGE) == 0
    params = pltpu.CompilerParams(vmem_limit_bytes=48 * 1024 * 1024)
    f32 = jnp.float32
    tiles = depth * EDGE // LANES
    field = 2 * (depth + tiles)
    near_shape = jax.ShapeDtypeStruct((field + depth // ROWS, ROWS, LANES), f32)
    far_shape = jax.ShapeDtypeStruct((field + 1, ROWS, LANES), f32)

    even_block, odd_block, cross_block = pl.pallas_call(
        functools.partial(pack_kernel, depth),
        out_shape=(near_shape, near_shape, far_shape),
        in_specs=[pl.BlockSpec(memory_space=pltpu.HBM)] * 3,
        out_specs=tuple(whole(3)),
        scratch_shapes=[
            pltpu.VMEM((depth, rows, columns), jnp.int32),
            pltpu.VMEM((depth, rows, columns), f32),
            pltpu.VMEM((depth, rows, columns), f32),
            pltpu.SemaphoreType.DMA((3,)),
        ],
        compiler_params=params,
        name="pack",
    )(
        *(
            pltpu.with_memory_space_constraint(value, pltpu.HBM)
            for value in (probe_bits[0], kappa_sq, observed)
        )
    )

    def swaps(pairs):
        return [way for a, b in pairs for way in ((a, b), (b, a))]

    even_pairs = [(i, i + 1) for i in range(0, tile_count - 1, 2)]
    odd_pairs = [(i, i + 1) for i in range(1, tile_count - 1, 2)]
    own_far = lax.ppermute(cross_block, "level", swaps([(0, 1)]))
    even = lax.ppermute(even_block, "tile", swaps(even_pairs))
    odd = lax.ppermute(odd_block, "tile", swaps(odd_pairs))
    odd_far = lax.ppermute(own_far, "tile", swaps(odd_pairs))
    even_far = lax.ppermute(
        cross_block,
        ("tile", "level"),
        swaps([(2 * a + level, 2 * b + 1 - level) for a, b in even_pairs for level in range(2)]),
    )

    quarter = jax.ShapeDtypeStruct((depth, ROWS, columns // probes), f32)
    factor, data = pl.pallas_call(
        functools.partial(observed_kernel, depth, probes),
        out_shape=(quarter, quarter),
        in_specs=whole(5),
        out_specs=tuple(whole(2)),
        compiler_params=params,
        name="observed",
    )(kappa_sq, observed, even, odd, own_far)

    levels = 2 * depth
    padded = pltpu.VMEM((levels + 1, 3 * ROWS, 2 * LANES), f32)
    plain = pltpu.VMEM((levels, 3 * ROWS, 2 * LANES), f32)
    terms, gram = pl.pallas_call(
        functools.partial(basis_kernel, depth),
        out_shape=(
            jax.ShapeDtypeStruct((ITERS, levels, ROWS, LANES), f32),
            jax.ShapeDtypeStruct((2 * SLOTS, LANES), f32),
        ),
        in_specs=whole(6),
        out_specs=tuple(whole(2)),
        scratch_shapes=[
            pltpu.VMEM((levels + 2, 3 * ROWS, 2 * LANES), f32),
            plain,
            plain,
            padded,
            padded,
            plain,
            plain,
            padded,
            pltpu.VMEM((levels, ROWS, 2 * LANES), f32),
            pltpu.VMEM((ITERS - 1, levels, ROWS, 2 * LANES), f32),
            pltpu.VMEM((2 * SLOTS, ROWS, LANES), f32),
        ],
        compiler_params=params,
        name="basis",
    )(even_block, own_far, even, even_far, odd, odd_far)

    both = jnp.concatenate([gram, lax.ppermute(gram, "level", [(0, 1), (1, 0)])], axis=0)
    if tile_count in (2, 4):
        partials = [both] + [
            lax.ppermute(both, "tile", [(i, i ^ k) for i in range(tile_count)])
            for k in range(1, tile_count)
        ]
    else:
        partials = [lax.all_gather(both, "tile", axis=0, tiled=True)]
    piece = jax.ShapeDtypeStruct((2, depth // 2, ROWS, LANES), f32)
    keep, send = pl.pallas_call(
        functools.partial(combine_kernel, depth),
        out_shape=(piece, piece),
        in_specs=whole(1 + len(partials)),
        out_specs=tuple(whole(2)),
        compiler_params=params,
        name="combine",
    )(terms, *partials)

    summed = keep + lax.ppermute(send, "probe", [(0, 1), (1, 0), (2, 3), (3, 2)])
    half = lax.axis_index("probe") // 2
    straight = lax.dynamic_index_in_dim(summed, half, 0, keepdims=False)
    turned = lax.dynamic_index_in_dim(summed, 1 - half, 0, keepdims=False)

    def routes(flip):
        pairs = []
        for x in range(2):
            for core in range(2):
                for level in range(2):
                    target = x if not flip else 1 - x
                    pairs.append(((2 * x + core) * 2 + level, (2 * level + core) * 2 + target))
        return pairs

    trace_a = lax.ppermute(straight, ("probe", "level"), routes(False))
    trace_b = lax.ppermute(turned, ("probe", "level"), routes(True))
    return pl.pallas_call(
        functools.partial(gradient_kernel, depth),
        out_shape=quarter,
        in_specs=whole(4),
        out_specs=pl.BlockSpec(memory_space=pltpu.VMEM),
        compiler_params=params,
        name="gradient",
    )(trace_a, trace_b, factor, data)


def solution(mesh):
    in_specs = (
        P("probe", "level", "tile", None),
        P("level", "tile", None),
        P("level", "tile", None),
    )
    out_specs = P("level", "tile", "probe")
    return jax.shard_map(body, mesh=mesh, in_specs=in_specs, out_specs=out_specs, check_vma=False)
```

```python
import functools

import jax
import jax.numpy as jnp
from jax import lax
from jax.experimental import pallas as pl
from jax.experimental.pallas import tpu as pltpu
from jax.sharding import PartitionSpec as P

ITERS = 4
VERTICAL = 2.0
LANES = 128
ROWS = 8
EDGE = 8
GROUP = 8
SHIFTS = (1.0, 0.0, -2.0)
PAIRS = [(i, j) for j in range(ITERS) for i in range(j + 1)]
COUNT = len(PAIRS) + ITERS
SLOTS = 16


def two_sum(a, b):
    total = a + b
    part = total - a
    return total, (a - (total - part)) + (b - part)


def two_product(a, b):
    def split(v):
        big = v * 4097.0
        high = big - (big - v)
        return high, v - high

    product = a * b
    a_high, a_low = split(a)
    b_high, b_low = split(b)
    return product, ((a_high * b_high - product) + a_high * b_low + a_low * b_high) + a_low * b_low


def pair_add(first, second):
    total, rest = two_sum(first[0], second[0])
    rest = rest + (first[1] + second[1])
    high = total + rest
    return high, rest - (high - total)


def lane_ids(shape):
    return lax.broadcasted_iota(jnp.int32, shape, len(shape) - 1)


def row_ids(shape):
    return lax.broadcasted_iota(jnp.int32, shape, len(shape) - 2)


def split_three(values):
    high = values.astype(jnp.bfloat16)
    rest = values - high.astype(jnp.float32)
    middle = rest.astype(jnp.bfloat16)
    low = (rest - middle.astype(jnp.float32)).astype(jnp.bfloat16)
    return high, middle, low


def pick(values, chosen):
    high, middle, low = (
        jnp.dot(part, chosen, preferred_element_type=jnp.float32) for part in split_three(values)
    )
    return high + (middle + low)


def columns_of(half):
    shape = (2 * LANES, 2 * LANES)
    ids, lane = row_ids(shape), lane_ids(shape)
    odd = (lane // (LANES // 2)) % 2
    main = LANES * half + 2 * (lane % (LANES // 2)) + odd
    edge = LANES - EDGE * half + 2 * (lane % (EDGE // 2)) + odd
    wanted = jnp.where(lane < LANES, main, edge)
    return jnp.where(ids == wanted, 1.0, 0.0).astype(jnp.bfloat16)


def pack_kernel(
    depth,
    bits_hbm,
    kappa_hbm,
    observed_hbm,
    own_ref,
    even_ref,
    odd_ref,
    cross_ref,
    bits_ref,
    kappa_ref,
    observed_ref,
    arrived,
):
    copies = [
        pltpu.make_async_copy(source, target, arrived.at[place])
        for place, (source, target) in enumerate(
            ((bits_hbm, bits_ref), (kappa_hbm, kappa_ref), (observed_hbm, observed_ref))
        )
    ]
    for copy in copies:
        copy.start()
    level = lax.axis_index("level")
    first = level == 0
    in_first_core = lax.rem(lax.axis_index("probe"), 2) == 0
    per_tile = LANES // EDGE
    tiles = depth // per_tile
    field = depth + tiles
    slot_ids = (lane_ids((ROWS, LANES)) % (LANES // 2)) // (EDGE // 2)
    same_columns, cross_columns = columns_of(level), columns_of(1 - level)

    def blocks(picked):
        picked = picked.reshape(depth, ROWS, 2 * LANES)
        edges = []
        for tile in range(tiles):
            packed = picked[tile * per_tile, :, LANES:]
            for slot in range(1, per_tile):
                packed = jnp.where(slot_ids == slot, picked[tile * per_tile + slot, :, LANES:], packed)
            edges.append(packed)
        return [picked[z, :, :LANES] for z in range(depth)], edges

    def write(refs, base, values):
        for place, value in enumerate(values):
            for ref in refs:
                ref[base + place] = value

    copies[0].wait()
    signs = (2 * bits_ref[...] - 1).astype(jnp.float32).reshape(depth * ROWS, 2 * LANES)
    signs = signs.astype(jnp.bfloat16)
    for refs, chosen in (((own_ref, even_ref, odd_ref), same_columns), ((cross_ref,), cross_columns)):
        main, edges = blocks(jnp.dot(signs, chosen, preferred_element_type=jnp.float32))
        write(refs, 0, main + edges)
    copies[1].wait()
    kappa = kappa_ref[...].reshape(depth * ROWS, 2 * LANES)
    for refs, chosen in (((even_ref, odd_ref), same_columns), ((cross_ref,), cross_columns)):
        main, edges = blocks(pick(kappa, chosen))
        if len(refs) == 2:
            write((own_ref,), field, main + edges)
        low = main[: depth // 2] + edges[: tiles // 2]
        high = main[depth // 2 :] + edges[tiles // 2 :]
        write(refs, field, [jnp.where(in_first_core, a, b) for a, b in zip(low, high)])
    copies[2].wait()
    base = field + field // 2
    in_low = lax.axis_index("probe") < lax.axis_size("probe") // 2

    def half(value):
        return jnp.where(in_low, value[..., :LANES], value[..., LANES:])

    top = half(observed_ref[:, ROWS - 1, :])
    bottom = half(observed_ref[:, 0, :])
    goes_up = lax.rem(lax.axis_index("tile"), 2) == 0
    for tile in range(depth // ROWS):
        here = slice(tile * ROWS, (tile + 1) * ROWS)
        even_ref[base + tile] = jnp.where(goes_up, top[here], bottom[here])
        odd_ref[base + tile] = jnp.where(goes_up, bottom[here], top[here])
    cross_ref[base] = jnp.where(first, half(observed_ref[depth - 1]), half(observed_ref[0]))


def beside(values):
    rows = values.shape[0]
    even, odd = values[:, :LANES], values[:, LANES:]
    y_sides = jnp.concatenate(
        [odd + pltpu.roll(odd, 1, 1), even + pltpu.roll(even, LANES - 1, 1)], axis=1
    )
    return (pltpu.roll(values, 1, 0) + pltpu.roll(values, rows - 1, 0)) + y_sides


def inside_mask():
    shape = (3 * ROWS, 2 * LANES)
    tile = lax.axis_index("tile")
    half = LANES // 2
    lanes, ids = lane_ids(shape) % LANES, row_ids(shape)
    near = jnp.where(lax.axis_index("level") == 0, half, LANES - EDGE // 2)
    inside = (lanes < half) | ((lanes >= near) & (lanes < near + EDGE // 2))
    inside = inside & (ids >= jnp.where(tile > 0, 0, ROWS))
    inside = inside & (ids < jnp.where(tile < lax.axis_size("tile") - 1, 3 * ROWS, 2 * ROWS))
    return jnp.where(inside, 1.0, 0.0)


def join(z, even, own, odd):
    half, short = LANES // 2, EDGE // 2
    level = lax.axis_index("level")
    from_even = lax.rem(lax.axis_index("tile"), 2) == 1
    mine = lane_ids((ROWS, LANES)) < half
    shift = half + (half - short) * level - short * lax.rem(z, LANES // EDGE)
    shift = lax.rem(shift + LANES, LANES)
    left = [jnp.where(from_even, a, b) for a, b in zip(even, odd)]
    right = [jnp.where(from_even, b, a) for a, b in zip(even, odd)]
    evens, odds = [], []
    for main, edge in (left, own, right):
        edge = pltpu.roll(edge, shift, 1)
        evens.append(jnp.where(mine, main, edge))
        odds.append(pltpu.roll(jnp.where(mine, edge, main), half, 1))
    return jnp.concatenate([jnp.concatenate(evens, axis=0), jnp.concatenate(odds, axis=0)], axis=1)


def unpack(depth, signs, half_diag, mask, sign_pieces, kappa_pieces):
    level = lax.axis_index("level")
    per_tile = LANES // EDGE

    def place(z):
        return jnp.where(level == 0, z, depth - 1 - z)

    def sign_level(z, unused):
        pieces = [(ref[z], ref[depth + z // per_tile]) for ref in sign_pieces]
        signs[place(z) + 1] = join(z, *pieces) * mask
        return unused

    lax.fori_loop(0, depth, sign_level, 0, unroll=per_tile)
    core = lax.rem(lax.axis_index("probe"), 2)
    for start, pieces in zip((core, 1 - core), kappa_pieces):
        start = start * (depth // 2)

        def kappa_level(step, unused, start=start, pieces=pieces):
            z = start + step
            tiles = []
            for ref, base, whole_field in pieces:
                if whole_field:
                    tiles.append((ref[base + z], ref[base + depth + z // per_tile]))
                else:
                    tiles.append((ref[base + step], ref[base + depth // 2 + step // per_tile]))
            half_diag[place(z)] = 0.5 * join(z, *tiles) + (2.0 + VERTICAL)
            return unused

        lax.fori_loop(0, depth // 2, kappa_level, 0, unroll=per_tile)


OWN_ROWS = slice(ROWS, 2 * ROWS)


def near_kernel(
    depth,
    own_ref,
    even_ref,
    odd_ref,
    swapped_ref,
    half_diag,
    lower,
    forward,
    own_signs,
    k_signs,
    signs,
):
    field = own_ref.shape[0] // 2
    mask = inside_mask()
    zero = jnp.zeros(mask.shape, jnp.float32)
    signs[0] = zero
    signs[depth + 1] = zero
    kappa_pieces = (
        ((even_ref, field, False), (own_ref, field, True), (odd_ref, field, False)),
        ((swapped_ref, 0, False), (own_ref, field, True), (swapped_ref, field // 2, False)),
    )
    unpack(depth, signs, half_diag, mask, (even_ref, own_ref, odd_ref), kappa_pieces)

    def down(k, carry):
        ratio, value = carry
        ratio = mask / (half_diag[k] - ratio)
        here = signs[k + 1]
        value = ratio * (here + value)
        lower[k] = ratio
        forward[k] = value
        image = half_diag[k] * here - (signs[k] + signs[k + 2]) - 0.5 * beside(here)
        own_signs[k] = here[OWN_ROWS]
        k_signs[k] = image[OWN_ROWS]
        return ratio, value

    lax.fori_loop(0, depth, down, (zero, zero), unroll=GROUP)


def basis_kernel(
    depth,
    near_diag,
    near_lower,
    near_forward,
    near_signs,
    own_far_ref,
    even_far_ref,
    odd_far_ref,
    swapped_ref,
    swapped_far_ref,
    basis_ref,
    image_ref,
    far_signs,
    far_k_signs,
    gram_ref,
    signs,
    far_diag,
    far_lower,
    upper,
    basis,
    forward,
    sides,
    backward,
    sums,
):
    levels = 2 * depth
    mask = inside_mask()
    half_mask = 0.5 * mask
    zero = jnp.zeros(mask.shape, jnp.float32)
    own_zero = jnp.zeros((ROWS, LANES), jnp.float32)
    mine = lane_ids((ROWS, LANES)) < LANES // 2
    field = swapped_ref.shape[0] // 3 * 2
    signs[0] = zero
    signs[0, OWN_ROWS] = near_signs[depth - 1]
    signs[depth + 1] = zero
    backward[levels] = zero
    upper[levels] = zero
    basis[levels] = zero
    kappa_pieces = (
        tuple((ref, field, False) for ref in (even_far_ref, own_far_ref, odd_far_ref)),
        (
            (swapped_far_ref, 0, False),
            (swapped_ref, field, False),
            (swapped_far_ref, field // 2, False),
        ),
    )
    unpack(depth, signs, far_diag, mask, (even_far_ref, own_far_ref, odd_far_ref), kappa_pieces)

    def start_down(k, carry):
        ratio, value, from_end = carry
        ratio = mask / (far_diag[k] - ratio)
        here = signs[k + 1]
        value = ratio * (here + value)
        far_lower[k] = ratio
        forward[depth + k] = value
        other = depth - 1 - k
        from_end = mask / (far_diag[other] - from_end)
        upper[depth + other] = from_end
        image = far_diag[k] * here - (signs[k] + signs[k + 2]) - 0.5 * beside(here)
        far_signs[k] = here[OWN_ROWS]
        far_k_signs[k] = image[OWN_ROWS]
        return ratio, value, from_end

    start = (near_lower[depth - 1], near_forward[depth - 1], zero)
    carry = lax.fori_loop(0, depth, start_down, start, unroll=GROUP)

    def start_up_far(step, carry):
        k = depth - 1 - step
        solved, value = carry
        solved = forward[depth + k] + far_lower[k] * solved
        value = upper[depth + k] * (solved + value)
        backward[depth + k] = value
        return solved, value

    solved, value = lax.fori_loop(0, depth, start_up_far, (zero, zero), unroll=GROUP)

    def start_up_near(step, carry):
        k = depth - 1 - step
        ratio, solved, value = carry
        ratio = mask / (near_diag[k] - ratio)
        solved = near_forward[k] + near_lower[k] * solved
        value = ratio * (solved + value)
        upper[k] = ratio
        backward[k] = value
        return ratio, solved, value

    lax.fori_loop(0, depth, start_up_near, (carry[2], solved, value), unroll=GROUP)

    parts = (
        (0, near_diag, near_lower, lambda k: near_signs[k]),
        (depth, far_diag, far_lower, lambda k: signs[k + 1, OWN_ROWS]),
    )
    place = 0
    for index in range(ITERS):
        final = index + 1 == ITERS
        group_size = 2 * GROUP if final else GROUP

        def next_basis(k, previous, index=index):
            solved = backward[k] + upper[k] * previous
            if index == 0:
                value = solved
            elif SHIFTS[index - 1] == 0.0:
                value = -solved
            else:
                value = SHIFTS[index - 1] * basis[k] - solved
            return solved, value

        solved, here = next_basis(0, zero)
        if not final:
            basis[0] = here
        carry = (solved, zero, here, zero) + (own_zero,) * (2 * (index + 2))
        for offset, half_diag, lower, sign_of in parts:

            def down(group, carry):
                solved, above, here, value, *totals = carry
                products = []
                for step in range(group_size):
                    k = group * group_size + step
                    solved, below = next_basis(offset + k + 1, solved)
                    if not final:
                        basis[offset + k + 1] = below
                    side = beside(here)
                    image = half_diag[k] * here - (above + below) - half_mask * side
                    if not final:
                        value = lower[k] * (beside(image) + value)
                        forward[offset + k] = value
                        sides[offset + k] = side
                    my_basis, my_image = here[OWN_ROWS], image[OWN_ROWS]
                    basis_ref[index, offset + k] = my_basis
                    image_ref[index, offset + k] = my_image
                    factors = [(image_ref[other, offset + k], my_image) for other in range(index)]
                    factors += [(my_image, my_image), (my_basis, sign_of(k))]
                    products.append(
                        [a[:, :LANES] * b[:, :LANES] + a[:, LANES:] * b[:, LANES:] for a, b in factors]
                    )
                    above, here = here, below
                for slot in range(index + 2):
                    for four in range(0, group_size, 4):
                        added = (products[four][slot] + products[four + 1][slot]) + (
                            products[four + 2][slot] + products[four + 3][slot]
                        )
                        totals[2 * slot], rest = two_sum(totals[2 * slot], added)
                        totals[2 * slot + 1] = totals[2 * slot + 1] + rest
                return (solved, above, here, value, *totals)

            carry = lax.fori_loop(0, depth // group_size, down, carry)
        totals = [jnp.where(mine, total, 0.0) for total in carry[4:]]
        for slot in range(index + 1):
            sums[2 * (place + slot)] = totals[2 * slot]
            sums[2 * (place + slot) + 1] = totals[2 * slot + 1]
        place += index + 1
        sums[2 * (len(PAIRS) + index)] = totals[2 * index + 2]
        sums[2 * (len(PAIRS) + index) + 1] = totals[2 * index + 3]
        if final:
            break
        carry = (zero, zero)
        for offset, half_diag, lower, sign_of in reversed(parts):

            def up(step, carry):
                k = depth - 1 - step
                solved, value = carry
                solved = forward[offset + k] + lower[k] * solved
                value = upper[offset + k] * ((sides[offset + k] + solved) + value)
                backward[offset + k] = value
                return solved, value

            carry = lax.fori_loop(0, depth, up, carry, unroll=GROUP)

    ids = row_ids((ROWS, LANES))
    for block in range(SLOTS // ROWS):
        high, low = own_zero, own_zero
        for slot in range(block * ROWS, min((block + 1) * ROWS, COUNT)):
            pair = (sums[2 * slot], sums[2 * slot + 1])
            for shift in (4, 2, 1):
                pair = pair_add(pair, tuple(pltpu.roll(part, shift, 0) for part in pair))
            here = ids == slot - block * ROWS
            high, low = jnp.where(here, pair[0], high), jnp.where(here, pair[1], low)
        gram_ref[block * ROWS : (block + 1) * ROWS] = high
        gram_ref[SLOTS + block * ROWS : SLOTS + (block + 1) * ROWS] = low
    ones = jnp.ones((LANES, LANES), jnp.bfloat16)

    def lane_sum(part):
        return jnp.dot(part, ones, preferred_element_type=jnp.float32)

    high, middle, low = (lane_sum(part) for part in split_three(gram_ref[:SLOTS]))
    high, rest = two_sum(high, middle)
    gram_ref[:SLOTS] = high
    gram_ref[SLOTS:] = rest + (low + lane_sum(gram_ref[SLOTS:].astype(jnp.bfloat16)))


def terms_kernel(
    depth, basis_ref, image_ref, near_signs, near_k_signs, far_signs, far_k_signs, terms_ref
):
    level = lax.axis_index("level")
    half = LANES // 2
    mine = lane_ids((ROWS, LANES)) < half
    for offset, signs, k_signs in ((0, near_signs, near_k_signs), (depth, far_signs, far_k_signs)):

        def step(k, unused, offset=offset, signs=signs, k_signs=k_signs):
            z = offset + k
            target = jnp.where(level == 0, z, 2 * depth - 1 - z)
            sign, image = signs[k], k_signs[k]
            for index in range(ITERS):
                term = basis_ref[index, z] * image + image_ref[index, z] * sign
                terms_ref[index, target] = jnp.where(
                    mine, term[:, :LANES], pltpu.roll(term[:, LANES:], half, 1)
                )
            return unused

        if offset == 0:
            lax.fori_loop(0, depth - 1, step, 0, unroll=GROUP)
            sign, image = signs[depth - 1], k_signs[depth - 1] - far_signs[0]
            target = jnp.where(level == 0, depth - 1, depth)
            for index in range(ITERS):
                term = basis_ref[index, depth - 1] * image + image_ref[index, depth - 1] * sign
                terms_ref[index, target] = jnp.where(
                    mine, term[:, :LANES], pltpu.roll(term[:, LANES:], half, 1)
                )
        else:
            lax.fori_loop(0, depth, step, 0, unroll=GROUP)


def solve_small(high, low):
    def entry(index):
        return tuple(jnp.broadcast_to(part[index : index + 1], (ROWS, LANES)) for part in (high, low))

    gram = {}
    for place, (i, j) in enumerate(PAIRS):
        gram[i, j] = gram[j, i] = entry(place)
    right = [entry(len(PAIRS) + j) for j in range(ITERS)]
    work = {key: pair[0] for key, pair in gram.items()}
    ratios, inverses = {}, []
    for i in range(ITERS):
        pivot = work[i, i]
        good = pivot > 1e-7 * gram[i, i][0]
        inverses.append(jnp.where(good, 1.0 / jnp.where(good, pivot, 1.0), 0.0))
        for r in range(i + 1, ITERS):
            ratios[r, i] = work[r, i] * inverses[i]
        for r in range(i + 1, ITERS):
            for c in range(i + 1, r + 1):
                work[r, c] = work[c, r] = work[r, c] - ratios[r, i] * work[c, i]

    def solve(values):
        values = list(values)
        for i in range(ITERS):
            for r in range(i + 1, ITERS):
                values[r] = values[r] - ratios[r, i] * values[i]
        values = [value * inverse for value, inverse in zip(values, inverses)]
        for i in reversed(range(ITERS)):
            for r in range(i):
                values[r] = values[r] - ratios[i, r] * values[i]
        return values

    found = solve([pair[0] for pair in right])
    for unused in range(2):
        rest = []
        for i in range(ITERS):
            total = right[i]
            for j in range(ITERS):
                product, error = two_product(gram[i, j][0], found[j])
                total = pair_add(total, (-product, -(error + gram[i, j][1] * found[j])))
            rest.append(total[0] + total[1])
        found = [a + b for a, b in zip(found, solve(rest))]
    return found


def combine_kernel(depth, terms_ref, *refs):
    gram_refs, (keep_ref, send_ref) = refs[:-2], refs[-2:]
    pairs = []
    for ref in gram_refs:
        for start in range(0, ref.shape[0], 2 * SLOTS):
            pairs.append((ref[start : start + SLOTS], ref[start + SLOTS : start + 2 * SLOTS]))
    while len(pairs) > 1:
        merged = [pair_add(pairs[i], pairs[i + 1]) for i in range(0, len(pairs) - 1, 2)]
        pairs = merged + pairs[2 * len(merged) :]
    found = solve_small(*pairs[0])
    core = lax.rem(lax.axis_index("probe"), 2)
    width = LANES // 4
    first_lanes = lane_ids((ROWS, LANES)) % (2 * width) < width
    pairs_deep = depth // 2

    def step(z, unused):
        for half in range(2):
            def total(k):
                value = found[0] * terms_ref[0, k]
                for j in range(1, ITERS):
                    value = value + found[j] * terms_ref[j, k]
                return value

            one = total(half * depth + z)
            two = total(half * depth + pairs_deep + z)
            low = jnp.where(first_lanes, one, pltpu.roll(two, width, 1))
            high = jnp.where(first_lanes, pltpu.roll(one, LANES - width, 1), two)
            keep_ref[half, z] = jnp.where(core == 0, low, high)
            send_ref[half, z] = jnp.where(core == 0, high, low)
        return unused

    lax.fori_loop(0, pairs_deep, step, 0, unroll=2)


def observed_kernel(
    depth, probes, kappa_ref, observed_ref, even_ref, odd_ref, far_ref, factor_ref, data_ref
):
    level = lax.axis_index("level")
    tile = lax.axis_index("tile")
    last_tile = lax.axis_size("tile") - 1
    probe = lax.axis_index("probe")
    in_low = probe < probes // 2
    even = lax.rem(probe, 2) == 0
    width = LANES // 2
    lanes = lane_ids((ROWS, 2 * LANES))
    ids = row_ids((ROWS, LANES))
    base = even_ref.shape[0] - depth // ROWS
    from_even = lax.rem(tile, 2) == 1

    def half(value):
        return jnp.where(in_low, value[..., :LANES], value[..., LANES:])

    def take(value):
        return jnp.where(even, value, pltpu.roll(value, width, 1))[:, :width]

    far_edge = far_ref[far_ref.shape[0] - 1]
    for z in range(depth):
        value = observed_ref[z]
        mine = half(value)
        y_sides = jnp.where(lanes > 0, pltpu.roll(value, 1, 1), 0.0) + jnp.where(
            lanes < 2 * LANES - 1, pltpu.roll(value, 2 * LANES - 1, 1), 0.0
        )
        first = even_ref[base + z // ROWS, z % ROWS : z % ROWS + 1, :]
        second = odd_ref[base + z // ROWS, z % ROWS : z % ROWS + 1, :]
        left, right = jnp.where(from_even, first, second), jnp.where(from_even, second, first)
        before = jnp.where(ids > 0, pltpu.roll(mine, 1, 0), jnp.where(tile > 0, left, 0.0))
        after = jnp.where(
            ids < ROWS - 1, pltpu.roll(mine, ROWS - 1, 0), jnp.where(tile < last_tile, right, 0.0)
        )
        above = half(observed_ref[z - 1]) if z > 0 else jnp.where(level > 0, far_edge, 0.0)
        below = half(observed_ref[z + 1]) if z < depth - 1 else jnp.where(level == 0, far_edge, 0.0)
        kappa = half(kappa_ref[z])
        k_observed = (
            (kappa + (4.0 + 2.0 * VERTICAL)) * mine
            - (before + after)
            - half(y_sides)
            - VERTICAL * (above + below)
        )
        factor_ref[z] = take(kappa * (0.5 / probes))
        data_ref[z] = take(kappa * (2.0 * mine * k_observed))


def gradient_kernel(depth, trace_a_ref, trace_b_ref, factor_ref, data_ref, out_ref):
    width = LANES // 2
    square = (LANES, LANES)
    lane = lane_ids(square)
    source = (width // 2) * (lane // width) + (lane % width) // 2 + width * (lane % 2)
    chosen = jnp.where(row_ids(square) == source, 1.0, 0.0).astype(jnp.bfloat16)
    traces = pick((trace_a_ref[...] + trace_b_ref[...]).reshape(-1, LANES), chosen)
    traces = traces.reshape(depth // 2, ROWS, LANES)
    for z in range(depth // 2):
        out_ref[z] = factor_ref[z] * traces[z, :, :width] - data_ref[z]
        later = depth // 2 + z
        second = pltpu.roll(traces[z], width, 1)[:, :width]
        out_ref[later] = factor_ref[later] * second - data_ref[later]


def whole(count):
    return [pl.BlockSpec(memory_space=pltpu.VMEM)] * count


def body(probe_bits, kappa_sq, observed):
    probes, tile_count = lax.axis_size("probe"), lax.axis_size("tile")
    unused, depth, rows, columns = probe_bits.shape
    assert probe_bits.shape[0] == 1 and lax.axis_size("level") == 2 and probes == 4
    assert rows == ROWS and columns == 2 * LANES and depth % (2 * LANES // EDGE) == 0
    params = pltpu.CompilerParams(vmem_limit_bytes=48 * 1024 * 1024)
    f32 = jnp.float32
    tiles = depth * EDGE // LANES
    field = depth + tiles
    sent = field + field // 2
    own_shape = jax.ShapeDtypeStruct((2 * field, ROWS, LANES), f32)
    near_shape = jax.ShapeDtypeStruct((sent + depth // ROWS, ROWS, LANES), f32)
    far_shape = jax.ShapeDtypeStruct((sent + 1, ROWS, LANES), f32)

    own_block, even_block, odd_block, cross_block = pl.pallas_call(
        functools.partial(pack_kernel, depth),
        out_shape=(own_shape, near_shape, near_shape, far_shape),
        in_specs=[pl.BlockSpec(memory_space=pltpu.HBM)] * 3,
        out_specs=tuple(whole(4)),
        scratch_shapes=[
            pltpu.VMEM((depth, rows, columns), jnp.int32),
            pltpu.VMEM((depth, rows, columns), f32),
            pltpu.VMEM((depth, rows, columns), f32),
            pltpu.SemaphoreType.DMA((3,)),
        ],
        compiler_params=params,
        name="pack",
    )(
        *(
            pltpu.with_memory_space_constraint(value, pltpu.HBM)
            for value in (probe_bits[0], kappa_sq, observed)
        )
    )

    def swaps(pairs):
        return [way for a, b in pairs for way in ((a, b), (b, a))]

    even_pairs = [(i, i + 1) for i in range(0, tile_count - 1, 2)]
    odd_pairs = [(i, i + 1) for i in range(1, tile_count - 1, 2)]
    own_far = lax.ppermute(cross_block, "level", swaps([(0, 1)]))
    even = lax.ppermute(even_block, "tile", swaps(even_pairs))
    odd = lax.ppermute(odd_block, "tile", swaps(odd_pairs))
    odd_far = lax.ppermute(own_far, "tile", swaps(odd_pairs))
    even_far = lax.ppermute(
        cross_block,
        ("tile", "level"),
        swaps([(2 * a + level, 2 * b + 1 - level) for a, b in even_pairs for level in range(2)]),
    )

    quarter = jax.ShapeDtypeStruct((depth, ROWS, columns // probes), f32)
    factor, data = pl.pallas_call(
        functools.partial(observed_kernel, depth, probes),
        out_shape=(quarter, quarter),
        in_specs=whole(5),
        out_specs=tuple(whole(2)),
        compiler_params=params,
        name="observed",
    )(kappa_sq, observed, even, odd, own_far)

    def core_swap(*pieces):
        kappa = jnp.concatenate([piece[field:sent] for piece in pieces], axis=0)
        return lax.ppermute(kappa, "probe", swaps([(0, 1), (2, 3)]))

    swapped = core_swap(even, odd, own_far)
    levels = 2 * depth
    part = jax.ShapeDtypeStruct((depth, 3 * ROWS, 2 * LANES), f32)
    own_part = jax.ShapeDtypeStruct((depth, ROWS, 2 * LANES), f32)
    near_diag, near_lower, near_forward, near_signs, near_k_signs = pl.pallas_call(
        functools.partial(near_kernel, depth),
        out_shape=(part, part, part, own_part, own_part),
        in_specs=whole(4),
        out_specs=tuple(whole(5)),
        scratch_shapes=[pltpu.VMEM((depth + 2, 3 * ROWS, 2 * LANES), f32)],
        compiler_params=params,
        name="near",
    )(own_block, even, odd, swapped)

    swapped_far = core_swap(even_far, odd_far)
    padded = pltpu.VMEM((levels + 1, 3 * ROWS, 2 * LANES), f32)
    plain = pltpu.VMEM((levels, 3 * ROWS, 2 * LANES), f32)
    short = pltpu.VMEM((depth, 3 * ROWS, 2 * LANES), f32)
    fields = jax.ShapeDtypeStruct((ITERS, levels, ROWS, 2 * LANES), f32)
    basis, images, far_signs, far_k_signs, gram = pl.pallas_call(
        functools.partial(basis_kernel, depth),
        out_shape=(
            fields,
            fields,
            own_part,
            own_part,
            jax.ShapeDtypeStruct((2 * SLOTS, LANES), f32),
        ),
        in_specs=whole(9),
        out_specs=tuple(whole(5)),
        scratch_shapes=[
            pltpu.VMEM((depth + 2, 3 * ROWS, 2 * LANES), f32),
            short,
            short,
            padded,
            padded,
            plain,
            plain,
            padded,
            pltpu.VMEM((2 * SLOTS, ROWS, LANES), f32),
        ],
        compiler_params=params,
        name="basis",
    )(
        near_diag,
        near_lower,
        near_forward,
        near_signs,
        own_far,
        even_far,
        odd_far,
        swapped,
        swapped_far,
    )
    terms = pl.pallas_call(
        functools.partial(terms_kernel, depth),
        out_shape=jax.ShapeDtypeStruct((ITERS, levels, ROWS, LANES), f32),
        in_specs=whole(6),
        out_specs=pl.BlockSpec(memory_space=pltpu.VMEM),
        compiler_params=params,
        name="terms",
    )(basis, images, near_signs, near_k_signs, far_signs, far_k_signs)

    both = jnp.concatenate([gram, lax.ppermute(gram, "level", [(0, 1), (1, 0)])], axis=0)
    if tile_count in (2, 4):
        partials = [both] + [
            lax.ppermute(both, "tile", [(i, i ^ k) for i in range(tile_count)])
            for k in range(1, tile_count)
        ]
    else:
        partials = [lax.all_gather(both, "tile", axis=0, tiled=True)]
    piece = jax.ShapeDtypeStruct((2, depth // 2, ROWS, LANES), f32)
    keep, send = pl.pallas_call(
        functools.partial(combine_kernel, depth),
        out_shape=(piece, piece),
        in_specs=whole(1 + len(partials)),
        out_specs=tuple(whole(2)),
        compiler_params=params,
        name="combine",
    )(terms, *partials)

    summed = keep + lax.ppermute(send, "probe", [(0, 1), (1, 0), (2, 3), (3, 2)])
    half = lax.axis_index("probe") // 2
    straight = lax.dynamic_index_in_dim(summed, half, 0, keepdims=False)
    turned = lax.dynamic_index_in_dim(summed, 1 - half, 0, keepdims=False)

    def routes(flip):
        pairs = []
        for x in range(2):
            for core in range(2):
                for level in range(2):
                    target = x if not flip else 1 - x
                    pairs.append(((2 * x + core) * 2 + level, (2 * level + core) * 2 + target))
        return pairs

    trace_a = lax.ppermute(straight, ("probe", "level"), routes(False))
    trace_b = lax.ppermute(turned, ("probe", "level"), routes(True))
    return pl.pallas_call(
        functools.partial(gradient_kernel, depth),
        out_shape=quarter,
        in_specs=whole(4),
        out_specs=pl.BlockSpec(memory_space=pltpu.VMEM),
        compiler_params=params,
        name="gradient",
    )(trace_a, trace_b, factor, data)


def solution(mesh):
    in_specs = (
        P("probe", "level", "tile", None),
        P("level", "tile", None),
        P("level", "tile", None),
    )
    out_specs = P("level", "tile", "probe")
    return jax.shard_map(body, mesh=mesh, in_specs=in_specs, out_specs=out_specs, check_vma=False)
```

```python
import functools

import jax
import jax.numpy as jnp
from jax import lax
from jax.experimental import pallas as pl
from jax.experimental.pallas import tpu as pltpu
from jax.sharding import PartitionSpec as P

ITERS = 4
VERTICAL = 2.0
LANES = 128
ROWS = 8
EDGE = 8
GROUP = 8
SHIFTS = (1.0, 0.0, -2.0)
PAIRS = [(i, j) for j in range(ITERS) for i in range(j + 1)]
COUNT = len(PAIRS) + ITERS
SLOTS = 16


def two_sum(a, b):
    total = a + b
    part = total - a
    return total, (a - (total - part)) + (b - part)


def two_product(a, b):
    def split(v):
        big = v * 4097.0
        high = big - (big - v)
        return high, v - high

    product = a * b
    a_high, a_low = split(a)
    b_high, b_low = split(b)
    return product, ((a_high * b_high - product) + a_high * b_low + a_low * b_high) + a_low * b_low


def pair_add(first, second):
    total, rest = two_sum(first[0], second[0])
    rest = rest + (first[1] + second[1])
    high = total + rest
    return high, rest - (high - total)


def lane_ids(shape):
    return lax.broadcasted_iota(jnp.int32, shape, len(shape) - 1)


def row_ids(shape):
    return lax.broadcasted_iota(jnp.int32, shape, len(shape) - 2)


def split_three(values):
    high = values.astype(jnp.bfloat16)
    rest = values - high.astype(jnp.float32)
    middle = rest.astype(jnp.bfloat16)
    low = (rest - middle.astype(jnp.float32)).astype(jnp.bfloat16)
    return high, middle, low


def pick(values, chosen):
    high, middle, low = (
        jnp.dot(part, chosen, preferred_element_type=jnp.float32) for part in split_three(values)
    )
    return high + (middle + low)


def columns_of(half):
    shape = (2 * LANES, 2 * LANES)
    ids, lane = row_ids(shape), lane_ids(shape)
    odd = (lane // (LANES // 2)) % 2
    main = LANES * half + 2 * (lane % (LANES // 2)) + odd
    edge = LANES - EDGE * half + 2 * (lane % (EDGE // 2)) + odd
    wanted = jnp.where(lane < LANES, main, edge)
    return jnp.where(ids == wanted, 1.0, 0.0).astype(jnp.bfloat16)


def pack_kernel(
    depth,
    bits_hbm,
    kappa_hbm,
    observed_hbm,
    own_ref,
    even_ref,
    odd_ref,
    cross_ref,
    bits_ref,
    kappa_ref,
    observed_ref,
    arrived,
):
    copies = [
        pltpu.make_async_copy(source, target, arrived.at[place])
        for place, (source, target) in enumerate(
            ((bits_hbm, bits_ref), (kappa_hbm, kappa_ref), (observed_hbm, observed_ref))
        )
    ]
    for copy in copies:
        copy.start()
    level = lax.axis_index("level")
    first = level == 0
    in_first_core = lax.rem(lax.axis_index("probe"), 2) == 0
    per_tile = LANES // EDGE
    tiles = depth // per_tile
    field = depth + tiles
    slot_ids = (lane_ids((ROWS, LANES)) % (LANES // 2)) // (EDGE // 2)
    same_columns, cross_columns = columns_of(level), columns_of(1 - level)

    def blocks(picked):
        picked = picked.reshape(depth, ROWS, 2 * LANES)
        edges = []
        for tile in range(tiles):
            packed = picked[tile * per_tile, :, LANES:]
            for slot in range(1, per_tile):
                packed = jnp.where(slot_ids == slot, picked[tile * per_tile + slot, :, LANES:], packed)
            edges.append(packed)
        return [picked[z, :, :LANES] for z in range(depth)], edges

    def write(refs, base, values):
        for place, value in enumerate(values):
            for ref in refs:
                ref[base + place] = value

    copies[0].wait()
    signs = (2 * bits_ref[...] - 1).astype(jnp.float32).reshape(depth * ROWS, 2 * LANES)
    signs = signs.astype(jnp.bfloat16)
    for refs, chosen in (((own_ref, even_ref, odd_ref), same_columns), ((cross_ref,), cross_columns)):
        main, edges = blocks(jnp.dot(signs, chosen, preferred_element_type=jnp.float32))
        write(refs, 0, main + edges)
    copies[1].wait()
    kappa = kappa_ref[...].reshape(depth * ROWS, 2 * LANES)
    for refs, chosen in (((even_ref, odd_ref), same_columns), ((cross_ref,), cross_columns)):
        main, edges = blocks(pick(kappa, chosen))
        if len(refs) == 2:
            write((own_ref,), field, main + edges)
        low = main[: depth // 2] + edges[: tiles // 2]
        high = main[depth // 2 :] + edges[tiles // 2 :]
        write(refs, field, [jnp.where(in_first_core, a, b) for a, b in zip(low, high)])
    copies[2].wait()
    base = field + field // 2
    in_low = lax.axis_index("probe") < lax.axis_size("probe") // 2

    def half(value):
        return jnp.where(in_low, value[..., :LANES], value[..., LANES:])

    top = half(observed_ref[:, ROWS - 1, :])
    bottom = half(observed_ref[:, 0, :])
    goes_up = lax.rem(lax.axis_index("tile"), 2) == 0
    for tile in range(depth // ROWS):
        here = slice(tile * ROWS, (tile + 1) * ROWS)
        even_ref[base + tile] = jnp.where(goes_up, top[here], bottom[here])
        odd_ref[base + tile] = jnp.where(goes_up, bottom[here], top[here])
    cross_ref[base] = jnp.where(first, half(observed_ref[depth - 1]), half(observed_ref[0]))


def beside(values):
    rows = values.shape[0]
    even, odd = values[:, :LANES], values[:, LANES:]
    y_sides = jnp.concatenate(
        [odd + pltpu.roll(odd, 1, 1), even + pltpu.roll(even, LANES - 1, 1)], axis=1
    )
    return (pltpu.roll(values, 1, 0) + pltpu.roll(values, rows - 1, 0)) + y_sides


def inside_mask():
    shape = (3 * ROWS, 2 * LANES)
    tile = lax.axis_index("tile")
    half = LANES // 2
    lanes, ids = lane_ids(shape) % LANES, row_ids(shape)
    near = jnp.where(lax.axis_index("level") == 0, half, LANES - EDGE // 2)
    inside = (lanes < half) | ((lanes >= near) & (lanes < near + EDGE // 2))
    inside = inside & (ids >= jnp.where(tile > 0, 0, ROWS))
    inside = inside & (ids < jnp.where(tile < lax.axis_size("tile") - 1, 3 * ROWS, 2 * ROWS))
    return jnp.where(inside, 1.0, 0.0)


def join(z, even, own, odd):
    half, short = LANES // 2, EDGE // 2
    level = lax.axis_index("level")
    from_even = lax.rem(lax.axis_index("tile"), 2) == 1
    mine = lane_ids((ROWS, LANES)) < half
    shift = half + (half - short) * level - short * lax.rem(z, LANES // EDGE)
    shift = lax.rem(shift + LANES, LANES)
    left = [jnp.where(from_even, a, b) for a, b in zip(even, odd)]
    right = [jnp.where(from_even, b, a) for a, b in zip(even, odd)]
    evens, odds = [], []
    for main, edge in (left, own, right):
        edge = pltpu.roll(edge, shift, 1)
        evens.append(jnp.where(mine, main, edge))
        odds.append(pltpu.roll(jnp.where(mine, edge, main), half, 1))
    return jnp.concatenate([jnp.concatenate(evens, axis=0), jnp.concatenate(odds, axis=0)], axis=1)


def unpack(depth, signs, half_diag, mask, sign_pieces, kappa_pieces):
    level = lax.axis_index("level")
    per_tile = LANES // EDGE

    def place(z):
        return jnp.where(level == 0, z, depth - 1 - z)

    def sign_level(z, unused):
        pieces = [(ref[z], ref[depth + z // per_tile]) for ref in sign_pieces]
        signs[place(z) + 1] = join(z, *pieces) * mask
        return unused

    lax.fori_loop(0, depth, sign_level, 0, unroll=per_tile)
    core = lax.rem(lax.axis_index("probe"), 2)
    for start, pieces in zip((core, 1 - core), kappa_pieces):
        start = start * (depth // 2)

        def kappa_level(step, unused, start=start, pieces=pieces):
            z = start + step
            tiles = []
            for ref, base, whole_field in pieces:
                if whole_field:
                    tiles.append((ref[base + z], ref[base + depth + z // per_tile]))
                else:
                    tiles.append((ref[base + step], ref[base + depth // 2 + step // per_tile]))
            half_diag[place(z)] = 0.5 * join(z, *tiles) + (2.0 + VERTICAL)
            return unused

        lax.fori_loop(0, depth // 2, kappa_level, 0, unroll=per_tile)


OWN_ROWS = slice(ROWS, 2 * ROWS)


def near_kernel(
    depth,
    own_ref,
    even_ref,
    odd_ref,
    swapped_ref,
    half_diag,
    lower,
    forward,
    own_signs,
    k_signs,
    signs,
):
    field = own_ref.shape[0] // 2
    mask = inside_mask()
    zero = jnp.zeros(mask.shape, jnp.float32)
    signs[0] = zero
    signs[depth + 1] = zero
    kappa_pieces = (
        ((even_ref, field, False), (own_ref, field, True), (odd_ref, field, False)),
        ((swapped_ref, 0, False), (own_ref, field, True), (swapped_ref, field // 2, False)),
    )
    unpack(depth, signs, half_diag, mask, (even_ref, own_ref, odd_ref), kappa_pieces)

    def down(k, carry):
        ratio, value = carry
        ratio = mask / (half_diag[k] - ratio)
        here = signs[k + 1]
        value = ratio * (here + value)
        lower[k] = ratio
        forward[k] = value
        image = half_diag[k] * here - (signs[k] + signs[k + 2]) - 0.5 * beside(here)
        own_signs[k] = here[OWN_ROWS]
        k_signs[k] = image[OWN_ROWS]
        return ratio, value

    lax.fori_loop(0, depth, down, (zero, zero), unroll=GROUP)


def basis_kernel(
    depth,
    near_diag,
    near_lower,
    near_forward,
    near_signs,
    own_far_ref,
    even_far_ref,
    odd_far_ref,
    swapped_ref,
    swapped_far_ref,
    basis_ref,
    image_ref,
    far_signs,
    far_k_signs,
    gram_ref,
    signs,
    far_diag,
    far_lower,
    upper,
    basis,
    forward,
    sides,
    backward,
    sums,
):
    levels = 2 * depth
    mask = inside_mask()
    half_mask = 0.5 * mask
    zero = jnp.zeros(mask.shape, jnp.float32)
    own_zero = jnp.zeros((ROWS, LANES), jnp.float32)
    mine = lane_ids((ROWS, LANES)) < LANES // 2
    field = swapped_ref.shape[0] // 3 * 2
    signs[0] = zero
    signs[0, OWN_ROWS] = near_signs[depth - 1]
    signs[depth + 1] = zero
    backward[levels] = zero
    upper[levels] = zero
    basis[levels] = zero
    kappa_pieces = (
        tuple((ref, field, False) for ref in (even_far_ref, own_far_ref, odd_far_ref)),
        (
            (swapped_far_ref, 0, False),
            (swapped_ref, field, False),
            (swapped_far_ref, field // 2, False),
        ),
    )
    unpack(depth, signs, far_diag, mask, (even_far_ref, own_far_ref, odd_far_ref), kappa_pieces)

    def start_down(k, carry):
        ratio, value, from_end = carry
        ratio = mask / (far_diag[k] - ratio)
        here = signs[k + 1]
        value = ratio * (here + value)
        far_lower[k] = ratio
        forward[depth + k] = value
        other = depth - 1 - k
        from_end = mask / (far_diag[other] - from_end)
        upper[depth + other] = from_end
        image = far_diag[k] * here - (signs[k] + signs[k + 2]) - 0.5 * beside(here)
        far_signs[k] = here[OWN_ROWS]
        far_k_signs[k] = image[OWN_ROWS]
        return ratio, value, from_end

    start = (near_lower[depth - 1], near_forward[depth - 1], zero)
    carry = lax.fori_loop(0, depth, start_down, start, unroll=GROUP)

    def start_up_far(step, carry):
        k = depth - 1 - step
        solved, value = carry
        solved = forward[depth + k] + far_lower[k] * solved
        value = upper[depth + k] * (solved + value)
        backward[depth + k] = value
        return solved, value

    solved, value = lax.fori_loop(0, depth, start_up_far, (zero, zero), unroll=GROUP)

    def start_up_near(step, carry):
        k = depth - 1 - step
        ratio, solved, value = carry
        ratio = mask / (near_diag[k] - ratio)
        solved = near_forward[k] + near_lower[k] * solved
        value = ratio * (solved + value)
        upper[k] = ratio
        backward[k] = value
        return ratio, solved, value

    lax.fori_loop(0, depth, start_up_near, (carry[2], solved, value), unroll=GROUP)

    parts = (
        (0, near_diag, near_lower, lambda k: near_signs[k]),
        (depth, far_diag, far_lower, lambda k: signs[k + 1, OWN_ROWS]),
    )
    place = 0
    for index in range(ITERS):
        final = index + 1 == ITERS
        group_size = 2 * GROUP if final else GROUP

        def next_basis(k, previous, index=index):
            solved = backward[k] + upper[k] * previous
            if index == 0:
                value = solved
            elif SHIFTS[index - 1] == 0.0:
                value = -solved
            else:
                value = SHIFTS[index - 1] * basis[k] - solved
            return solved, value

        solved, here = next_basis(0, zero)
        if not final:
            basis[0] = here
        carry = (solved, zero, here, zero) + (own_zero,) * (2 * (index + 2))
        for offset, half_diag, lower, sign_of in parts:

            def down(group, carry):
                solved, above, here, value, *totals = carry
                products = []
                for step in range(group_size):
                    k = group * group_size + step
                    solved, below = next_basis(offset + k + 1, solved)
                    if not final:
                        basis[offset + k + 1] = below
                    side = beside(here)
                    image = half_diag[k] * here - (above + below) - half_mask * side
                    if not final:
                        value = lower[k] * (beside(image) + value)
                        forward[offset + k] = value
                        sides[offset + k] = side
                    my_basis, my_image = here[OWN_ROWS], image[OWN_ROWS]
                    basis_ref[index, offset + k] = my_basis
                    image_ref[index, offset + k] = my_image
                    factors = [(image_ref[other, offset + k], my_image) for other in range(index)]
                    factors += [(my_image, my_image), (my_basis, sign_of(k))]
                    products.append(
                        [a[:, :LANES] * b[:, :LANES] + a[:, LANES:] * b[:, LANES:] for a, b in factors]
                    )
                    above, here = here, below
                for slot in range(index + 2):
                    for four in range(0, group_size, 4):
                        added = (products[four][slot] + products[four + 1][slot]) + (
                            products[four + 2][slot] + products[four + 3][slot]
                        )
                        totals[2 * slot], rest = two_sum(totals[2 * slot], added)
                        totals[2 * slot + 1] = totals[2 * slot + 1] + rest
                return (solved, above, here, value, *totals)

            carry = lax.fori_loop(0, depth // group_size, down, carry)
        totals = [jnp.where(mine, total, 0.0) for total in carry[4:]]
        for slot in range(index + 1):
            sums[2 * (place + slot)] = totals[2 * slot]
            sums[2 * (place + slot) + 1] = totals[2 * slot + 1]
        place += index + 1
        sums[2 * (len(PAIRS) + index)] = totals[2 * index + 2]
        sums[2 * (len(PAIRS) + index) + 1] = totals[2 * index + 3]
        if final:
            break
        carry = (zero, zero)
        for offset, half_diag, lower, sign_of in reversed(parts):

            def up(step, carry):
                k = depth - 1 - step
                solved, value = carry
                solved = forward[offset + k] + lower[k] * solved
                value = upper[offset + k] * ((sides[offset + k] + solved) + value)
                backward[offset + k] = value
                return solved, value

            carry = lax.fori_loop(0, depth, up, carry, unroll=GROUP)

    ids = row_ids((ROWS, LANES))
    for block in range(SLOTS // ROWS):
        high, low = own_zero, own_zero
        for slot in range(block * ROWS, min((block + 1) * ROWS, COUNT)):
            pair = (sums[2 * slot], sums[2 * slot + 1])
            for shift in (4, 2, 1):
                pair = pair_add(pair, tuple(pltpu.roll(part, shift, 0) for part in pair))
            here = ids == slot - block * ROWS
            high, low = jnp.where(here, pair[0], high), jnp.where(here, pair[1], low)
        gram_ref[block * ROWS : (block + 1) * ROWS] = high
        gram_ref[SLOTS + block * ROWS : SLOTS + (block + 1) * ROWS] = low
    ones = jnp.ones((LANES, LANES), jnp.bfloat16)

    def lane_sum(part):
        return jnp.dot(part, ones, preferred_element_type=jnp.float32)

    high, middle, low = (lane_sum(part) for part in split_three(gram_ref[:SLOTS]))
    high, rest = two_sum(high, middle)
    gram_ref[:SLOTS] = high
    gram_ref[SLOTS:] = rest + (low + lane_sum(gram_ref[SLOTS:].astype(jnp.bfloat16)))


def terms_kernel(
    depth, basis_ref, image_ref, near_signs, near_k_signs, far_signs, far_k_signs, terms_ref
):
    level = lax.axis_index("level")
    half = LANES // 2
    mine = lane_ids((ROWS, LANES)) < half
    for offset, signs, k_signs in ((0, near_signs, near_k_signs), (depth, far_signs, far_k_signs)):

        def step(k, unused, offset=offset, signs=signs, k_signs=k_signs):
            z = offset + k
            target = jnp.where(level == 0, z, 2 * depth - 1 - z)
            sign, image = signs[k], k_signs[k]
            for index in range(ITERS):
                term = basis_ref[index, z] * image + image_ref[index, z] * sign
                terms_ref[index, target] = jnp.where(
                    mine, term[:, :LANES], pltpu.roll(term[:, LANES:], half, 1)
                )
            return unused

        if offset == 0:
            lax.fori_loop(0, depth - 1, step, 0, unroll=GROUP)
            sign, image = signs[depth - 1], k_signs[depth - 1] - far_signs[0]
            target = jnp.where(level == 0, depth - 1, depth)
            for index in range(ITERS):
                term = basis_ref[index, depth - 1] * image + image_ref[index, depth - 1] * sign
                terms_ref[index, target] = jnp.where(
                    mine, term[:, :LANES], pltpu.roll(term[:, LANES:], half, 1)
                )
        else:
            lax.fori_loop(0, depth, step, 0, unroll=GROUP)


def solve_small(high, low):
    def entry(index):
        return tuple(jnp.broadcast_to(part[index : index + 1], (ROWS, LANES)) for part in (high, low))

    gram = {}
    for place, (i, j) in enumerate(PAIRS):
        gram[i, j] = gram[j, i] = entry(place)
    right = [entry(len(PAIRS) + j) for j in range(ITERS)]
    work = {key: pair[0] for key, pair in gram.items()}
    ratios, inverses = {}, []
    for i in range(ITERS):
        pivot = work[i, i]
        good = pivot > 1e-7 * gram[i, i][0]
        inverses.append(jnp.where(good, 1.0 / jnp.where(good, pivot, 1.0), 0.0))
        for r in range(i + 1, ITERS):
            ratios[r, i] = work[r, i] * inverses[i]
        for r in range(i + 1, ITERS):
            for c in range(i + 1, r + 1):
                work[r, c] = work[c, r] = work[r, c] - ratios[r, i] * work[c, i]

    def solve(values):
        values = list(values)
        for i in range(ITERS):
            for r in range(i + 1, ITERS):
                values[r] = values[r] - ratios[r, i] * values[i]
        values = [value * inverse for value, inverse in zip(values, inverses)]
        for i in reversed(range(ITERS)):
            for r in range(i):
                values[r] = values[r] - ratios[i, r] * values[i]
        return values

    found = solve([pair[0] for pair in right])
    for unused in range(2):
        rest = []
        for i in range(ITERS):
            total = right[i]
            for j in range(ITERS):
                product, error = two_product(gram[i, j][0], found[j])
                total = pair_add(total, (-product, -(error + gram[i, j][1] * found[j])))
            rest.append(total[0] + total[1])
        found = [a + b for a, b in zip(found, solve(rest))]
    return found


def combine_kernel(depth, terms_ref, *refs):
    gram_refs, (keep_ref, send_ref) = refs[:-2], refs[-2:]
    pairs = []
    for ref in gram_refs:
        for start in range(0, ref.shape[0], 2 * SLOTS):
            pairs.append((ref[start : start + SLOTS], ref[start + SLOTS : start + 2 * SLOTS]))
    while len(pairs) > 1:
        merged = [pair_add(pairs[i], pairs[i + 1]) for i in range(0, len(pairs) - 1, 2)]
        pairs = merged + pairs[2 * len(merged) :]
    found = solve_small(*pairs[0])
    core = lax.rem(lax.axis_index("probe"), 2)
    width = LANES // 4
    first_lanes = lane_ids((ROWS, LANES)) % (2 * width) < width
    pairs_deep = depth // 2

    def step(z, unused):
        for half in range(2):
            def total(k):
                value = found[0] * terms_ref[0, k]
                for j in range(1, ITERS):
                    value = value + found[j] * terms_ref[j, k]
                return value

            one = total(half * depth + z)
            two = total(half * depth + pairs_deep + z)
            low = jnp.where(first_lanes, one, pltpu.roll(two, width, 1))
            high = jnp.where(first_lanes, pltpu.roll(one, LANES - width, 1), two)
            keep_ref[half, z] = jnp.where(core == 0, low, high)
            send_ref[half, z] = jnp.where(core == 0, high, low)
        return unused

    lax.fori_loop(0, pairs_deep, step, 0, unroll=2)


def observed_kernel(
    depth, probes, kappa_ref, observed_ref, even_ref, odd_ref, far_ref, factor_ref, data_ref
):
    level = lax.axis_index("level")
    tile = lax.axis_index("tile")
    last_tile = lax.axis_size("tile") - 1
    probe = lax.axis_index("probe")
    in_low = probe < probes // 2
    even = lax.rem(probe, 2) == 0
    width = LANES // 2
    lanes = lane_ids((ROWS, 2 * LANES))
    ids = row_ids((ROWS, LANES))
    base = even_ref.shape[0] - depth // ROWS
    from_even = lax.rem(tile, 2) == 1

    def half(value):
        return jnp.where(in_low, value[..., :LANES], value[..., LANES:])

    def take(value):
        return jnp.where(even, value, pltpu.roll(value, width, 1))[:, :width]

    far_edge = far_ref[far_ref.shape[0] - 1]
    for z in range(depth):
        value = observed_ref[z]
        mine = half(value)
        y_sides = jnp.where(lanes > 0, pltpu.roll(value, 1, 1), 0.0) + jnp.where(
            lanes < 2 * LANES - 1, pltpu.roll(value, 2 * LANES - 1, 1), 0.0
        )
        first = even_ref[base + z // ROWS, z % ROWS : z % ROWS + 1, :]
        second = odd_ref[base + z // ROWS, z % ROWS : z % ROWS + 1, :]
        left, right = jnp.where(from_even, first, second), jnp.where(from_even, second, first)
        before = jnp.where(ids > 0, pltpu.roll(mine, 1, 0), jnp.where(tile > 0, left, 0.0))
        after = jnp.where(
            ids < ROWS - 1, pltpu.roll(mine, ROWS - 1, 0), jnp.where(tile < last_tile, right, 0.0)
        )
        above = half(observed_ref[z - 1]) if z > 0 else jnp.where(level > 0, far_edge, 0.0)
        below = half(observed_ref[z + 1]) if z < depth - 1 else jnp.where(level == 0, far_edge, 0.0)
        kappa = half(kappa_ref[z])
        k_observed = (
            (kappa + (4.0 + 2.0 * VERTICAL)) * mine
            - (before + after)
            - half(y_sides)
            - VERTICAL * (above + below)
        )
        factor_ref[z] = take(kappa * (0.5 / probes))
        data_ref[z] = take(kappa * (2.0 * mine * k_observed))


def gradient_kernel(depth, trace_a_ref, trace_b_ref, factor_ref, data_ref, out_ref):
    width = LANES // 2
    square = (LANES, LANES)
    lane = lane_ids(square)
    source = (width // 2) * (lane // width) + (lane % width) // 2 + width * (lane % 2)
    chosen = jnp.where(row_ids(square) == source, 1.0, 0.0).astype(jnp.bfloat16)
    traces = pick((trace_a_ref[...] + trace_b_ref[...]).reshape(-1, LANES), chosen)
    traces = traces.reshape(depth // 2, ROWS, LANES)
    for z in range(depth // 2):
        out_ref[z] = factor_ref[z] * traces[z, :, :width] - data_ref[z]
        later = depth // 2 + z
        second = pltpu.roll(traces[z], width, 1)[:, :width]
        out_ref[later] = factor_ref[later] * second - data_ref[later]


def whole(count):
    return [pl.BlockSpec(memory_space=pltpu.VMEM)] * count


def body(probe_bits, kappa_sq, observed):
    probes, tile_count = lax.axis_size("probe"), lax.axis_size("tile")
    unused, depth, rows, columns = probe_bits.shape
    assert probe_bits.shape[0] == 1 and lax.axis_size("level") == 2 and probes == 4
    assert rows == ROWS and columns == 2 * LANES and depth % (2 * LANES // EDGE) == 0
    params = pltpu.CompilerParams(vmem_limit_bytes=24 * 1024 * 1024)
    f32 = jnp.float32
    tiles = depth * EDGE // LANES
    field = depth + tiles
    sent = field + field // 2
    own_shape = jax.ShapeDtypeStruct((2 * field, ROWS, LANES), f32)
    near_shape = jax.ShapeDtypeStruct((sent + depth // ROWS, ROWS, LANES), f32)
    far_shape = jax.ShapeDtypeStruct((sent + 1, ROWS, LANES), f32)

    own_block, even_block, odd_block, cross_block = pl.pallas_call(
        functools.partial(pack_kernel, depth),
        out_shape=(own_shape, near_shape, near_shape, far_shape),
        in_specs=[pl.BlockSpec(memory_space=pltpu.HBM)] * 3,
        out_specs=tuple(whole(4)),
        scratch_shapes=[
            pltpu.VMEM((depth, rows, columns), jnp.int32),
            pltpu.VMEM((depth, rows, columns), f32),
            pltpu.VMEM((depth, rows, columns), f32),
            pltpu.SemaphoreType.DMA((3,)),
        ],
        compiler_params=params,
        name="pack",
    )(
        *(
            pltpu.with_memory_space_constraint(value, pltpu.HBM)
            for value in (probe_bits[0], kappa_sq, observed)
        )
    )

    def swaps(pairs):
        return [way for a, b in pairs for way in ((a, b), (b, a))]

    even_pairs = [(i, i + 1) for i in range(0, tile_count - 1, 2)]
    odd_pairs = [(i, i + 1) for i in range(1, tile_count - 1, 2)]
    own_far = lax.ppermute(cross_block, "level", swaps([(0, 1)]))
    even = lax.ppermute(even_block, "tile", swaps(even_pairs))
    odd = lax.ppermute(odd_block, "tile", swaps(odd_pairs))
    odd_far = lax.ppermute(own_far, "tile", swaps(odd_pairs))
    even_far = lax.ppermute(
        cross_block,
        ("tile", "level"),
        swaps([(2 * a + level, 2 * b + 1 - level) for a, b in even_pairs for level in range(2)]),
    )

    quarter = jax.ShapeDtypeStruct((depth, ROWS, columns // probes), f32)
    factor, data = pl.pallas_call(
        functools.partial(observed_kernel, depth, probes),
        out_shape=(quarter, quarter),
        in_specs=whole(5),
        out_specs=tuple(whole(2)),
        compiler_params=params,
        name="observed",
    )(kappa_sq, observed, even, odd, own_far)

    def core_swap(*pieces):
        kappa = jnp.concatenate([piece[field:sent] for piece in pieces], axis=0)
        return lax.ppermute(kappa, "probe", swaps([(0, 1), (2, 3)]))

    swapped = core_swap(even, odd, own_far)
    levels = 2 * depth
    part = jax.ShapeDtypeStruct((depth, 3 * ROWS, 2 * LANES), f32)
    own_part = jax.ShapeDtypeStruct((depth, ROWS, 2 * LANES), f32)
    near_diag, near_lower, near_forward, near_signs, near_k_signs = pl.pallas_call(
        functools.partial(near_kernel, depth),
        out_shape=(part, part, part, own_part, own_part),
        in_specs=whole(4),
        out_specs=tuple(whole(5)),
        scratch_shapes=[pltpu.VMEM((depth + 2, 3 * ROWS, 2 * LANES), f32)],
        compiler_params=params,
        name="near",
    )(own_block, even, odd, swapped)

    swapped_far = core_swap(even_far, odd_far)
    padded = pltpu.VMEM((levels + 1, 3 * ROWS, 2 * LANES), f32)
    plain = pltpu.VMEM((levels, 3 * ROWS, 2 * LANES), f32)
    short = pltpu.VMEM((depth, 3 * ROWS, 2 * LANES), f32)
    fields = jax.ShapeDtypeStruct((ITERS, levels, ROWS, 2 * LANES), f32)
    basis, images, far_signs, far_k_signs, gram = pl.pallas_call(
        functools.partial(basis_kernel, depth),
        out_shape=(
            fields,
            fields,
            own_part,
            own_part,
            jax.ShapeDtypeStruct((2 * SLOTS, LANES), f32),
        ),
        in_specs=whole(9),
        out_specs=tuple(whole(5)),
        scratch_shapes=[
            pltpu.VMEM((depth + 2, 3 * ROWS, 2 * LANES), f32),
            short,
            short,
            padded,
            padded,
            plain,
            plain,
            padded,
            pltpu.VMEM((2 * SLOTS, ROWS, LANES), f32),
        ],
        compiler_params=params,
        name="basis",
    )(
        near_diag,
        near_lower,
        near_forward,
        near_signs,
        own_far,
        even_far,
        odd_far,
        swapped,
        swapped_far,
    )
    terms = pl.pallas_call(
        functools.partial(terms_kernel, depth),
        out_shape=jax.ShapeDtypeStruct((ITERS, levels, ROWS, LANES), f32),
        in_specs=whole(6),
        out_specs=pl.BlockSpec(memory_space=pltpu.VMEM),
        compiler_params=params,
        name="terms",
    )(basis, images, near_signs, near_k_signs, far_signs, far_k_signs)

    both = jnp.concatenate([gram, lax.ppermute(gram, "level", [(0, 1), (1, 0)])], axis=0)
    if tile_count in (2, 4):
        partials = [both] + [
            lax.ppermute(both, "tile", [(i, i ^ k) for i in range(tile_count)])
            for k in range(1, tile_count)
        ]
    else:
        partials = [lax.all_gather(both, "tile", axis=0, tiled=True)]
    piece = jax.ShapeDtypeStruct((2, depth // 2, ROWS, LANES), f32)
    keep, send = pl.pallas_call(
        functools.partial(combine_kernel, depth),
        out_shape=(piece, piece),
        in_specs=whole(1 + len(partials)),
        out_specs=tuple(whole(2)),
        compiler_params=params,
        name="combine",
    )(terms, *partials)

    summed = keep + lax.ppermute(send, "probe", [(0, 1), (1, 0), (2, 3), (3, 2)])
    half = lax.axis_index("probe") // 2
    straight = lax.dynamic_index_in_dim(summed, half, 0, keepdims=False)
    turned = lax.dynamic_index_in_dim(summed, 1 - half, 0, keepdims=False)

    def routes(flip):
        pairs = []
        for x in range(2):
            for core in range(2):
                for level in range(2):
                    target = x if not flip else 1 - x
                    pairs.append(((2 * x + core) * 2 + level, (2 * level + core) * 2 + target))
        return pairs

    trace_a = lax.ppermute(straight, ("probe", "level"), routes(False))
    trace_b = lax.ppermute(turned, ("probe", "level"), routes(True))
    return pl.pallas_call(
        functools.partial(gradient_kernel, depth),
        out_shape=quarter,
        in_specs=whole(4),
        out_specs=pl.BlockSpec(memory_space=pltpu.VMEM),
        compiler_params=params,
        name="gradient",
    )(trace_a, trace_b, factor, data)


def solution(mesh):
    in_specs = (
        P("probe", "level", "tile", None),
        P("level", "tile", None),
        P("level", "tile", None),
    )
    out_specs = P("level", "tile", "probe")
    return jax.shard_map(body, mesh=mesh, in_specs=in_specs, out_specs=out_specs, check_vma=False)
```

```python
import functools

import jax
import jax.numpy as jnp
from jax import lax
from jax.experimental import pallas as pl
from jax.experimental.pallas import tpu as pltpu
from jax.sharding import PartitionSpec as P

ITERS = 4
VERTICAL = 2.0
LANES = 128
ROWS = 8
EDGE = 8
GROUP = 8
SHIFTS = (1.0, 0.0, -2.0)
PAIRS = [(i, j) for j in range(ITERS) for i in range(j + 1)]
COUNT = len(PAIRS) + ITERS
SLOTS = 16


def two_sum(a, b):
    total = a + b
    part = total - a
    return total, (a - (total - part)) + (b - part)


def two_product(a, b):
    def split(v):
        big = v * 4097.0
        high = big - (big - v)
        return high, v - high

    product = a * b
    a_high, a_low = split(a)
    b_high, b_low = split(b)
    return product, ((a_high * b_high - product) + a_high * b_low + a_low * b_high) + a_low * b_low


def pair_add(first, second):
    total, rest = two_sum(first[0], second[0])
    rest = rest + (first[1] + second[1])
    high = total + rest
    return high, rest - (high - total)


def lane_ids(shape):
    return lax.broadcasted_iota(jnp.int32, shape, len(shape) - 1)


def row_ids(shape):
    return lax.broadcasted_iota(jnp.int32, shape, len(shape) - 2)


def split_three(values):
    high = values.astype(jnp.bfloat16)
    rest = values - high.astype(jnp.float32)
    middle = rest.astype(jnp.bfloat16)
    low = (rest - middle.astype(jnp.float32)).astype(jnp.bfloat16)
    return high, middle, low


def pick(values, chosen):
    high, middle, low = (
        jnp.dot(part, chosen, preferred_element_type=jnp.float32) for part in split_three(values)
    )
    return high + (middle + low)


def y_half():
    return lax.rem(lax.axis_index("level") + lax.axis_index("probe") // 2, 2)


def columns_of(half):
    shape = (2 * LANES, 2 * LANES)
    ids, lane = row_ids(shape), lane_ids(shape)
    odd = (lane // (LANES // 2)) % 2
    main = LANES * half + 2 * (lane % (LANES // 2)) + odd
    edge = LANES - EDGE * half + 2 * (lane % (EDGE // 2)) + odd
    wanted = jnp.where(lane < LANES, main, edge)
    return jnp.where(ids == wanted, 1.0, 0.0).astype(jnp.bfloat16)


def pack_kernel(
    depth,
    bits_hbm,
    kappa_hbm,
    observed_hbm,
    own_ref,
    even_ref,
    odd_ref,
    cross_ref,
    bits_ref,
    kappa_ref,
    observed_ref,
    arrived,
):
    copies = [
        pltpu.make_async_copy(source, target, arrived.at[place])
        for place, (source, target) in enumerate(
            ((bits_hbm, bits_ref), (kappa_hbm, kappa_ref), (observed_hbm, observed_ref))
        )
    ]
    for copy in copies:
        copy.start()
    level = lax.axis_index("level")
    first = level == 0
    in_first_core = lax.rem(lax.axis_index("probe"), 2) == 0
    per_tile = LANES // EDGE
    tiles = depth // per_tile
    field = depth + tiles
    slot_ids = (lane_ids((ROWS, LANES)) % (LANES // 2)) // (EDGE // 2)
    same_columns, cross_columns = columns_of(y_half()), columns_of(1 - y_half())

    def blocks(picked):
        picked = picked.reshape(depth, ROWS, 2 * LANES)
        edges = []
        for tile in range(tiles):
            packed = picked[tile * per_tile, :, LANES:]
            for slot in range(1, per_tile):
                packed = jnp.where(slot_ids == slot, picked[tile * per_tile + slot, :, LANES:], packed)
            edges.append(packed)
        return [picked[z, :, :LANES] for z in range(depth)], edges

    def write(refs, base, values):
        for place, value in enumerate(values):
            for ref in refs:
                ref[base + place] = value

    copies[0].wait()
    signs = (2 * bits_ref[...] - 1).astype(jnp.float32).reshape(depth * ROWS, 2 * LANES)
    signs = signs.astype(jnp.bfloat16)
    for refs, chosen in (((own_ref, even_ref, odd_ref), same_columns), ((cross_ref,), cross_columns)):
        main, edges = blocks(jnp.dot(signs, chosen, preferred_element_type=jnp.float32))
        write(refs, 0, main + edges)
    copies[1].wait()
    kappa = kappa_ref[...].reshape(depth * ROWS, 2 * LANES)
    for refs, chosen in (((even_ref, odd_ref), same_columns), ((cross_ref,), cross_columns)):
        main, edges = blocks(pick(kappa, chosen))
        if len(refs) == 2:
            write((own_ref,), field, main + edges)
        low = main[: depth // 2] + edges[: tiles // 2]
        high = main[depth // 2 :] + edges[tiles // 2 :]
        write(refs, field, [jnp.where(in_first_core, a, b) for a, b in zip(low, high)])
    copies[2].wait()
    base = field + field // 2
    in_low = lax.axis_index("probe") < lax.axis_size("probe") // 2

    def half(value):
        return jnp.where(in_low, value[..., :LANES], value[..., LANES:])

    top = half(observed_ref[:, ROWS - 1, :])
    bottom = half(observed_ref[:, 0, :])
    goes_up = lax.rem(lax.axis_index("tile"), 2) == 0
    for tile in range(depth // ROWS):
        here = slice(tile * ROWS, (tile + 1) * ROWS)
        even_ref[base + tile] = jnp.where(goes_up, top[here], bottom[here])
        odd_ref[base + tile] = jnp.where(goes_up, bottom[here], top[here])
    cross_ref[base] = jnp.where(first, half(observed_ref[depth - 1]), half(observed_ref[0]))


def beside(values):
    rows = values.shape[0]
    even, odd = values[:, :LANES], values[:, LANES:]
    y_sides = jnp.concatenate(
        [odd + pltpu.roll(odd, 1, 1), even + pltpu.roll(even, LANES - 1, 1)], axis=1
    )
    return (pltpu.roll(values, 1, 0) + pltpu.roll(values, rows - 1, 0)) + y_sides


def inside_mask():
    shape = (3 * ROWS, 2 * LANES)
    tile = lax.axis_index("tile")
    half = LANES // 2
    lanes, ids = lane_ids(shape) % LANES, row_ids(shape)
    near = jnp.where(y_half() == 0, half, LANES - EDGE // 2)
    inside = (lanes < half) | ((lanes >= near) & (lanes < near + EDGE // 2))
    inside = inside & (ids >= jnp.where(tile > 0, 0, ROWS))
    inside = inside & (ids < jnp.where(tile < lax.axis_size("tile") - 1, 3 * ROWS, 2 * ROWS))
    return jnp.where(inside, 1.0, 0.0)


def join(z, even, own, odd):
    half, short = LANES // 2, EDGE // 2
    from_even = lax.rem(lax.axis_index("tile"), 2) == 1
    mine = lane_ids((ROWS, LANES)) < half
    shift = half + (half - short) * y_half() - short * lax.rem(z, LANES // EDGE)
    shift = lax.rem(shift + LANES, LANES)
    left = [jnp.where(from_even, a, b) for a, b in zip(even, odd)]
    right = [jnp.where(from_even, b, a) for a, b in zip(even, odd)]
    evens, odds = [], []
    for main, edge in (left, own, right):
        edge = pltpu.roll(edge, shift, 1)
        evens.append(jnp.where(mine, main, edge))
        odds.append(pltpu.roll(jnp.where(mine, edge, main), half, 1))
    return jnp.concatenate([jnp.concatenate(evens, axis=0), jnp.concatenate(odds, axis=0)], axis=1)


def unpack(depth, signs, half_diag, mask, sign_pieces, kappa_pieces):
    level = lax.axis_index("level")
    per_tile = LANES // EDGE

    def place(z):
        return jnp.where(level == 0, z, depth - 1 - z)

    def sign_level(z, unused):
        pieces = [(ref[z], ref[depth + z // per_tile]) for ref in sign_pieces]
        signs[place(z) + 1] = join(z, *pieces) * mask
        return unused

    lax.fori_loop(0, depth, sign_level, 0, unroll=per_tile)
    core = lax.rem(lax.axis_index("probe"), 2)
    for start, pieces in zip((core, 1 - core), kappa_pieces):
        start = start * (depth // 2)

        def kappa_level(step, unused, start=start, pieces=pieces):
            z = start + step
            tiles = []
            for ref, base, whole_field in pieces:
                if whole_field:
                    tiles.append((ref[base + z], ref[base + depth + z // per_tile]))
                else:
                    tiles.append((ref[base + step], ref[base + depth // 2 + step // per_tile]))
            half_diag[place(z)] = 0.5 * join(z, *tiles) + (2.0 + VERTICAL)
            return unused

        lax.fori_loop(0, depth // 2, kappa_level, 0, unroll=per_tile)


OWN_ROWS = slice(ROWS, 2 * ROWS)


def near_kernel(
    depth,
    own_ref,
    even_ref,
    odd_ref,
    swapped_ref,
    half_diag,
    lower,
    forward,
    own_signs,
    k_signs,
    signs,
):
    field = own_ref.shape[0] // 2
    mask = inside_mask()
    zero = jnp.zeros(mask.shape, jnp.float32)
    signs[0] = zero
    signs[depth + 1] = zero
    kappa_pieces = (
        ((even_ref, field, False), (own_ref, field, True), (odd_ref, field, False)),
        ((swapped_ref, 0, False), (own_ref, field, True), (swapped_ref, field // 2, False)),
    )
    unpack(depth, signs, half_diag, mask, (even_ref, own_ref, odd_ref), kappa_pieces)

    def down(k, carry):
        ratio, value = carry
        ratio = mask / (half_diag[k] - ratio)
        here = signs[k + 1]
        value = ratio * (here + value)
        lower[k] = ratio
        forward[k] = value
        image = half_diag[k] * here - (signs[k] + signs[k + 2]) - 0.5 * beside(here)
        own_signs[k] = here[OWN_ROWS]
        k_signs[k] = image[OWN_ROWS]
        return ratio, value

    lax.fori_loop(0, depth, down, (zero, zero), unroll=GROUP)


def basis_kernel(
    depth,
    near_diag,
    near_lower,
    near_forward,
    near_signs,
    own_far_ref,
    even_far_ref,
    odd_far_ref,
    swapped_ref,
    swapped_far_ref,
    basis_ref,
    image_ref,
    far_signs,
    far_k_signs,
    gram_ref,
    signs,
    far_diag,
    far_lower,
    upper,
    basis,
    forward,
    sides,
    backward,
    sums,
):
    levels = 2 * depth
    mask = inside_mask()
    half_mask = 0.5 * mask
    zero = jnp.zeros(mask.shape, jnp.float32)
    own_zero = jnp.zeros((ROWS, LANES), jnp.float32)
    mine = lane_ids((ROWS, LANES)) < LANES // 2
    field = swapped_ref.shape[0] // 3 * 2
    signs[0] = zero
    signs[0, OWN_ROWS] = near_signs[depth - 1]
    signs[depth + 1] = zero
    backward[levels] = zero
    upper[levels] = zero
    basis[levels] = zero
    kappa_pieces = (
        tuple((ref, field, False) for ref in (even_far_ref, own_far_ref, odd_far_ref)),
        (
            (swapped_far_ref, 0, False),
            (swapped_ref, field, False),
            (swapped_far_ref, field // 2, False),
        ),
    )
    unpack(depth, signs, far_diag, mask, (even_far_ref, own_far_ref, odd_far_ref), kappa_pieces)

    def start_down(k, carry):
        ratio, value, from_end = carry
        ratio = mask / (far_diag[k] - ratio)
        here = signs[k + 1]
        value = ratio * (here + value)
        far_lower[k] = ratio
        forward[depth + k] = value
        other = depth - 1 - k
        from_end = mask / (far_diag[other] - from_end)
        upper[depth + other] = from_end
        image = far_diag[k] * here - (signs[k] + signs[k + 2]) - 0.5 * beside(here)
        far_signs[k] = here[OWN_ROWS]
        far_k_signs[k] = image[OWN_ROWS]
        return ratio, value, from_end

    start = (near_lower[depth - 1], near_forward[depth - 1], zero)
    carry = lax.fori_loop(0, depth, start_down, start, unroll=GROUP)

    def start_up_far(step, carry):
        k = depth - 1 - step
        solved, value = carry
        solved = forward[depth + k] + far_lower[k] * solved
        value = upper[depth + k] * (solved + value)
        backward[depth + k] = value
        return solved, value

    solved, value = lax.fori_loop(0, depth, start_up_far, (zero, zero), unroll=GROUP)

    def start_up_near(step, carry):
        k = depth - 1 - step
        ratio, solved, value = carry
        ratio = mask / (near_diag[k] - ratio)
        solved = near_forward[k] + near_lower[k] * solved
        value = ratio * (solved + value)
        upper[k] = ratio
        backward[k] = value
        return ratio, solved, value

    lax.fori_loop(0, depth, start_up_near, (carry[2], solved, value), unroll=GROUP)

    parts = (
        (0, near_diag, near_lower, lambda k: near_signs[k]),
        (depth, far_diag, far_lower, lambda k: signs[k + 1, OWN_ROWS]),
    )
    place = 0
    for index in range(ITERS):
        final = index + 1 == ITERS
        group_size = 2 * GROUP if final else GROUP

        def next_basis(k, previous, index=index):
            solved = backward[k] + upper[k] * previous
            if index == 0:
                value = solved
            elif SHIFTS[index - 1] == 0.0:
                value = -solved
            else:
                value = SHIFTS[index - 1] * basis[k] - solved
            return solved, value

        solved, here = next_basis(0, zero)
        if not final:
            basis[0] = here
        carry = (solved, zero, here, zero) + (own_zero,) * (2 * (index + 2))
        for offset, half_diag, lower, sign_of in parts:

            def down(group, carry):
                solved, above, here, value, *totals = carry
                products = []
                for step in range(group_size):
                    k = group * group_size + step
                    solved, below = next_basis(offset + k + 1, solved)
                    if not final:
                        basis[offset + k + 1] = below
                    side = beside(here)
                    image = half_diag[k] * here - (above + below) - half_mask * side
                    if not final:
                        value = lower[k] * (beside(image) + value)
                        forward[offset + k] = value
                        sides[offset + k] = side
                    my_basis, my_image = here[OWN_ROWS], image[OWN_ROWS]
                    basis_ref[index, offset + k] = my_basis
                    image_ref[index, offset + k] = my_image
                    factors = [(image_ref[other, offset + k], my_image) for other in range(index)]
                    factors += [(my_image, my_image), (my_basis, sign_of(k))]
                    products.append(
                        [a[:, :LANES] * b[:, :LANES] + a[:, LANES:] * b[:, LANES:] for a, b in factors]
                    )
                    above, here = here, below
                for slot in range(index + 2):
                    for four in range(0, group_size, 4):
                        added = (products[four][slot] + products[four + 1][slot]) + (
                            products[four + 2][slot] + products[four + 3][slot]
                        )
                        totals[2 * slot], rest = two_sum(totals[2 * slot], added)
                        totals[2 * slot + 1] = totals[2 * slot + 1] + rest
                return (solved, above, here, value, *totals)

            carry = lax.fori_loop(0, depth // group_size, down, carry)
        totals = [jnp.where(mine, total, 0.0) for total in carry[4:]]
        for slot in range(index + 1):
            sums[2 * (place + slot)] = totals[2 * slot]
            sums[2 * (place + slot) + 1] = totals[2 * slot + 1]
        place += index + 1
        sums[2 * (len(PAIRS) + index)] = totals[2 * index + 2]
        sums[2 * (len(PAIRS) + index) + 1] = totals[2 * index + 3]
        if final:
            break
        carry = (zero, zero)
        for offset, half_diag, lower, sign_of in reversed(parts):

            def up(step, carry):
                k = depth - 1 - step
                solved, value = carry
                solved = forward[offset + k] + lower[k] * solved
                value = upper[offset + k] * ((sides[offset + k] + solved) + value)
                backward[offset + k] = value
                return solved, value

            carry = lax.fori_loop(0, depth, up, carry, unroll=4 * GROUP)

    ids = row_ids((ROWS, LANES))
    sides_of = [[], []]
    for block in range(SLOTS // ROWS):
        high, low = own_zero, own_zero
        for slot in range(block * ROWS, min((block + 1) * ROWS, COUNT)):
            pair = (sums[2 * slot], sums[2 * slot + 1])
            for shift in (4, 2, 1):
                pair = pair_add(pair, tuple(pltpu.roll(part, shift, 0) for part in pair))
            here = ids == slot - block * ROWS
            high, low = jnp.where(here, pair[0], high), jnp.where(here, pair[1], low)
        sides_of[0].append(high)
        sides_of[1].append(low)
    ones = jnp.ones((LANES, LANES), jnp.bfloat16)

    def lane_sum(part):
        return jnp.dot(part, ones, preferred_element_type=jnp.float32)

    high, low = (jnp.concatenate(blocks, axis=0) for blocks in sides_of)
    first, second, third = (lane_sum(part) for part in split_three(high))
    high, rest = two_sum(first, second)
    low = rest + (third + lane_sum(low.astype(jnp.bfloat16)))
    quarter = lane_ids((ROWS, LANES)) // (LANES // 4)
    tile = high[:ROWS]
    for place, block in enumerate((high[ROWS:], low[:ROWS], low[ROWS:])):
        tile = jnp.where(quarter == place + 1, block, tile)
    gram_ref[...] = tile


def terms_kernel(
    depth, basis_ref, image_ref, near_signs, near_k_signs, far_signs, far_k_signs, terms_ref
):
    level = lax.axis_index("level")
    half = LANES // 2
    mine = lane_ids((ROWS, LANES)) < half
    for offset, signs, k_signs in ((0, near_signs, near_k_signs), (depth, far_signs, far_k_signs)):

        def step(k, unused, offset=offset, signs=signs, k_signs=k_signs):
            z = offset + k
            target = jnp.where(level == 0, z, 2 * depth - 1 - z)
            sign, image = signs[k], k_signs[k]
            for index in range(ITERS):
                term = basis_ref[index, z] * image + image_ref[index, z] * sign
                terms_ref[index, target] = jnp.where(
                    mine, term[:, :LANES], pltpu.roll(term[:, LANES:], half, 1)
                )
            return unused

        if offset == 0:
            lax.fori_loop(0, depth - 1, step, 0, unroll=GROUP)
            sign, image = signs[depth - 1], k_signs[depth - 1] - far_signs[0]
            target = jnp.where(level == 0, depth - 1, depth)
            for index in range(ITERS):
                term = basis_ref[index, depth - 1] * image + image_ref[index, depth - 1] * sign
                terms_ref[index, target] = jnp.where(
                    mine, term[:, :LANES], pltpu.roll(term[:, LANES:], half, 1)
                )
        else:
            lax.fori_loop(0, depth, step, 0, unroll=GROUP)


def solve_small(high, low):
    def entry(index):
        return tuple(jnp.broadcast_to(part[index : index + 1], (ROWS, LANES)) for part in (high, low))

    gram = {}
    for place, (i, j) in enumerate(PAIRS):
        gram[i, j] = gram[j, i] = entry(place)
    right = [entry(len(PAIRS) + j) for j in range(ITERS)]
    work = {key: pair[0] for key, pair in gram.items()}
    ratios, inverses = {}, []
    for i in range(ITERS):
        pivot = work[i, i]
        good = pivot > 1e-7 * gram[i, i][0]
        inverses.append(jnp.where(good, 1.0 / jnp.where(good, pivot, 1.0), 0.0))
        for r in range(i + 1, ITERS):
            ratios[r, i] = work[r, i] * inverses[i]
        for r in range(i + 1, ITERS):
            for c in range(i + 1, r + 1):
                work[r, c] = work[c, r] = work[r, c] - ratios[r, i] * work[c, i]

    def solve(values):
        values = list(values)
        for i in range(ITERS):
            for r in range(i + 1, ITERS):
                values[r] = values[r] - ratios[r, i] * values[i]
        values = [value * inverse for value, inverse in zip(values, inverses)]
        for i in reversed(range(ITERS)):
            for r in range(i):
                values[r] = values[r] - ratios[i, r] * values[i]
        return values

    found = solve([pair[0] for pair in right])
    for unused in range(2):
        rest = []
        for i in range(ITERS):
            total = right[i]
            for j in range(ITERS):
                product, error = two_product(gram[i, j][0], found[j])
                total = pair_add(total, (-product, -(error + gram[i, j][1] * found[j])))
            rest.append(total[0] + total[1])
        found = [a + b for a, b in zip(found, solve(rest))]
    return found


def combine_kernel(depth, terms_ref, *refs):
    gram_refs, (keep_ref, send_ref) = refs[:-2], refs[-2:]
    half, width = LANES // 2, LANES // 4
    pairs = []
    for ref in gram_refs:
        for start in range(0, ref.shape[0], ROWS):
            tile = ref[start : start + ROWS]
            pairs.append((tile, pltpu.roll(tile, half, 1)))
    while len(pairs) > 1:
        merged = [pair_add(pairs[i], pairs[i + 1]) for i in range(0, len(pairs) - 1, 2)]
        pairs = merged + pairs[2 * len(merged) :]
    lanes = lane_ids((ROWS, LANES))

    def spread(part, block):
        part = jnp.where(lanes // width == block, part, 0.0)
        part = part + pltpu.roll(part, width, 1)
        return part + pltpu.roll(part, half, 1)

    found = solve_small(
        *(jnp.concatenate([spread(part, 0), spread(part, 1)], axis=0) for part in pairs[0])
    )
    core = lax.rem(lax.axis_index("probe"), 2)
    first_lanes = lanes % half < width
    pairs_deep = depth // 2

    def step(z, unused):
        for which in range(2):
            def total(k):
                value = found[0] * terms_ref[0, k]
                for j in range(1, ITERS):
                    value = value + found[j] * terms_ref[j, k]
                return value

            one = total(which * depth + z)
            two = total(which * depth + pairs_deep + z)
            low = jnp.where(first_lanes, one, pltpu.roll(two, width, 1))
            high = jnp.where(first_lanes, pltpu.roll(one, LANES - width, 1), two)
            keep_ref[which, z] = jnp.where(core == 0, low, high)
            send_ref[which, z] = jnp.where(core == 0, high, low)
        return unused

    lax.fori_loop(0, pairs_deep, step, 0, unroll=GROUP)


def observed_kernel(
    depth, probes, kappa_ref, observed_ref, even_ref, odd_ref, far_ref, factor_ref, data_ref
):
    level = lax.axis_index("level")
    tile = lax.axis_index("tile")
    last_tile = lax.axis_size("tile") - 1
    probe = lax.axis_index("probe")
    in_low = probe < probes // 2
    even = lax.rem(probe, 2) == 0
    width = LANES // 2
    lanes = lane_ids((ROWS, 2 * LANES))
    ids = row_ids((ROWS, LANES))
    base = even_ref.shape[0] - depth // ROWS
    from_even = lax.rem(tile, 2) == 1

    def half(value):
        return jnp.where(in_low, value[..., :LANES], value[..., LANES:])

    def take(value):
        return jnp.where(even, value, pltpu.roll(value, width, 1))

    far_edge = far_ref[far_ref.shape[0] - 1]
    factors, parts = [], []
    for z in range(depth):
        value = observed_ref[z]
        mine = half(value)
        y_sides = jnp.where(lanes > 0, pltpu.roll(value, 1, 1), 0.0) + jnp.where(
            lanes < 2 * LANES - 1, pltpu.roll(value, 2 * LANES - 1, 1), 0.0
        )
        first = even_ref[base + z // ROWS, z % ROWS : z % ROWS + 1, :]
        second = odd_ref[base + z // ROWS, z % ROWS : z % ROWS + 1, :]
        left, right = jnp.where(from_even, first, second), jnp.where(from_even, second, first)
        before = jnp.where(ids > 0, pltpu.roll(mine, 1, 0), jnp.where(tile > 0, left, 0.0))
        after = jnp.where(
            ids < ROWS - 1, pltpu.roll(mine, ROWS - 1, 0), jnp.where(tile < last_tile, right, 0.0)
        )
        above = half(observed_ref[z - 1]) if z > 0 else jnp.where(level > 0, far_edge, 0.0)
        below = half(observed_ref[z + 1]) if z < depth - 1 else jnp.where(level == 0, far_edge, 0.0)
        kappa = half(kappa_ref[z])
        k_observed = (
            (kappa + (4.0 + 2.0 * VERTICAL)) * mine
            - (before + after)
            - half(y_sides)
            - VERTICAL * (above + below)
        )
        factors.append(take(kappa * (0.5 / probes)))
        parts.append(take(kappa * (2.0 * mine * k_observed)))
    first_lanes = lane_ids((ROWS, LANES)) < width
    for ref, values in ((factor_ref, factors), (data_ref, parts)):
        for z in range(depth // 2):
            ref[z] = jnp.where(first_lanes, values[z], pltpu.roll(values[depth // 2 + z], width, 1))


def gradient_kernel(
    depth, trace_a_ref, trace_b_ref, straight_ref, factor_ref, data_ref, out_ref
):
    width = LANES // 2
    square = (LANES, LANES)
    lane = lane_ids(square)
    source = (width // 2) * (lane // width) + (lane % width) // 2 + width * (lane % 2)
    chosen = jnp.where(row_ids(square) == source, 1.0, 0.0).astype(jnp.bfloat16)
    stays = lax.axis_index("level") == 0
    traces = trace_a_ref[...] + jnp.where(stays, straight_ref[...], trace_b_ref[...])
    traces = pick(traces.reshape(-1, LANES), chosen).reshape(traces.shape)
    values = factor_ref[...] * traces - data_ref[...]
    for z in range(depth // 2):
        out_ref[z] = values[z, :, :width]
        out_ref[depth // 2 + z] = pltpu.roll(values[z], width, 1)[:, :width]


def whole(count):
    return [pl.BlockSpec(memory_space=pltpu.VMEM)] * count


def body(probe_bits, kappa_sq, observed):
    probes, tile_count = lax.axis_size("probe"), lax.axis_size("tile")
    unused, depth, rows, columns = probe_bits.shape
    assert probe_bits.shape[0] == 1 and lax.axis_size("level") == 2 and probes == 4
    assert rows == ROWS and columns == 2 * LANES and depth % (2 * LANES // EDGE) == 0
    params = pltpu.CompilerParams(vmem_limit_bytes=24 * 1024 * 1024)
    f32 = jnp.float32
    tiles = depth * EDGE // LANES
    field = depth + tiles
    sent = field + field // 2
    own_shape = jax.ShapeDtypeStruct((2 * field, ROWS, LANES), f32)
    near_shape = jax.ShapeDtypeStruct((sent + depth // ROWS, ROWS, LANES), f32)
    far_shape = jax.ShapeDtypeStruct((sent + 1, ROWS, LANES), f32)

    own_block, even_block, odd_block, cross_block = pl.pallas_call(
        functools.partial(pack_kernel, depth),
        out_shape=(own_shape, near_shape, near_shape, far_shape),
        in_specs=[pl.BlockSpec(memory_space=pltpu.HBM)] * 3,
        out_specs=tuple(whole(4)),
        scratch_shapes=[
            pltpu.VMEM((depth, rows, columns), jnp.int32),
            pltpu.VMEM((depth, rows, columns), f32),
            pltpu.VMEM((depth, rows, columns), f32),
            pltpu.SemaphoreType.DMA((3,)),
        ],
        compiler_params=params,
        name="pack",
    )(
        *(
            pltpu.with_memory_space_constraint(value, pltpu.HBM)
            for value in (probe_bits[0], kappa_sq, observed)
        )
    )

    def swaps(pairs):
        return [way for a, b in pairs for way in ((a, b), (b, a))]

    even_pairs = [(i, i + 1) for i in range(0, tile_count - 1, 2)]
    odd_pairs = [(i, i + 1) for i in range(1, tile_count - 1, 2)]
    own_far = lax.ppermute(cross_block, "level", swaps([(0, 1)]))
    even = lax.ppermute(even_block, "tile", swaps(even_pairs))
    odd = lax.ppermute(odd_block, "tile", swaps(odd_pairs))
    odd_far = lax.ppermute(own_far, "tile", swaps(odd_pairs))
    even_far = lax.ppermute(
        cross_block,
        ("tile", "level"),
        swaps([(2 * a + level, 2 * b + 1 - level) for a, b in even_pairs for level in range(2)]),
    )

    quarter = jax.ShapeDtypeStruct((depth, ROWS, columns // probes), f32)
    paired = jax.ShapeDtypeStruct((depth // 2, ROWS, LANES), f32)
    factor, data = pl.pallas_call(
        functools.partial(observed_kernel, depth, probes),
        out_shape=(paired, paired),
        in_specs=whole(5),
        out_specs=tuple(whole(2)),
        compiler_params=params,
        name="observed",
    )(kappa_sq, observed, even, odd, own_far)

    def core_swap(*pieces):
        kappa = jnp.concatenate([piece[field:sent] for piece in pieces], axis=0)
        return lax.ppermute(kappa, "probe", swaps([(0, 1), (2, 3)]))

    swapped = core_swap(even, odd, own_far)
    levels = 2 * depth
    part = jax.ShapeDtypeStruct((depth, 3 * ROWS, 2 * LANES), f32)
    own_part = jax.ShapeDtypeStruct((depth, ROWS, 2 * LANES), f32)
    near_diag, near_lower, near_forward, near_signs, near_k_signs = pl.pallas_call(
        functools.partial(near_kernel, depth),
        out_shape=(part, part, part, own_part, own_part),
        in_specs=whole(4),
        out_specs=tuple(whole(5)),
        scratch_shapes=[pltpu.VMEM((depth + 2, 3 * ROWS, 2 * LANES), f32)],
        compiler_params=params,
        name="near",
    )(own_block, even, odd, swapped)

    swapped_far = core_swap(even_far, odd_far)
    padded = pltpu.VMEM((levels + 1, 3 * ROWS, 2 * LANES), f32)
    plain = pltpu.VMEM((levels, 3 * ROWS, 2 * LANES), f32)
    short = pltpu.VMEM((depth, 3 * ROWS, 2 * LANES), f32)
    fields = jax.ShapeDtypeStruct((ITERS, levels, ROWS, 2 * LANES), f32)
    basis, images, far_signs, far_k_signs, gram = pl.pallas_call(
        functools.partial(basis_kernel, depth),
        out_shape=(
            fields,
            fields,
            own_part,
            own_part,
            jax.ShapeDtypeStruct((ROWS, LANES), f32),
        ),
        in_specs=whole(9),
        out_specs=tuple(whole(5)),
        scratch_shapes=[
            pltpu.VMEM((depth + 2, 3 * ROWS, 2 * LANES), f32),
            short,
            short,
            padded,
            padded,
            plain,
            plain,
            padded,
            pltpu.VMEM((2 * SLOTS, ROWS, LANES), f32),
        ],
        compiler_params=params,
        name="basis",
    )(
        near_diag,
        near_lower,
        near_forward,
        near_signs,
        own_far,
        even_far,
        odd_far,
        swapped,
        swapped_far,
    )
    terms = pl.pallas_call(
        functools.partial(terms_kernel, depth),
        out_shape=jax.ShapeDtypeStruct((ITERS, levels, ROWS, LANES), f32),
        in_specs=whole(6),
        out_specs=pl.BlockSpec(memory_space=pltpu.VMEM),
        compiler_params=params,
        name="terms",
    )(basis, images, near_signs, near_k_signs, far_signs, far_k_signs)

    if tile_count in (2, 4):
        group = [gram] + [
            lax.ppermute(
                gram,
                ("tile", "level"),
                swaps([(i, i ^ k) for i in range(2 * tile_count) if i < i ^ k]),
            )
            for k in (1, 2, 3)
        ]
        partials = [jnp.concatenate(group, axis=0)]
        if tile_count == 4:
            partials.append(lax.ppermute(partials[0], "tile", swaps([(0, 2), (1, 3)])))
    else:
        partials = [lax.all_gather(gram, ("tile", "level"), axis=0, tiled=True)]
    piece = jax.ShapeDtypeStruct((2, depth // 2, ROWS, LANES), f32)
    keep, send = pl.pallas_call(
        functools.partial(combine_kernel, depth),
        out_shape=(piece, piece),
        in_specs=whole(1 + len(partials)),
        out_specs=tuple(whole(2)),
        compiler_params=params,
        name="combine",
    )(terms, *partials)

    summed = keep + lax.ppermute(send, "probe", swaps([(0, 1), (2, 3)]))
    level = lax.axis_index("level")
    turned = lax.dynamic_index_in_dim(summed, 1 - level, 0, keepdims=False)
    straight = lax.dynamic_index_in_dim(summed, level, 0, keepdims=False)

    def device(x, core, level):
        return (2 * x + core) * 2 + level

    chips = [(x, core) for x in range(2) for core in range(2)]
    trace_a = lax.ppermute(
        turned,
        ("probe", "level"),
        [(device(x, core, 0), device(x, core, 1)) for x, core in chips]
        + [(device(x, core, 1), device(1 - x, core, 0)) for x, core in chips],
    )
    trace_b = lax.ppermute(
        straight,
        ("probe", "level"),
        [(device(x, core, 1), device(1 - x, core, 1)) for x, core in chips],
    )
    return pl.pallas_call(
        functools.partial(gradient_kernel, depth),
        out_shape=quarter,
        in_specs=whole(5),
        out_specs=pl.BlockSpec(memory_space=pltpu.VMEM),
        compiler_params=params,
        name="gradient",
    )(trace_a, trace_b, straight, factor, data)


def solution(mesh):
    in_specs = (
        P("probe", "level", "tile", None),
        P("level", "tile", None),
        P("level", "tile", None),
    )
    out_specs = P("level", "tile", "probe")
    return jax.shard_map(body, mesh=mesh, in_specs=in_specs, out_specs=out_specs, check_vma=False)
```

```python
import functools

import jax
import jax.numpy as jnp
from jax import lax
from jax.experimental import pallas as pl
from jax.experimental.pallas import tpu as pltpu
from jax.sharding import PartitionSpec as P

ITERS = 4
VERTICAL = 2.0
LANES = 128
ROWS = 8
EDGE = 8
GROUP = 8
SHIFTS = (1.0, -1.0, 0.0)
PAIRS = [(i, j) for j in range(ITERS) for i in range(j + 1)]
COUNT = len(PAIRS) + ITERS
SLOTS = 16


def two_sum(a, b):
    total = a + b
    part = total - a
    return total, (a - (total - part)) + (b - part)


def two_product(a, b):
    def split(v):
        big = v * 4097.0
        high = big - (big - v)
        return high, v - high

    product = a * b
    a_high, a_low = split(a)
    b_high, b_low = split(b)
    return product, ((a_high * b_high - product) + a_high * b_low + a_low * b_high) + a_low * b_low


def pair_add(first, second):
    total, rest = two_sum(first[0], second[0])
    rest = rest + (first[1] + second[1])
    high = total + rest
    return high, rest - (high - total)


def lane_ids(shape):
    return lax.broadcasted_iota(jnp.int32, shape, len(shape) - 1)


def row_ids(shape):
    return lax.broadcasted_iota(jnp.int32, shape, len(shape) - 2)


def split_three(values):
    high = values.astype(jnp.bfloat16)
    rest = values - high.astype(jnp.float32)
    middle = rest.astype(jnp.bfloat16)
    low = (rest - middle.astype(jnp.float32)).astype(jnp.bfloat16)
    return high, middle, low


def pick(values, chosen):
    high, middle, low = (
        jnp.dot(part, chosen, preferred_element_type=jnp.float32) for part in split_three(values)
    )
    return high + (middle + low)


def y_half():
    return lax.rem(lax.axis_index("level") + lax.axis_index("probe") // 2, 2)


def columns_of(half):
    shape = (2 * LANES, 2 * LANES)
    ids, lane = row_ids(shape), lane_ids(shape)
    odd = (lane // (LANES // 2)) % 2
    main = LANES * half + 2 * (lane % (LANES // 2)) + odd
    edge = LANES - EDGE * half + 2 * (lane % (EDGE // 2)) + odd
    wanted = jnp.where(lane < LANES, main, edge)
    return jnp.where(ids == wanted, 1.0, 0.0).astype(jnp.bfloat16)


def pack_kernel(
    depth,
    bits_hbm,
    kappa_hbm,
    observed_hbm,
    own_ref,
    even_ref,
    odd_ref,
    cross_ref,
    bits_ref,
    kappa_ref,
    observed_ref,
    arrived,
):
    copies = [
        pltpu.make_async_copy(source, target, arrived.at[place])
        for place, (source, target) in enumerate(
            ((bits_hbm, bits_ref), (kappa_hbm, kappa_ref), (observed_hbm, observed_ref))
        )
    ]
    for copy in copies:
        copy.start()
    level = lax.axis_index("level")
    first = level == 0
    in_first_core = lax.rem(lax.axis_index("probe"), 2) == 0
    per_tile = LANES // EDGE
    tiles = depth // per_tile
    field = depth + tiles
    slot_ids = (lane_ids((ROWS, LANES)) % (LANES // 2)) // (EDGE // 2)
    same_columns, cross_columns = columns_of(y_half()), columns_of(1 - y_half())

    def blocks(picked):
        picked = picked.reshape(depth, ROWS, 2 * LANES)
        edges = []
        for tile in range(tiles):
            packed = picked[tile * per_tile, :, LANES:]
            for slot in range(1, per_tile):
                packed = jnp.where(slot_ids == slot, picked[tile * per_tile + slot, :, LANES:], packed)
            edges.append(packed)
        return [picked[z, :, :LANES] for z in range(depth)], edges

    def write(refs, base, values):
        for place, value in enumerate(values):
            for ref in refs:
                ref[base + place] = value

    copies[0].wait()
    signs = (2 * bits_ref[...] - 1).astype(jnp.float32).reshape(depth * ROWS, 2 * LANES)
    signs = signs.astype(jnp.bfloat16)
    for refs, chosen in (((own_ref, even_ref, odd_ref), same_columns), ((cross_ref,), cross_columns)):
        main, edges = blocks(jnp.dot(signs, chosen, preferred_element_type=jnp.float32))
        write(refs, 0, main + edges)
    copies[1].wait()
    kappa = kappa_ref[...].reshape(depth * ROWS, 2 * LANES)
    for refs, chosen in (((even_ref, odd_ref), same_columns), ((cross_ref,), cross_columns)):
        main, edges = blocks(pick(kappa, chosen))
        if len(refs) == 2:
            write((own_ref,), field, main + edges)
        low = main[: depth // 2] + edges[: tiles // 2]
        high = main[depth // 2 :] + edges[tiles // 2 :]
        write(refs, field, [jnp.where(in_first_core, a, b) for a, b in zip(low, high)])
    copies[2].wait()
    base = field + field // 2
    in_low = lax.axis_index("probe") < lax.axis_size("probe") // 2

    def half(value):
        return jnp.where(in_low, value[..., :LANES], value[..., LANES:])

    top = half(observed_ref[:, ROWS - 1, :])
    bottom = half(observed_ref[:, 0, :])
    goes_up = lax.rem(lax.axis_index("tile"), 2) == 0
    for tile in range(depth // ROWS):
        here = slice(tile * ROWS, (tile + 1) * ROWS)
        even_ref[base + tile] = jnp.where(goes_up, top[here], bottom[here])
        odd_ref[base + tile] = jnp.where(goes_up, bottom[here], top[here])
    cross_ref[base] = jnp.where(first, half(observed_ref[depth - 1]), half(observed_ref[0]))


def beside(values):
    rows = values.shape[0]
    even, odd = values[:, :LANES], values[:, LANES:]
    y_sides = jnp.concatenate(
        [odd + pltpu.roll(odd, 1, 1), even + pltpu.roll(even, LANES - 1, 1)], axis=1
    )
    return (pltpu.roll(values, 1, 0) + pltpu.roll(values, rows - 1, 0)) + y_sides


def inside_mask():
    shape = (3 * ROWS, 2 * LANES)
    tile = lax.axis_index("tile")
    half = LANES // 2
    lanes, ids = lane_ids(shape) % LANES, row_ids(shape)
    near = jnp.where(y_half() == 0, half, LANES - EDGE // 2)
    inside = (lanes < half) | ((lanes >= near) & (lanes < near + EDGE // 2))
    inside = inside & (ids >= jnp.where(tile > 0, 0, ROWS))
    inside = inside & (ids < jnp.where(tile < lax.axis_size("tile") - 1, 3 * ROWS, 2 * ROWS))
    return jnp.where(inside, 1.0, 0.0)


def join(z, even, own, odd):
    half, short = LANES // 2, EDGE // 2
    from_even = lax.rem(lax.axis_index("tile"), 2) == 1
    mine = lane_ids((ROWS, LANES)) < half
    shift = half + (half - short) * y_half() - short * lax.rem(z, LANES // EDGE)
    shift = lax.rem(shift + LANES, LANES)
    left = [jnp.where(from_even, a, b) for a, b in zip(even, odd)]
    right = [jnp.where(from_even, b, a) for a, b in zip(even, odd)]
    evens, odds = [], []
    for main, edge in (left, own, right):
        edge = pltpu.roll(edge, shift, 1)
        evens.append(jnp.where(mine, main, edge))
        odds.append(pltpu.roll(jnp.where(mine, edge, main), half, 1))
    return jnp.concatenate([jnp.concatenate(evens, axis=0), jnp.concatenate(odds, axis=0)], axis=1)


def unpack(depth, signs, half_diag, mask, sign_pieces, kappa_pieces):
    level = lax.axis_index("level")
    per_tile = LANES // EDGE

    def place(z):
        return jnp.where(level == 0, z, depth - 1 - z)

    def sign_level(z, unused):
        pieces = [(ref[z], ref[depth + z // per_tile]) for ref in sign_pieces]
        signs[place(z) + 1] = join(z, *pieces) * mask
        return unused

    lax.fori_loop(0, depth, sign_level, 0, unroll=per_tile)
    core = lax.rem(lax.axis_index("probe"), 2)
    for start, pieces in zip((core, 1 - core), kappa_pieces):
        start = start * (depth // 2)

        def kappa_level(step, unused, start=start, pieces=pieces):
            z = start + step
            tiles = []
            for ref, base, whole_field in pieces:
                if whole_field:
                    tiles.append((ref[base + z], ref[base + depth + z // per_tile]))
                else:
                    tiles.append((ref[base + step], ref[base + depth // 2 + step // per_tile]))
            half_diag[place(z)] = 0.5 * join(z, *tiles) + (2.0 + VERTICAL)
            return unused

        lax.fori_loop(0, depth // 2, kappa_level, 0, unroll=per_tile)


OWN_ROWS = slice(ROWS, 2 * ROWS)


def near_kernel(
    depth,
    own_ref,
    even_ref,
    odd_ref,
    swapped_ref,
    half_diag,
    lower,
    forward,
    own_signs,
    k_signs,
    signs,
):
    field = own_ref.shape[0] // 2
    mask = inside_mask()
    zero = jnp.zeros(mask.shape, jnp.float32)
    signs[0] = zero
    signs[depth + 1] = zero
    kappa_pieces = (
        ((even_ref, field, False), (own_ref, field, True), (odd_ref, field, False)),
        ((swapped_ref, 0, False), (own_ref, field, True), (swapped_ref, field // 2, False)),
    )
    unpack(depth, signs, half_diag, mask, (even_ref, own_ref, odd_ref), kappa_pieces)

    def down(k, carry):
        ratio, value = carry
        ratio = mask / (half_diag[k] - ratio)
        here = signs[k + 1]
        value = ratio * (here + value)
        lower[k] = ratio
        forward[k] = value
        image = half_diag[k] * here - (signs[k] + signs[k + 2]) - 0.5 * beside(here)
        own_signs[k] = here[OWN_ROWS]
        k_signs[k] = image[OWN_ROWS]
        return ratio, value

    lax.fori_loop(0, depth, down, (zero, zero), unroll=GROUP)


def basis_kernel(
    depth,
    near_diag,
    near_lower,
    near_forward,
    near_signs,
    own_far_ref,
    even_far_ref,
    odd_far_ref,
    swapped_ref,
    swapped_far_ref,
    basis_ref,
    image_ref,
    far_signs,
    far_k_signs,
    gram_ref,
    signs,
    far_diag,
    far_lower,
    upper,
    basis,
    forward,
    sides,
    backward,
    sums,
    masks,
):
    levels = 2 * depth
    mask = inside_mask()
    half_mask = 0.5 * mask
    masks[...] = half_mask
    zero = jnp.zeros(mask.shape, jnp.float32)
    own_zero = jnp.zeros((ROWS, LANES), jnp.float32)
    mine = lane_ids((ROWS, LANES)) < LANES // 2
    field = swapped_ref.shape[0] // 3 * 2
    signs[0] = zero
    signs[0, OWN_ROWS] = near_signs[depth - 1]
    signs[depth + 1] = zero
    backward[levels] = zero
    upper[levels] = zero
    basis[levels] = zero
    kappa_pieces = (
        tuple((ref, field, False) for ref in (even_far_ref, own_far_ref, odd_far_ref)),
        (
            (swapped_far_ref, 0, False),
            (swapped_ref, field, False),
            (swapped_far_ref, field // 2, False),
        ),
    )
    unpack(depth, signs, far_diag, mask, (even_far_ref, own_far_ref, odd_far_ref), kappa_pieces)

    def start_down(k, carry):
        ratio, value, from_end = carry
        ratio = mask / (far_diag[k] - ratio)
        here = signs[k + 1]
        value = ratio * (here + value)
        far_lower[k] = ratio
        forward[depth + k] = value
        other = depth - 1 - k
        from_end = mask / (far_diag[other] - from_end)
        upper[depth + other] = from_end
        image = far_diag[k] * here - (signs[k] + signs[k + 2]) - 0.5 * beside(here)
        far_signs[k] = here[OWN_ROWS]
        far_k_signs[k] = image[OWN_ROWS]
        return ratio, value, from_end

    start = (near_lower[depth - 1], near_forward[depth - 1], zero)
    carry = lax.fori_loop(0, depth, start_down, start, unroll=depth)

    def start_up_far(step, carry):
        k = depth - 1 - step
        solved, value = carry
        solved = forward[depth + k] + far_lower[k] * solved
        value = upper[depth + k] * (solved + value)
        backward[depth + k] = value
        return solved, value

    solved, value = lax.fori_loop(0, depth, start_up_far, (zero, zero), unroll=depth)

    def start_up_near(step, carry):
        k = depth - 1 - step
        ratio, solved, value = carry
        ratio = mask / (near_diag[k] - ratio)
        solved = near_forward[k] + near_lower[k] * solved
        value = ratio * (solved + value)
        upper[k] = ratio
        backward[k] = value
        return ratio, solved, value

    lax.fori_loop(0, depth, start_up_near, (carry[2], solved, value), unroll=depth)

    parts = (
        (0, near_diag, near_lower, lambda k: near_signs[k]),
        (depth, far_diag, far_lower, lambda k: signs[k + 1, OWN_ROWS]),
    )
    place = 0
    for index in range(ITERS):
        final = index + 1 == ITERS
        group_size = 2 * GROUP if final else GROUP

        def next_basis(k, previous, index=index):
            solved = backward[k] + upper[k] * previous
            if index == 0:
                value = solved
            elif SHIFTS[index - 1] == 0.0:
                value = solved
            elif SHIFTS[index - 1] == 1.0:
                value = basis[k] - solved
            elif SHIFTS[index - 1] == -1.0:
                value = basis[k] + solved
            else:
                value = SHIFTS[index - 1] * basis[k] - solved
            return solved, value

        solved, here = next_basis(0, zero)
        if not final:
            basis[0] = here
        carry = (solved, zero, here, zero)
        slots = list(range(place, place + index + 1)) + [len(PAIRS) + index]
        for offset, half_diag, lower, sign_of in parts:

            def down(group, carry):
                solved, above, here, value = carry
                added = [None] * len(slots)
                for step in range(group_size):
                    k = group * group_size + step
                    solved, below = next_basis(offset + k + 1, solved)
                    if not final:
                        basis[offset + k + 1] = below
                    side = beside(here)
                    image = half_diag[k] * here - (above + below) - masks[...] * side
                    if not final:
                        value = lower[k] * (beside(image) + value)
                        forward[offset + k] = value
                        sides[offset + k] = side
                    my_basis, my_image = here[OWN_ROWS], image[OWN_ROWS]
                    basis_ref[index, offset + k] = my_basis
                    image_ref[index, offset + k] = my_image
                    factors = [(image_ref[other, offset + k], my_image) for other in range(index)]
                    factors += [(my_image, my_image), (my_basis, sign_of(k))]
                    for slot, (a, b) in enumerate(factors):
                        product = a[:, :LANES] * b[:, :LANES] + a[:, LANES:] * b[:, LANES:]
                        added[slot] = product if step % GROUP == 0 else added[slot] + product
                        if step % GROUP == GROUP - 1:
                            at = (offset + group * group_size + step) // GROUP
                            sums[slots[slot], at] = added[slot]
                    above, here = here, below
                return solved, above, here, value

            carry = lax.fori_loop(0, depth // group_size, down, carry)
        place += index + 1
        if final:
            break
        carry = (zero, zero)
        for offset, half_diag, lower, sign_of in reversed(parts):

            def up(step, carry):
                k = depth - 1 - step
                solved, value = carry
                solved = forward[offset + k] + lower[k] * solved
                value = upper[offset + k] * ((sides[offset + k] + solved) + value)
                backward[offset + k] = value
                return solved, value

            carry = lax.fori_loop(0, depth, up, carry, unroll=4 * GROUP)

    ids = row_ids((ROWS, LANES))
    sides_of = [[], []]
    for block in range(SLOTS // ROWS):
        high, low = own_zero, own_zero
        for slot in range(block * ROWS, min((block + 1) * ROWS, COUNT)):
            pair = (sums[slot, 0], own_zero)
            for at in range(1, sums.shape[1]):
                total, rest = two_sum(pair[0], sums[slot, at])
                pair = (total, pair[1] + rest)
            pair = tuple(jnp.where(mine, part, 0.0) for part in pair)
            for shift in (4, 2, 1):
                pair = pair_add(pair, tuple(pltpu.roll(part, shift, 0) for part in pair))
            here = ids == slot - block * ROWS
            high, low = jnp.where(here, pair[0], high), jnp.where(here, pair[1], low)
        sides_of[0].append(high)
        sides_of[1].append(low)
    ones = jnp.ones((LANES, LANES), jnp.bfloat16)

    def lane_sum(part):
        return jnp.dot(part, ones, preferred_element_type=jnp.float32)

    high, low = (jnp.concatenate(blocks, axis=0) for blocks in sides_of)
    first, second, third = (lane_sum(part) for part in split_three(high))
    high, rest = two_sum(first, second)
    low = rest + (third + lane_sum(low.astype(jnp.bfloat16)))
    quarter = lane_ids((ROWS, LANES)) // (LANES // 4)
    tile = high[:ROWS]
    for place, block in enumerate((high[ROWS:], low[:ROWS], low[ROWS:])):
        tile = jnp.where(quarter == place + 1, block, tile)
    gram_ref[...] = tile


def terms_kernel(
    depth, basis_ref, image_ref, near_signs, near_k_signs, far_signs, far_k_signs, terms_ref
):
    level = lax.axis_index("level")
    half = LANES // 2
    mine = lane_ids((ROWS, LANES)) < half
    for offset, signs, k_signs in ((0, near_signs, near_k_signs), (depth, far_signs, far_k_signs)):

        def step(k, unused, offset=offset, signs=signs, k_signs=k_signs):
            z = offset + k
            target = jnp.where(level == 0, z, 2 * depth - 1 - z)
            sign, image = signs[k], k_signs[k]
            for index in range(ITERS):
                term = basis_ref[index, z] * image + image_ref[index, z] * sign
                terms_ref[index, target] = jnp.where(
                    mine, term[:, :LANES], pltpu.roll(term[:, LANES:], half, 1)
                )
            return unused

        if offset == 0:
            lax.fori_loop(0, depth - 1, step, 0, unroll=GROUP)
            sign, image = signs[depth - 1], k_signs[depth - 1] - far_signs[0]
            target = jnp.where(level == 0, depth - 1, depth)
            for index in range(ITERS):
                term = basis_ref[index, depth - 1] * image + image_ref[index, depth - 1] * sign
                terms_ref[index, target] = jnp.where(
                    mine, term[:, :LANES], pltpu.roll(term[:, LANES:], half, 1)
                )
        else:
            lax.fori_loop(0, depth, step, 0, unroll=GROUP)


def solve_small(high, low):
    def entry(index):
        return tuple(jnp.broadcast_to(part[index : index + 1], (ROWS, LANES)) for part in (high, low))

    gram = {}
    for place, (i, j) in enumerate(PAIRS):
        gram[i, j] = gram[j, i] = entry(place)
    right = [entry(len(PAIRS) + j) for j in range(ITERS)]
    work = {key: pair[0] for key, pair in gram.items()}
    ratios, inverses = {}, []
    for i in range(ITERS):
        pivot = work[i, i]
        good = pivot > 1e-7 * gram[i, i][0]
        inverses.append(jnp.where(good, 1.0 / jnp.where(good, pivot, 1.0), 0.0))
        for r in range(i + 1, ITERS):
            ratios[r, i] = work[r, i] * inverses[i]
        for r in range(i + 1, ITERS):
            for c in range(i + 1, r + 1):
                work[r, c] = work[c, r] = work[r, c] - ratios[r, i] * work[c, i]

    def solve(values):
        values = list(values)
        for i in range(ITERS):
            for r in range(i + 1, ITERS):
                values[r] = values[r] - ratios[r, i] * values[i]
        values = [value * inverse for value, inverse in zip(values, inverses)]
        for i in reversed(range(ITERS)):
            for r in range(i):
                values[r] = values[r] - ratios[i, r] * values[i]
        return values

    found = solve([pair[0] for pair in right])
    for unused in range(2):
        rest = []
        for i in range(ITERS):
            total = right[i]
            for j in range(ITERS):
                product, error = two_product(gram[i, j][0], found[j])
                total = pair_add(total, (-product, -(error + gram[i, j][1] * found[j])))
            rest.append(total[0] + total[1])
        found = [a + b for a, b in zip(found, solve(rest))]
    return found


def combine_kernel(depth, terms_ref, *refs):
    gram_refs, (keep_ref, send_ref) = refs[:-2], refs[-2:]
    half, width = LANES // 2, LANES // 4
    pairs = []
    for ref in gram_refs:
        for start in range(0, ref.shape[0], ROWS):
            tile = ref[start : start + ROWS]
            pairs.append((tile, pltpu.roll(tile, half, 1)))
    while len(pairs) > 1:
        merged = [pair_add(pairs[i], pairs[i + 1]) for i in range(0, len(pairs) - 1, 2)]
        pairs = merged + pairs[2 * len(merged) :]
    lanes = lane_ids((ROWS, LANES))

    def spread(part, block):
        part = jnp.where(lanes // width == block, part, 0.0)
        part = part + pltpu.roll(part, width, 1)
        return part + pltpu.roll(part, half, 1)

    found = solve_small(
        *(jnp.concatenate([spread(part, 0), spread(part, 1)], axis=0) for part in pairs[0])
    )
    core = lax.rem(lax.axis_index("probe"), 2)
    first_lanes = lanes % half < width
    pairs_deep = depth // 2

    def step(z, unused):
        for which in range(2):
            def total(k):
                value = found[0] * terms_ref[0, k]
                for j in range(1, ITERS):
                    value = value + found[j] * terms_ref[j, k]
                return value

            one = total(which * depth + z)
            two = total(which * depth + pairs_deep + z)
            low = jnp.where(first_lanes, one, pltpu.roll(two, width, 1))
            high = jnp.where(first_lanes, pltpu.roll(one, LANES - width, 1), two)
            keep_ref[which, z] = jnp.where(core == 0, low, high)
            send_ref[which, z] = jnp.where(core == 0, high, low)
        return unused

    lax.fori_loop(0, pairs_deep, step, 0, unroll=GROUP)


def observed_kernel(
    depth, probes, kappa_ref, observed_ref, even_ref, odd_ref, far_ref, factor_ref, data_ref
):
    level = lax.axis_index("level")
    tile = lax.axis_index("tile")
    last_tile = lax.axis_size("tile") - 1
    probe = lax.axis_index("probe")
    in_low = probe < probes // 2
    even = lax.rem(probe, 2) == 0
    width = LANES // 2
    lanes = lane_ids((ROWS, 2 * LANES))
    ids = row_ids((ROWS, LANES))
    base = even_ref.shape[0] - depth // ROWS
    from_even = lax.rem(tile, 2) == 1

    def half(value):
        return jnp.where(in_low, value[..., :LANES], value[..., LANES:])

    def take(value):
        return jnp.where(even, value, pltpu.roll(value, width, 1))

    far_edge = far_ref[far_ref.shape[0] - 1]
    factors, parts = [], []
    for z in range(depth):
        value = observed_ref[z]
        mine = half(value)
        y_sides = jnp.where(lanes > 0, pltpu.roll(value, 1, 1), 0.0) + jnp.where(
            lanes < 2 * LANES - 1, pltpu.roll(value, 2 * LANES - 1, 1), 0.0
        )
        first = even_ref[base + z // ROWS, z % ROWS : z % ROWS + 1, :]
        second = odd_ref[base + z // ROWS, z % ROWS : z % ROWS + 1, :]
        left, right = jnp.where(from_even, first, second), jnp.where(from_even, second, first)
        before = jnp.where(ids > 0, pltpu.roll(mine, 1, 0), jnp.where(tile > 0, left, 0.0))
        after = jnp.where(
            ids < ROWS - 1, pltpu.roll(mine, ROWS - 1, 0), jnp.where(tile < last_tile, right, 0.0)
        )
        above = half(observed_ref[z - 1]) if z > 0 else jnp.where(level > 0, far_edge, 0.0)
        below = half(observed_ref[z + 1]) if z < depth - 1 else jnp.where(level == 0, far_edge, 0.0)
        kappa = half(kappa_ref[z])
        k_observed = (
            (kappa + (4.0 + 2.0 * VERTICAL)) * mine
            - (before + after)
            - half(y_sides)
            - VERTICAL * (above + below)
        )
        factors.append(take(kappa * (0.5 / probes)))
        parts.append(take(kappa * (2.0 * mine * k_observed)))
    first_lanes = lane_ids((ROWS, LANES)) < width
    for ref, values in ((factor_ref, factors), (data_ref, parts)):
        for z in range(depth // 2):
            ref[z] = jnp.where(first_lanes, values[z], pltpu.roll(values[depth // 2 + z], width, 1))


def gradient_kernel(
    depth, trace_b_ref, trace_a_ref, straight_ref, factor_ref, data_ref, out_ref
):
    width = LANES // 2
    square = (LANES, LANES)
    lane = lane_ids(square)
    source = (width // 2) * (lane // width) + (lane % width) // 2 + width * (lane % 2)
    chosen = jnp.where(row_ids(square) == source, 1.0, 0.0).astype(jnp.bfloat16)
    stays = lax.axis_index("level") == 0
    traces = trace_a_ref[...] + jnp.where(stays, straight_ref[...], trace_b_ref[...])
    traces = pick(traces.reshape(-1, LANES), chosen).reshape(traces.shape)
    values = factor_ref[...] * traces - data_ref[...]
    for z in range(depth // 2):
        out_ref[z] = values[z, :, :width]
        out_ref[depth // 2 + z] = pltpu.roll(values[z], width, 1)[:, :width]


def whole(count):
    return [pl.BlockSpec(memory_space=pltpu.VMEM)] * count


def body(probe_bits, kappa_sq, observed):
    probes, tile_count = lax.axis_size("probe"), lax.axis_size("tile")
    unused, depth, rows, columns = probe_bits.shape
    assert probe_bits.shape[0] == 1 and lax.axis_size("level") == 2 and probes == 4
    assert rows == ROWS and columns == 2 * LANES and depth % (2 * LANES // EDGE) == 0
    params = pltpu.CompilerParams(vmem_limit_bytes=24 * 1024 * 1024)
    f32 = jnp.float32
    tiles = depth * EDGE // LANES
    field = depth + tiles
    sent = field + field // 2
    own_shape = jax.ShapeDtypeStruct((2 * field, ROWS, LANES), f32)
    near_shape = jax.ShapeDtypeStruct((sent + depth // ROWS, ROWS, LANES), f32)
    far_shape = jax.ShapeDtypeStruct((sent + 1, ROWS, LANES), f32)

    own_block, even_block, odd_block, cross_block = pl.pallas_call(
        functools.partial(pack_kernel, depth),
        out_shape=(own_shape, near_shape, near_shape, far_shape),
        in_specs=[pl.BlockSpec(memory_space=pltpu.HBM)] * 3,
        out_specs=tuple(whole(4)),
        scratch_shapes=[
            pltpu.VMEM((depth, rows, columns), jnp.int32),
            pltpu.VMEM((depth, rows, columns), f32),
            pltpu.VMEM((depth, rows, columns), f32),
            pltpu.SemaphoreType.DMA((3,)),
        ],
        compiler_params=params,
        name="pack",
    )(
        *(
            pltpu.with_memory_space_constraint(value, pltpu.HBM)
            for value in (probe_bits[0], kappa_sq, observed)
        )
    )

    def swaps(pairs):
        return [way for a, b in pairs for way in ((a, b), (b, a))]

    even_pairs = [(i, i + 1) for i in range(0, tile_count - 1, 2)]
    odd_pairs = [(i, i + 1) for i in range(1, tile_count - 1, 2)]
    own_far = lax.ppermute(cross_block, "level", swaps([(0, 1)]))
    even = lax.ppermute(even_block, "tile", swaps(even_pairs))
    odd = lax.ppermute(odd_block, "tile", swaps(odd_pairs))
    odd_far = lax.ppermute(own_far, "tile", swaps(odd_pairs))
    even_far = lax.ppermute(
        cross_block,
        ("tile", "level"),
        swaps([(2 * a + level, 2 * b + 1 - level) for a, b in even_pairs for level in range(2)]),
    )

    quarter = jax.ShapeDtypeStruct((depth, ROWS, columns // probes), f32)
    paired = jax.ShapeDtypeStruct((depth // 2, ROWS, LANES), f32)
    factor, data = pl.pallas_call(
        functools.partial(observed_kernel, depth, probes),
        out_shape=(paired, paired),
        in_specs=whole(5),
        out_specs=tuple(whole(2)),
        compiler_params=params,
        name="observed",
    )(kappa_sq, observed, even, odd, own_far)

    def core_swap(*pieces):
        kappa = jnp.concatenate([piece[field:sent] for piece in pieces], axis=0)
        return lax.ppermute(kappa, "probe", swaps([(0, 1), (2, 3)]))

    swapped = core_swap(even, odd, own_far)
    levels = 2 * depth
    part = jax.ShapeDtypeStruct((depth, 3 * ROWS, 2 * LANES), f32)
    own_part = jax.ShapeDtypeStruct((depth, ROWS, 2 * LANES), f32)
    near_diag, near_lower, near_forward, near_signs, near_k_signs = pl.pallas_call(
        functools.partial(near_kernel, depth),
        out_shape=(part, part, part, own_part, own_part),
        in_specs=whole(4),
        out_specs=tuple(whole(5)),
        scratch_shapes=[pltpu.VMEM((depth + 2, 3 * ROWS, 2 * LANES), f32)],
        compiler_params=params,
        name="near",
    )(own_block, even, odd, swapped)

    swapped_far = core_swap(even_far, odd_far)
    padded = pltpu.VMEM((levels + 1, 3 * ROWS, 2 * LANES), f32)
    plain = pltpu.VMEM((levels, 3 * ROWS, 2 * LANES), f32)
    short = pltpu.VMEM((depth, 3 * ROWS, 2 * LANES), f32)
    fields = jax.ShapeDtypeStruct((ITERS, levels, ROWS, 2 * LANES), f32)
    basis, images, far_signs, far_k_signs, gram = pl.pallas_call(
        functools.partial(basis_kernel, depth),
        out_shape=(
            fields,
            fields,
            own_part,
            own_part,
            jax.ShapeDtypeStruct((ROWS, LANES), f32),
        ),
        in_specs=whole(9),
        out_specs=tuple(whole(5)),
        scratch_shapes=[
            pltpu.VMEM((depth + 2, 3 * ROWS, 2 * LANES), f32),
            short,
            short,
            padded,
            padded,
            plain,
            plain,
            padded,
            pltpu.VMEM((SLOTS, levels // GROUP, ROWS, LANES), f32),
            pltpu.VMEM((3 * ROWS, 2 * LANES), f32),
        ],
        compiler_params=params,
        name="basis",
    )(
        near_diag,
        near_lower,
        near_forward,
        near_signs,
        own_far,
        even_far,
        odd_far,
        swapped,
        swapped_far,
    )
    terms = pl.pallas_call(
        functools.partial(terms_kernel, depth),
        out_shape=jax.ShapeDtypeStruct((ITERS, levels, ROWS, LANES), f32),
        in_specs=whole(6),
        out_specs=pl.BlockSpec(memory_space=pltpu.VMEM),
        compiler_params=params,
        name="terms",
    )(basis, images, near_signs, near_k_signs, far_signs, far_k_signs)

    if tile_count in (2, 4):
        group = [gram] + [
            lax.ppermute(
                gram,
                ("tile", "level"),
                swaps([(i, i ^ k) for i in range(2 * tile_count) if i < i ^ k]),
            )
            for k in (1, 2, 3)
        ]
        partials = [jnp.concatenate(group, axis=0)]
        if tile_count == 4:
            partials.append(lax.ppermute(partials[0], "tile", swaps([(0, 2), (1, 3)])))
    else:
        partials = [lax.all_gather(gram, ("tile", "level"), axis=0, tiled=True)]
    piece = jax.ShapeDtypeStruct((2, depth // 2, ROWS, LANES), f32)
    keep, send = pl.pallas_call(
        functools.partial(combine_kernel, depth),
        out_shape=(piece, piece),
        in_specs=whole(1 + len(partials)),
        out_specs=tuple(whole(2)),
        compiler_params=params,
        name="combine",
    )(terms, *partials)

    summed = keep + lax.ppermute(send, "probe", swaps([(0, 1), (2, 3)]))
    level = lax.axis_index("level")
    turned = lax.dynamic_index_in_dim(summed, 1 - level, 0, keepdims=False)
    straight = lax.dynamic_index_in_dim(summed, level, 0, keepdims=False)

    def device(x, core, level):
        return (2 * x + core) * 2 + level

    chips = [(x, core) for x in range(2) for core in range(2)]
    trace_a = lax.ppermute(
        turned,
        ("probe", "level"),
        [(device(x, core, 0), device(x, core, 1)) for x, core in chips]
        + [(device(x, core, 1), device(1 - x, core, 0)) for x, core in chips],
    )
    trace_b = lax.ppermute(
        straight,
        ("probe", "level"),
        [(device(x, core, 1), device(1 - x, core, 1)) for x, core in chips],
    )
    return pl.pallas_call(
        functools.partial(gradient_kernel, depth),
        out_shape=quarter,
        in_specs=whole(5),
        out_specs=pl.BlockSpec(memory_space=pltpu.VMEM),
        compiler_params=params,
        name="gradient",
    )(trace_b, trace_a, straight, factor, data)


def solution(mesh):
    in_specs = (
        P("probe", "level", "tile", None),
        P("level", "tile", None),
        P("level", "tile", None),
    )
    out_specs = P("level", "tile", "probe")
    return jax.shard_map(body, mesh=mesh, in_specs=in_specs, out_specs=out_specs, check_vma=False)
```

```python
import functools

import jax
import jax.numpy as jnp
from jax import lax
from jax.experimental import pallas as pl
from jax.experimental.pallas import tpu as pltpu
from jax.sharding import PartitionSpec as P

ITERS = 4
VERTICAL = 2.0
LANES = 128
ROWS = 8
EDGE = 8
GROUP = 8
SHIFTS = (1.0, -1.0, 0.0)
PAIRS = [(i, j) for j in range(ITERS) for i in range(j + 1)]
COUNT = len(PAIRS) + ITERS
SLOTS = 16


def two_sum(a, b):
    total = a + b
    part = total - a
    return total, (a - (total - part)) + (b - part)


def two_product(a, b):
    def split(v):
        big = v * 4097.0
        high = big - (big - v)
        return high, v - high

    product = a * b
    a_high, a_low = split(a)
    b_high, b_low = split(b)
    return product, ((a_high * b_high - product) + a_high * b_low + a_low * b_high) + a_low * b_low


def pair_add(first, second):
    total, rest = two_sum(first[0], second[0])
    rest = rest + (first[1] + second[1])
    high = total + rest
    return high, rest - (high - total)


def lane_ids(shape):
    return lax.broadcasted_iota(jnp.int32, shape, len(shape) - 1)


def row_ids(shape):
    return lax.broadcasted_iota(jnp.int32, shape, len(shape) - 2)


def split_three(values):
    high = values.astype(jnp.bfloat16)
    rest = values - high.astype(jnp.float32)
    middle = rest.astype(jnp.bfloat16)
    low = (rest - middle.astype(jnp.float32)).astype(jnp.bfloat16)
    return high, middle, low


def pick(values, chosen):
    high, middle, low = (
        jnp.dot(part, chosen, preferred_element_type=jnp.float32) for part in split_three(values)
    )
    return high + (middle + low)


def y_half():
    return lax.rem(lax.axis_index("level") + lax.axis_index("probe") // 2, 2)


def columns_of(half):
    shape = (2 * LANES, 2 * LANES)
    ids, lane = row_ids(shape), lane_ids(shape)
    odd = (lane // (LANES // 2)) % 2
    main = LANES * half + 2 * (lane % (LANES // 2)) + odd
    edge = LANES - EDGE * half + 2 * (lane % (EDGE // 2)) + odd
    wanted = jnp.where(lane < LANES, main, edge)
    return jnp.where(ids == wanted, 1.0, 0.0).astype(jnp.bfloat16)


def pack_kernel(
    depth,
    bits_hbm,
    kappa_hbm,
    observed_hbm,
    own_ref,
    even_ref,
    odd_ref,
    cross_ref,
    bits_ref,
    kappa_ref,
    observed_ref,
    arrived,
):
    copies = [
        pltpu.make_async_copy(source, target, arrived.at[place])
        for place, (source, target) in enumerate(
            ((bits_hbm, bits_ref), (kappa_hbm, kappa_ref), (observed_hbm, observed_ref))
        )
    ]
    for copy in copies:
        copy.start()
    level = lax.axis_index("level")
    first = level == 0
    in_first_core = lax.rem(lax.axis_index("probe"), 2) == 0
    per_tile = LANES // EDGE
    tiles = depth // per_tile
    field = depth + tiles
    slot_ids = (lane_ids((ROWS, LANES)) % (LANES // 2)) // (EDGE // 2)
    same_columns, cross_columns = columns_of(y_half()), columns_of(1 - y_half())

    def blocks(picked):
        picked = picked.reshape(depth, ROWS, 2 * LANES)
        edges = []
        for tile in range(tiles):
            packed = picked[tile * per_tile, :, LANES:]
            for slot in range(1, per_tile):
                packed = jnp.where(slot_ids == slot, picked[tile * per_tile + slot, :, LANES:], packed)
            edges.append(packed)
        return [picked[z, :, :LANES] for z in range(depth)], edges

    def write(refs, base, values):
        for place, value in enumerate(values):
            for ref in refs:
                ref[base + place] = value

    copies[0].wait()
    signs = (2 * bits_ref[...] - 1).astype(jnp.float32).reshape(depth * ROWS, 2 * LANES)
    signs = signs.astype(jnp.bfloat16)
    for refs, chosen in (((own_ref, even_ref, odd_ref), same_columns), ((cross_ref,), cross_columns)):
        main, edges = blocks(jnp.dot(signs, chosen, preferred_element_type=jnp.float32))
        write(refs, 0, main + edges)
    copies[1].wait()
    kappa = kappa_ref[...].reshape(depth * ROWS, 2 * LANES)
    for refs, chosen in (((even_ref, odd_ref), same_columns), ((cross_ref,), cross_columns)):
        main, edges = blocks(pick(kappa, chosen))
        if len(refs) == 2:
            write((own_ref,), field, main + edges)
        low = main[: depth // 2] + edges[: tiles // 2]
        high = main[depth // 2 :] + edges[tiles // 2 :]
        write(refs, field, [jnp.where(in_first_core, a, b) for a, b in zip(low, high)])
    copies[2].wait()
    base = field + field // 2
    in_low = lax.axis_index("probe") < lax.axis_size("probe") // 2

    def half(value):
        return jnp.where(in_low, value[..., :LANES], value[..., LANES:])

    top = half(observed_ref[:, ROWS - 1, :])
    bottom = half(observed_ref[:, 0, :])
    goes_up = lax.rem(lax.axis_index("tile"), 2) == 0
    for tile in range(depth // ROWS):
        here = slice(tile * ROWS, (tile + 1) * ROWS)
        even_ref[base + tile] = jnp.where(goes_up, top[here], bottom[here])
        odd_ref[base + tile] = jnp.where(goes_up, bottom[here], top[here])
    cross_ref[base] = jnp.where(first, half(observed_ref[depth - 1]), half(observed_ref[0]))


def beside(values):
    rows = values.shape[0]
    even, odd = values[:, :LANES], values[:, LANES:]
    y_sides = jnp.concatenate(
        [odd + pltpu.roll(odd, 1, 1), even + pltpu.roll(even, LANES - 1, 1)], axis=1
    )
    return (pltpu.roll(values, 1, 0) + pltpu.roll(values, rows - 1, 0)) + y_sides


def inside_mask():
    shape = (3 * ROWS, 2 * LANES)
    tile = lax.axis_index("tile")
    half = LANES // 2
    lanes, ids = lane_ids(shape) % LANES, row_ids(shape)
    near = jnp.where(y_half() == 0, half, LANES - EDGE // 2)
    inside = (lanes < half) | ((lanes >= near) & (lanes < near + EDGE // 2))
    inside = inside & (ids >= jnp.where(tile > 0, 0, ROWS))
    inside = inside & (ids < jnp.where(tile < lax.axis_size("tile") - 1, 3 * ROWS, 2 * ROWS))
    return jnp.where(inside, 1.0, 0.0)


def join(z, even, own, odd):
    half, short = LANES // 2, EDGE // 2
    from_even = lax.rem(lax.axis_index("tile"), 2) == 1
    mine = lane_ids((ROWS, LANES)) < half
    shift = half + (half - short) * y_half() - short * lax.rem(z, LANES // EDGE)
    shift = lax.rem(shift + LANES, LANES)
    left = [jnp.where(from_even, a, b) for a, b in zip(even, odd)]
    right = [jnp.where(from_even, b, a) for a, b in zip(even, odd)]
    evens, odds = [], []
    for main, edge in (left, own, right):
        edge = pltpu.roll(edge, shift, 1)
        evens.append(jnp.where(mine, main, edge))
        odds.append(pltpu.roll(jnp.where(mine, edge, main), half, 1))
    return jnp.concatenate([jnp.concatenate(evens, axis=0), jnp.concatenate(odds, axis=0)], axis=1)


def unpack(depth, signs, half_diag, mask, sign_pieces, kappa_pieces):
    level = lax.axis_index("level")
    per_tile = LANES // EDGE

    def place(z):
        return jnp.where(level == 0, z, depth - 1 - z)

    def sign_level(z, unused):
        pieces = [(ref[z], ref[depth + z // per_tile]) for ref in sign_pieces]
        signs[place(z) + 1] = join(z, *pieces) * mask
        return unused

    lax.fori_loop(0, depth, sign_level, 0, unroll=per_tile)
    core = lax.rem(lax.axis_index("probe"), 2)
    for start, pieces in zip((core, 1 - core), kappa_pieces):
        start = start * (depth // 2)

        def kappa_level(step, unused, start=start, pieces=pieces):
            z = start + step
            tiles = []
            for ref, base, whole_field in pieces:
                if whole_field:
                    tiles.append((ref[base + z], ref[base + depth + z // per_tile]))
                else:
                    tiles.append((ref[base + step], ref[base + depth // 2 + step // per_tile]))
            half_diag[place(z)] = 0.5 * join(z, *tiles) + (2.0 + VERTICAL)
            return unused

        lax.fori_loop(0, depth // 2, kappa_level, 0, unroll=per_tile)


OWN_ROWS = slice(ROWS, 2 * ROWS)


def near_kernel(
    depth,
    own_ref,
    even_ref,
    odd_ref,
    swapped_ref,
    half_diag,
    lower,
    forward,
    own_signs,
    k_signs,
    signs,
):
    field = own_ref.shape[0] // 2
    mask = inside_mask()
    zero = jnp.zeros(mask.shape, jnp.float32)
    signs[0] = zero
    signs[depth + 1] = zero
    kappa_pieces = (
        ((even_ref, field, False), (own_ref, field, True), (odd_ref, field, False)),
        ((swapped_ref, 0, False), (own_ref, field, True), (swapped_ref, field // 2, False)),
    )
    unpack(depth, signs, half_diag, mask, (even_ref, own_ref, odd_ref), kappa_pieces)

    def down(k, carry):
        ratio, value = carry
        ratio = mask / (half_diag[k] - ratio)
        here = signs[k + 1]
        value = ratio * (here + value)
        lower[k] = ratio
        forward[k] = value
        image = half_diag[k] * here - (signs[k] + signs[k + 2]) - 0.5 * beside(here)
        own_signs[k] = here[OWN_ROWS]
        k_signs[k] = image[OWN_ROWS]
        return ratio, value

    lax.fori_loop(0, depth, down, (zero, zero), unroll=GROUP)


def basis_kernel(
    depth,
    near_diag,
    near_lower,
    near_forward,
    near_signs,
    own_far_ref,
    even_far_ref,
    odd_far_ref,
    swapped_ref,
    swapped_far_ref,
    basis_ref,
    image_ref,
    far_signs,
    far_k_signs,
    gram_ref,
    signs,
    far_diag,
    far_lower,
    upper,
    basis,
    forward,
    sides,
    backward,
    sums,
    masks,
):
    levels = 2 * depth
    mask = inside_mask()
    half_mask = 0.5 * mask
    masks[...] = half_mask
    zero = jnp.zeros(mask.shape, jnp.float32)
    own_zero = jnp.zeros((ROWS, LANES), jnp.float32)
    mine = lane_ids((ROWS, LANES)) < LANES // 2
    field = swapped_ref.shape[0] // 3 * 2
    signs[0] = zero
    signs[0, OWN_ROWS] = near_signs[depth - 1]
    signs[depth + 1] = zero
    backward[levels] = zero
    upper[levels] = zero
    basis[levels] = zero
    kappa_pieces = (
        tuple((ref, field, False) for ref in (even_far_ref, own_far_ref, odd_far_ref)),
        (
            (swapped_far_ref, 0, False),
            (swapped_ref, field, False),
            (swapped_far_ref, field // 2, False),
        ),
    )
    unpack(depth, signs, far_diag, mask, (even_far_ref, own_far_ref, odd_far_ref), kappa_pieces)

    def start_down(k, carry):
        ratio, value, from_end = carry
        ratio = mask / (far_diag[k] - ratio)
        here = signs[k + 1]
        value = ratio * (here + value)
        far_lower[k] = ratio
        forward[depth + k] = value
        other = depth - 1 - k
        from_end = mask / (far_diag[other] - from_end)
        upper[depth + other] = from_end
        image = far_diag[k] * here - (signs[k] + signs[k + 2]) - 0.5 * beside(here)
        far_signs[k] = here[OWN_ROWS]
        far_k_signs[k] = image[OWN_ROWS]
        return ratio, value, from_end

    start = (near_lower[depth - 1], near_forward[depth - 1], zero)
    carry = lax.fori_loop(0, depth, start_down, start, unroll=depth)

    def start_up_far(step, carry):
        k = depth - 1 - step
        solved, value = carry
        solved = forward[depth + k] + far_lower[k] * solved
        value = upper[depth + k] * (solved + value)
        backward[depth + k] = value
        return solved, value

    solved, value = lax.fori_loop(0, depth, start_up_far, (zero, zero), unroll=depth)

    def start_up_near(step, carry):
        k = depth - 1 - step
        ratio, solved, value = carry
        ratio = mask / (near_diag[k] - ratio)
        solved = near_forward[k] + near_lower[k] * solved
        value = ratio * (solved + value)
        upper[k] = ratio
        backward[k] = value
        return ratio, solved, value

    lax.fori_loop(0, depth, start_up_near, (carry[2], solved, value), unroll=depth)

    parts = (
        (0, near_diag, near_lower, lambda k: near_signs[k]),
        (depth, far_diag, far_lower, lambda k: signs[k + 1, OWN_ROWS]),
    )
    place = 0
    for index in range(ITERS):
        final = index + 1 == ITERS
        group_size = 2 * GROUP if final else GROUP

        def next_basis(k, previous, index=index):
            solved = backward[k] + upper[k] * previous
            if index == 0:
                value = solved
            elif SHIFTS[index - 1] == 0.0:
                value = solved
            elif SHIFTS[index - 1] == 1.0:
                value = basis[k] - solved
            elif SHIFTS[index - 1] == -1.0:
                value = basis[k] + solved
            else:
                value = SHIFTS[index - 1] * basis[k] - solved
            return solved, value

        solved, here = next_basis(0, zero)
        if not final:
            basis[0] = here
        carry = (solved, zero, here, zero)
        slots = list(range(place, place + index + 1)) + [len(PAIRS) + index]
        for offset, half_diag, lower, sign_of in parts:

            def down(group, carry):
                solved, above, here, value = carry
                added = [None] * len(slots)
                for step in range(group_size):
                    k = group * group_size + step
                    solved, below = next_basis(offset + k + 1, solved)
                    if not final:
                        basis[offset + k + 1] = below
                    side = beside(here)
                    image = half_diag[k] * here - (above + below) - masks[...] * side
                    if not final:
                        value = lower[k] * (beside(image) + value)
                        forward[offset + k] = value
                        sides[offset + k] = side
                    my_basis, my_image = here[OWN_ROWS], image[OWN_ROWS]
                    basis_ref[index, offset + k] = my_basis
                    image_ref[index, offset + k] = my_image
                    factors = [(image_ref[other, offset + k], my_image) for other in range(index)]
                    factors += [(my_image, my_image), (my_basis, sign_of(k))]
                    for slot, (a, b) in enumerate(factors):
                        product = a[:, :LANES] * b[:, :LANES] + a[:, LANES:] * b[:, LANES:]
                        added[slot] = product if step % GROUP == 0 else added[slot] + product
                        if step % GROUP == GROUP - 1:
                            at = (offset + group * group_size + step) // GROUP
                            sums[slots[slot], at] = added[slot]
                    above, here = here, below
                return solved, above, here, value

            carry = lax.fori_loop(0, depth // group_size, down, carry)
        place += index + 1
        if final:
            break
        carry = (zero, zero)
        for offset, half_diag, lower, sign_of in reversed(parts):

            def up(step, carry):
                k = depth - 1 - step
                solved, value = carry
                solved = forward[offset + k] + lower[k] * solved
                value = upper[offset + k] * ((sides[offset + k] + solved) + value)
                backward[offset + k] = value
                return solved, value

            carry = lax.fori_loop(0, depth, up, carry, unroll=4 * GROUP)

    ids = row_ids((ROWS, LANES))
    sides_of = [[], []]
    for block in range(SLOTS // ROWS):
        high, low = own_zero, own_zero
        for slot in range(block * ROWS, min((block + 1) * ROWS, COUNT)):
            pair = (sums[slot, 0], own_zero)
            for at in range(1, sums.shape[1]):
                total, rest = two_sum(pair[0], sums[slot, at])
                pair = (total, pair[1] + rest)
            pair = tuple(jnp.where(mine, part, 0.0) for part in pair)
            for shift in (4, 2, 1):
                pair = pair_add(pair, tuple(pltpu.roll(part, shift, 0) for part in pair))
            here = ids == slot - block * ROWS
            high, low = jnp.where(here, pair[0], high), jnp.where(here, pair[1], low)
        sides_of[0].append(high)
        sides_of[1].append(low)
    ones = jnp.ones((LANES, LANES), jnp.bfloat16)

    def lane_sum(part):
        return jnp.dot(part, ones, preferred_element_type=jnp.float32)

    high, low = (jnp.concatenate(blocks, axis=0) for blocks in sides_of)
    first, second, third = (lane_sum(part) for part in split_three(high))
    high, rest = two_sum(first, second)
    low = rest + (third + lane_sum(low.astype(jnp.bfloat16)))
    quarter = lane_ids((ROWS, LANES)) // (LANES // 4)
    tile = high[:ROWS]
    for place, block in enumerate((high[ROWS:], low[:ROWS], low[ROWS:])):
        tile = jnp.where(quarter == place + 1, block, tile)
    gram_ref[...] = tile


def terms_kernel(
    depth, basis_ref, image_ref, near_signs, near_k_signs, far_signs, far_k_signs, terms_ref
):
    level = lax.axis_index("level")
    half = LANES // 2
    mine = lane_ids((ROWS, LANES)) < half
    for offset, signs, k_signs in ((0, near_signs, near_k_signs), (depth, far_signs, far_k_signs)):

        def step(k, unused, offset=offset, signs=signs, k_signs=k_signs):
            z = offset + k
            target = jnp.where(level == 0, z, 2 * depth - 1 - z)
            sign, image = signs[k], k_signs[k]
            for index in range(ITERS):
                term = basis_ref[index, z] * image + image_ref[index, z] * sign
                terms_ref[index, target] = jnp.where(
                    mine, term[:, :LANES], pltpu.roll(term[:, LANES:], half, 1)
                )
            return unused

        if offset == 0:
            lax.fori_loop(0, depth - 1, step, 0, unroll=GROUP)
            sign, image = signs[depth - 1], k_signs[depth - 1] - far_signs[0]
            target = jnp.where(level == 0, depth - 1, depth)
            for index in range(ITERS):
                term = basis_ref[index, depth - 1] * image + image_ref[index, depth - 1] * sign
                terms_ref[index, target] = jnp.where(
                    mine, term[:, :LANES], pltpu.roll(term[:, LANES:], half, 1)
                )
        else:
            lax.fori_loop(0, depth, step, 0, unroll=GROUP)


def solve_small(high, low):
    def entry(index):
        return tuple(jnp.broadcast_to(part[index : index + 1], (ROWS, LANES)) for part in (high, low))

    gram = {}
    for place, (i, j) in enumerate(PAIRS):
        gram[i, j] = gram[j, i] = entry(place)
    right = [entry(len(PAIRS) + j) for j in range(ITERS)]
    work = {key: pair[0] for key, pair in gram.items()}
    ratios, inverses = {}, []
    for i in range(ITERS):
        pivot = work[i, i]
        good = pivot > 1e-7 * gram[i, i][0]
        inverses.append(jnp.where(good, 1.0 / jnp.where(good, pivot, 1.0), 0.0))
        for r in range(i + 1, ITERS):
            ratios[r, i] = work[r, i] * inverses[i]
        for r in range(i + 1, ITERS):
            for c in range(i + 1, r + 1):
                work[r, c] = work[c, r] = work[r, c] - ratios[r, i] * work[c, i]

    def solve(values):
        values = list(values)
        for i in range(ITERS):
            for r in range(i + 1, ITERS):
                values[r] = values[r] - ratios[r, i] * values[i]
        values = [value * inverse for value, inverse in zip(values, inverses)]
        for i in reversed(range(ITERS)):
            for r in range(i):
                values[r] = values[r] - ratios[i, r] * values[i]
        return values

    found = solve([pair[0] for pair in right])
    for unused in range(2):
        rest = []
        for i in range(ITERS):
            total = right[i]
            for j in range(ITERS):
                product, error = two_product(gram[i, j][0], found[j])
                total = pair_add(total, (-product, -(error + gram[i, j][1] * found[j])))
            rest.append(total[0] + total[1])
        found = [a + b for a, b in zip(found, solve(rest))]
    return found


def combine_kernel(depth, terms_ref, *refs):
    gram_refs, (keep_ref, send_ref) = refs[:-2], refs[-2:]
    half, width = LANES // 2, LANES // 4
    pairs = []
    for ref in gram_refs:
        for start in range(0, ref.shape[0], ROWS):
            tile = ref[start : start + ROWS]
            pairs.append((tile, pltpu.roll(tile, half, 1)))
    while len(pairs) > 1:
        merged = [pair_add(pairs[i], pairs[i + 1]) for i in range(0, len(pairs) - 1, 2)]
        pairs = merged + pairs[2 * len(merged) :]
    lanes = lane_ids((ROWS, LANES))

    def spread(part, block):
        part = jnp.where(lanes // width == block, part, 0.0)
        part = part + pltpu.roll(part, width, 1)
        return part + pltpu.roll(part, half, 1)

    found = solve_small(
        *(jnp.concatenate([spread(part, 0), spread(part, 1)], axis=0) for part in pairs[0])
    )
    core = lax.rem(lax.axis_index("probe"), 2)
    first_lanes = lanes % half < width
    pairs_deep = depth // 2

    def step(z, unused):
        for which in range(2):
            def total(k):
                value = found[0] * terms_ref[0, k]
                for j in range(1, ITERS):
                    value = value + found[j] * terms_ref[j, k]
                return value

            one = total(which * depth + z)
            two = total(which * depth + pairs_deep + z)
            low = jnp.where(first_lanes, one, pltpu.roll(two, width, 1))
            high = jnp.where(first_lanes, pltpu.roll(one, LANES - width, 1), two)
            keep_ref[which, z] = jnp.where(core == 0, low, high)
            send_ref[which, z] = jnp.where(core == 0, high, low)
        return unused

    lax.fori_loop(0, pairs_deep, step, 0, unroll=GROUP)


def observed_kernel(
    depth, probes, kappa_ref, observed_ref, even_ref, odd_ref, far_ref, factor_ref, data_ref
):
    level = lax.axis_index("level")
    tile = lax.axis_index("tile")
    last_tile = lax.axis_size("tile") - 1
    probe = lax.axis_index("probe")
    in_low = probe < probes // 2
    even = lax.rem(probe, 2) == 0
    width = LANES // 2
    lanes = lane_ids((ROWS, 2 * LANES))
    ids = row_ids((ROWS, LANES))
    base = even_ref.shape[0] - depth // ROWS
    from_even = lax.rem(tile, 2) == 1

    def half(value):
        return jnp.where(in_low, value[..., :LANES], value[..., LANES:])

    def take(value):
        return jnp.where(even, value, pltpu.roll(value, width, 1))

    far_edge = far_ref[far_ref.shape[0] - 1]
    factors, parts = [], []
    for z in range(depth):
        value = observed_ref[z]
        mine = half(value)
        y_sides = jnp.where(lanes > 0, pltpu.roll(value, 1, 1), 0.0) + jnp.where(
            lanes < 2 * LANES - 1, pltpu.roll(value, 2 * LANES - 1, 1), 0.0
        )
        first = even_ref[base + z // ROWS, z % ROWS : z % ROWS + 1, :]
        second = odd_ref[base + z // ROWS, z % ROWS : z % ROWS + 1, :]
        left, right = jnp.where(from_even, first, second), jnp.where(from_even, second, first)
        before = jnp.where(ids > 0, pltpu.roll(mine, 1, 0), jnp.where(tile > 0, left, 0.0))
        after = jnp.where(
            ids < ROWS - 1, pltpu.roll(mine, ROWS - 1, 0), jnp.where(tile < last_tile, right, 0.0)
        )
        above = half(observed_ref[z - 1]) if z > 0 else jnp.where(level > 0, far_edge, 0.0)
        below = half(observed_ref[z + 1]) if z < depth - 1 else jnp.where(level == 0, far_edge, 0.0)
        kappa = half(kappa_ref[z])
        k_observed = (
            (kappa + (4.0 + 2.0 * VERTICAL)) * mine
            - (before + after)
            - half(y_sides)
            - VERTICAL * (above + below)
        )
        factors.append(take(kappa * (0.5 / probes)))
        parts.append(take(kappa * (2.0 * mine * k_observed)))
    first_lanes = lane_ids((ROWS, LANES)) < width
    for ref, values in ((factor_ref, factors), (data_ref, parts)):
        for z in range(depth // 2):
            ref[z] = jnp.where(first_lanes, values[z], pltpu.roll(values[depth // 2 + z], width, 1))


def gradient_kernel(
    depth, trace_b_ref, trace_a_ref, straight_ref, factor_ref, data_ref, out_ref
):
    width = LANES // 2
    square = (LANES, LANES)
    lane = lane_ids(square)
    source = (width // 2) * (lane // width) + (lane % width) // 2 + width * (lane % 2)
    chosen = jnp.where(row_ids(square) == source, 1.0, 0.0).astype(jnp.bfloat16)
    stays = lax.axis_index("level") == 0
    traces = trace_a_ref[...] + jnp.where(stays, straight_ref[...], trace_b_ref[...])
    traces = pick(traces.reshape(-1, LANES), chosen).reshape(traces.shape)
    values = factor_ref[...] * traces - data_ref[...]
    for z in range(depth // 2):
        out_ref[z] = values[z, :, :width]
        out_ref[depth // 2 + z] = pltpu.roll(values[z], width, 1)[:, :width]


def whole(count):
    return [pl.BlockSpec(memory_space=pltpu.VMEM)] * count


def body(probe_bits, kappa_sq, observed):
    probes, tile_count = lax.axis_size("probe"), lax.axis_size("tile")
    unused, depth, rows, columns = probe_bits.shape
    assert probe_bits.shape[0] == 1 and lax.axis_size("level") == 2 and probes == 4
    assert rows == ROWS and columns == 2 * LANES and depth % (2 * LANES // EDGE) == 0
    params = pltpu.CompilerParams(vmem_limit_bytes=24 * 1024 * 1024)
    f32 = jnp.float32
    tiles = depth * EDGE // LANES
    field = depth + tiles
    sent = field + field // 2
    own_shape = jax.ShapeDtypeStruct((2 * field, ROWS, LANES), f32)
    near_shape = jax.ShapeDtypeStruct((sent + depth // ROWS, ROWS, LANES), f32)
    far_shape = jax.ShapeDtypeStruct((sent + 1, ROWS, LANES), f32)

    own_block, even_block, odd_block, cross_block = pl.pallas_call(
        functools.partial(pack_kernel, depth),
        out_shape=(own_shape, near_shape, near_shape, far_shape),
        in_specs=[pl.BlockSpec(memory_space=pltpu.HBM)] * 3,
        out_specs=tuple(whole(4)),
        scratch_shapes=[
            pltpu.VMEM((depth, rows, columns), jnp.int32),
            pltpu.VMEM((depth, rows, columns), f32),
            pltpu.VMEM((depth, rows, columns), f32),
            pltpu.SemaphoreType.DMA((3,)),
        ],
        compiler_params=params,
        name="pack",
    )(
        *(
            pltpu.with_memory_space_constraint(value, pltpu.HBM)
            for value in (probe_bits[0], kappa_sq, observed)
        )
    )

    def swaps(pairs):
        return [way for a, b in pairs for way in ((a, b), (b, a))]

    def tile_swap(block, first, flip):
        partner = dict(swaps([(i, i + 1) for i in range(first, tile_count - 1, 2)]))

        def device(probe, tile, level):
            return (probe * tile_count + tile) * 2 + level

        ways = []
        for probe in range(probes):
            for tile in range(tile_count):
                for level in range(2):
                    if tile in partner:
                        target = device(probe, partner[tile], level ^ flip)
                    else:
                        target = device(probe ^ 1, tile, level)
                    ways.append((device(probe, tile, level), target))
        return lax.ppermute(block, ("probe", "tile", "level"), ways)

    own_far = lax.ppermute(cross_block, "level", swaps([(0, 1)]))
    even = tile_swap(even_block, 0, 0)
    odd = tile_swap(odd_block, 1, 0)
    odd_far = tile_swap(own_far, 1, 0)
    even_far = tile_swap(cross_block, 0, 1)

    quarter = jax.ShapeDtypeStruct((depth, ROWS, columns // probes), f32)
    paired = jax.ShapeDtypeStruct((depth // 2, ROWS, LANES), f32)
    factor, data = pl.pallas_call(
        functools.partial(observed_kernel, depth, probes),
        out_shape=(paired, paired),
        in_specs=whole(5),
        out_specs=tuple(whole(2)),
        compiler_params=params,
        name="observed",
    )(kappa_sq, observed, even, odd, own_far)

    def core_swap(*pieces):
        kappa = jnp.concatenate([piece[field:sent] for piece in pieces], axis=0)
        return lax.ppermute(kappa, "probe", swaps([(0, 1), (2, 3)]))

    swapped = core_swap(even, odd, own_far)
    levels = 2 * depth
    part = jax.ShapeDtypeStruct((depth, 3 * ROWS, 2 * LANES), f32)
    own_part = jax.ShapeDtypeStruct((depth, ROWS, 2 * LANES), f32)
    near_diag, near_lower, near_forward, near_signs, near_k_signs = pl.pallas_call(
        functools.partial(near_kernel, depth),
        out_shape=(part, part, part, own_part, own_part),
        in_specs=whole(4),
        out_specs=tuple(whole(5)),
        scratch_shapes=[pltpu.VMEM((depth + 2, 3 * ROWS, 2 * LANES), f32)],
        compiler_params=params,
        name="near",
    )(own_block, even, odd, swapped)

    swapped_far = core_swap(even_far, odd_far)
    padded = pltpu.VMEM((levels + 1, 3 * ROWS, 2 * LANES), f32)
    plain = pltpu.VMEM((levels, 3 * ROWS, 2 * LANES), f32)
    short = pltpu.VMEM((depth, 3 * ROWS, 2 * LANES), f32)
    fields = jax.ShapeDtypeStruct((ITERS, levels, ROWS, 2 * LANES), f32)
    basis, images, far_signs, far_k_signs, gram = pl.pallas_call(
        functools.partial(basis_kernel, depth),
        out_shape=(
            fields,
            fields,
            own_part,
            own_part,
            jax.ShapeDtypeStruct((ROWS, LANES), f32),
        ),
        in_specs=whole(9),
        out_specs=tuple(whole(5)),
        scratch_shapes=[
            pltpu.VMEM((depth + 2, 3 * ROWS, 2 * LANES), f32),
            short,
            short,
            padded,
            padded,
            plain,
            plain,
            padded,
            pltpu.VMEM((SLOTS, levels // GROUP, ROWS, LANES), f32),
            pltpu.VMEM((3 * ROWS, 2 * LANES), f32),
        ],
        compiler_params=params,
        name="basis",
    )(
        near_diag,
        near_lower,
        near_forward,
        near_signs,
        own_far,
        even_far,
        odd_far,
        swapped,
        swapped_far,
    )
    terms = pl.pallas_call(
        functools.partial(terms_kernel, depth),
        out_shape=jax.ShapeDtypeStruct((ITERS, levels, ROWS, LANES), f32),
        in_specs=whole(6),
        out_specs=pl.BlockSpec(memory_space=pltpu.VMEM),
        compiler_params=params,
        name="terms",
    )(basis, images, near_signs, near_k_signs, far_signs, far_k_signs)

    if tile_count in (2, 4):
        group = [gram] + [
            lax.ppermute(
                gram,
                ("tile", "level"),
                swaps([(i, i ^ k) for i in range(2 * tile_count) if i < i ^ k]),
            )
            for k in (1, 2, 3)
        ]
        partials = [jnp.concatenate(group, axis=0)]
        if tile_count == 4:
            partials.append(lax.ppermute(partials[0], "tile", swaps([(0, 2), (1, 3)])))
    else:
        partials = [lax.all_gather(gram, ("tile", "level"), axis=0, tiled=True)]
    piece = jax.ShapeDtypeStruct((2, depth // 2, ROWS, LANES), f32)
    keep, send = pl.pallas_call(
        functools.partial(combine_kernel, depth),
        out_shape=(piece, piece),
        in_specs=whole(1 + len(partials)),
        out_specs=tuple(whole(2)),
        compiler_params=params,
        name="combine",
    )(terms, *partials)

    summed = keep + lax.ppermute(send, "probe", swaps([(0, 1), (2, 3)]))
    level = lax.axis_index("level")
    turned = lax.dynamic_index_in_dim(summed, 1 - level, 0, keepdims=False)
    straight = lax.dynamic_index_in_dim(summed, level, 0, keepdims=False)

    def device(x, core, level):
        return (2 * x + core) * 2 + level

    chips = [(x, core) for x in range(2) for core in range(2)]
    trace_a = lax.ppermute(
        turned,
        ("probe", "level"),
        [(device(x, core, 0), device(x, core, 1)) for x, core in chips]
        + [(device(x, core, 1), device(1 - x, core, 0)) for x, core in chips],
    )
    trace_b = lax.ppermute(
        straight,
        ("probe", "level"),
        [(device(x, core, 1), device(1 - x, core, 1)) for x, core in chips]
        + [(device(x, core, 0), device(x, 1 - core, 0)) for x, core in chips],
    )
    return pl.pallas_call(
        functools.partial(gradient_kernel, depth),
        out_shape=quarter,
        in_specs=whole(5),
        out_specs=pl.BlockSpec(memory_space=pltpu.VMEM),
        compiler_params=params,
        name="gradient",
    )(trace_b, trace_a, straight, factor, data)


def solution(mesh):
    in_specs = (
        P("probe", "level", "tile", None),
        P("level", "tile", None),
        P("level", "tile", None),
    )
    out_specs = P("level", "tile", "probe")
    return jax.shard_map(body, mesh=mesh, in_specs=in_specs, out_specs=out_specs, check_vma=False)
```

```python
import functools

import jax
import jax.numpy as jnp
from jax import lax
from jax.experimental import pallas as pl
from jax.experimental.pallas import tpu as pltpu
from jax.sharding import PartitionSpec as P

ITERS = 4
VERTICAL = 2.0
LANES = 128
ROWS = 8
HALO = ROWS - 1
EDGE = 8
GROUP = 8
SHIFTS = (1.0, -1.0, 0.0)
PAIRS = [(i, j) for j in range(ITERS) for i in range(j + 1)]
COUNT = len(PAIRS) + ITERS
SLOTS = 16


def two_sum(a, b):
    total = a + b
    part = total - a
    return total, (a - (total - part)) + (b - part)


def two_product(a, b):
    def split(v):
        big = v * 4097.0
        high = big - (big - v)
        return high, v - high

    product = a * b
    a_high, a_low = split(a)
    b_high, b_low = split(b)
    return product, ((a_high * b_high - product) + a_high * b_low + a_low * b_high) + a_low * b_low


def pair_add(first, second):
    total, rest = two_sum(first[0], second[0])
    rest = rest + (first[1] + second[1])
    high = total + rest
    return high, rest - (high - total)


def lane_ids(shape):
    return lax.broadcasted_iota(jnp.int32, shape, len(shape) - 1)


def row_ids(shape):
    return lax.broadcasted_iota(jnp.int32, shape, len(shape) - 2)


def split_three(values):
    high = values.astype(jnp.bfloat16)
    rest = values - high.astype(jnp.float32)
    middle = rest.astype(jnp.bfloat16)
    low = (rest - middle.astype(jnp.float32)).astype(jnp.bfloat16)
    return high, middle, low


def pick(values, chosen):
    high, middle, low = (
        jnp.dot(part, chosen, preferred_element_type=jnp.float32) for part in split_three(values)
    )
    return high + (middle + low)


def y_half():
    return lax.rem(lax.axis_index("level") + lax.axis_index("probe") // 2, 2)


def columns_of(half):
    shape = (2 * LANES, 2 * LANES)
    ids, lane = row_ids(shape), lane_ids(shape)
    odd = (lane // (LANES // 2)) % 2
    main = LANES * half + 2 * (lane % (LANES // 2)) + odd
    edge = LANES - EDGE * half + 2 * (lane % (EDGE // 2)) + odd
    wanted = jnp.where(lane < LANES, main, edge)
    return jnp.where(ids == wanted, 1.0, 0.0).astype(jnp.bfloat16)


def pack_kernel(
    depth,
    bits_hbm,
    kappa_hbm,
    observed_hbm,
    own_ref,
    even_ref,
    odd_ref,
    cross_ref,
    diagonal_ref,
    bits_ref,
    kappa_ref,
    observed_ref,
    arrived,
):
    copies = [
        pltpu.make_async_copy(source, target, arrived.at[place])
        for place, (source, target) in enumerate(
            ((bits_hbm, bits_ref), (kappa_hbm, kappa_ref), (observed_hbm, observed_ref))
        )
    ]
    for copy in copies:
        copy.start()
    level = lax.axis_index("level")
    first = level == 0
    in_first_core = lax.rem(lax.axis_index("probe"), 2) == 0
    per_tile = LANES // EDGE
    tiles = depth // per_tile
    slot_ids = (lane_ids((ROWS, LANES)) % (LANES // 2)) // (EDGE // 2)
    same_columns, cross_columns = columns_of(y_half()), columns_of(1 - y_half())

    def blocks(picked):
        picked = picked.reshape(depth, ROWS, 2 * LANES)
        edges = []
        for tile in range(tiles):
            packed = picked[tile * per_tile, :, LANES:]
            for slot in range(1, per_tile):
                packed = jnp.where(slot_ids == slot, picked[tile * per_tile + slot, :, LANES:], packed)
            edges.append(packed)
        return [picked[z, :, :LANES] for z in range(depth)], edges

    goes_up = lax.rem(lax.axis_index("tile"), 2) == 0

    def write(ref, base, main, edges, up=None):
        if up is not None:
            main = [jnp.where(up, pltpu.roll(tile, HALO, 0), tile)[:HALO] for tile in main]
        for tile in main + edges:
            ref[base : base + tile.shape[0]] = tile
            base += tile.shape[0]
        return base

    def halves(main, edges):
        low = main[: depth // 2] + edges[: tiles // 2]
        high = main[depth // 2 :] + edges[tiles // 2 :]
        both = [jnp.where(in_first_core, a, b) for a, b in zip(low, high)]
        return both[: depth // 2], both[depth // 2 :]

    copies[0].wait()
    signs = (2 * bits_ref[...] - 1).astype(jnp.float32).reshape(depth * ROWS, 2 * LANES)
    signs = signs.astype(jnp.bfloat16)
    same = blocks(jnp.dot(signs, same_columns, preferred_element_type=jnp.float32))
    cross = blocks(jnp.dot(signs, cross_columns, preferred_element_type=jnp.float32))
    own_base = write(own_ref, 0, *same)
    even_base = write(even_ref, 0, *same, goes_up)
    write(odd_ref, 0, *same, ~goes_up)
    cross_base = write(cross_ref, 0, *cross)
    write(diagonal_ref, 0, *cross, goes_up)
    copies[1].wait()
    kappa = kappa_ref[...].reshape(depth * ROWS, 2 * LANES)
    same = blocks(pick(kappa, same_columns))
    write(own_ref, own_base, *same)
    same, cross = halves(*same), halves(*blocks(pick(kappa, cross_columns)))
    write(odd_ref, even_base, *same, ~goes_up)
    cross_base = write(cross_ref, cross_base, *cross)
    write(diagonal_ref, even_base, *cross, goes_up)
    even_base = write(even_ref, even_base, *same, goes_up)
    copies[2].wait()
    in_low = lax.axis_index("probe") < lax.axis_size("probe") // 2

    def half(value):
        return jnp.where(in_low, value[..., :LANES], value[..., LANES:])

    top = half(observed_ref[:, ROWS - 1, :])
    bottom = half(observed_ref[:, 0, :])
    even_ref[even_base:] = jnp.where(goes_up, top, bottom)
    odd_ref[even_base:] = jnp.where(goes_up, bottom, top)
    cross_ref[cross_base:] = jnp.where(first, half(observed_ref[depth - 1]), half(observed_ref[0]))


def beside(values):
    rows = values.shape[0]
    even, odd = values[:, :LANES], values[:, LANES:]
    y_sides = jnp.concatenate(
        [odd + pltpu.roll(odd, 1, 1), even + pltpu.roll(even, LANES - 1, 1)], axis=1
    )
    return (pltpu.roll(values, 1, 0) + pltpu.roll(values, rows - 1, 0)) + y_sides


def inside_mask():
    shape = (3 * ROWS, 2 * LANES)
    tile = lax.axis_index("tile")
    half = LANES // 2
    lanes, ids = lane_ids(shape) % LANES, row_ids(shape)
    near = jnp.where(y_half() == 0, half, LANES - EDGE // 2)
    inside = (lanes < half) | ((lanes >= near) & (lanes < near + EDGE // 2))
    inside = inside & (ids >= jnp.where(tile > 0, 0, ROWS))
    inside = inside & (ids < jnp.where(tile < lax.axis_size("tile") - 1, 3 * ROWS, 2 * ROWS))
    return jnp.where(inside, 1.0, 0.0)


def join(z, even, own, odd):
    half, short = LANES // 2, EDGE // 2
    from_even = lax.rem(lax.axis_index("tile"), 2) == 1
    mine = lane_ids((ROWS, LANES)) < half
    shift = half + (half - short) * y_half() - short * lax.rem(z, LANES // EDGE)
    shift = lax.rem(shift + LANES, LANES)
    left = [jnp.where(from_even, a, b) for a, b in zip(even, odd)]
    right = [jnp.where(from_even, b, a) for a, b in zip(even, odd)]
    evens, odds = [], []
    for main, edge in (left, own, right):
        edge = pltpu.roll(edge, shift, 1)
        evens.append(jnp.where(mine, main, edge))
        odds.append(pltpu.roll(jnp.where(mine, edge, main), half, 1))
    return jnp.concatenate([jnp.concatenate(evens, axis=0), jnp.concatenate(odds, axis=0)], axis=1)


def unpack(depth, signs, half_diag, mask, sign_pieces, kappa_pieces):
    level = lax.axis_index("level")
    per_tile = LANES // EDGE

    def place(z):
        return jnp.where(level == 0, z, depth - 1 - z)

    def load(piece, count, z):
        ref, base, height, side = piece
        edge = base + height * count + ROWS * (z // per_tile)
        main = ref[base + height * z : base + height * z + ROWS]
        if side is not None:
            main = jnp.where(side, pltpu.roll(main, 1, 0), main)
        return main, ref[edge : edge + ROWS]

    for z in range(depth):
        signs[place(z) + 1] = join(z, *(load(piece, depth, z) for piece in sign_pieces)) * mask
    core = lax.rem(lax.axis_index("probe"), 2)
    short = depth // 2
    for start, pieces in zip((core, 1 - core), kappa_pieces):
        for step in range(short):
            z = start * short + step
            tiles = []
            for piece in pieces:
                if len(piece) == 2:
                    ref, base = piece
                    main = pl.multiple_of(base + ROWS * z, ROWS)
                    edge = base + ROWS * (depth + start * (short // per_tile) + step // per_tile)
                    edge = pl.multiple_of(edge, ROWS)
                    tiles.append((ref[pl.ds(main, ROWS)], ref[pl.ds(edge, ROWS)]))
                else:
                    tiles.append(load(piece, short, step))
            half_diag[place(z)] = 0.5 * join(step, *tiles) + (2.0 + VERTICAL)


def from_above():
    return lax.rem(lax.axis_index("tile"), 2) == 1


OWN_ROWS = slice(ROWS, 2 * ROWS)


def near_kernel(
    depth,
    own_ref,
    even_ref,
    odd_ref,
    swapped_ref,
    half_diag,
    lower,
    forward,
    own_signs,
    k_signs,
    signs,
):
    tiles = depth * EDGE // LANES
    field, thin = ROWS * (depth + tiles), HALO * depth + ROWS * tiles
    mask = inside_mask()
    zero = jnp.zeros(mask.shape, jnp.float32)
    signs[0] = zero
    signs[depth + 1] = zero
    above = from_above()
    kappa_pieces = (
        ((even_ref, thin, HALO, above), (own_ref, field), (odd_ref, thin, HALO, ~above)),
        ((swapped_ref, 0, HALO, above), (own_ref, field), (swapped_ref, thin // 2, HALO, ~above)),
    )
    sign_pieces = (
        (even_ref, 0, HALO, above),
        (own_ref, 0, ROWS, None),
        (odd_ref, 0, HALO, ~above),
    )
    unpack(depth, signs, half_diag, mask, sign_pieces, kappa_pieces)

    def down(k, carry):
        ratio, value = carry
        ratio = mask / (half_diag[k] - ratio)
        here = signs[k + 1]
        value = ratio * (here + value)
        lower[k] = ratio
        forward[k] = value
        image = half_diag[k] * here - (signs[k] + signs[k + 2]) - 0.5 * beside(here)
        own_signs[k] = here[OWN_ROWS]
        k_signs[k] = image[OWN_ROWS]
        return ratio, value

    lax.fori_loop(0, depth, down, (zero, zero), unroll=GROUP)


def basis_kernel(
    depth,
    near_diag,
    near_lower,
    near_forward,
    near_signs,
    own_far_ref,
    even_far_ref,
    odd_far_ref,
    swapped_ref,
    swapped_far_ref,
    basis_ref,
    image_ref,
    far_signs,
    far_k_signs,
    gram_ref,
    signs,
    far_diag,
    far_lower,
    upper,
    basis,
    forward,
    sides,
    backward,
    sums,
    masks,
):
    levels = 2 * depth
    mask = inside_mask()
    half_mask = 0.5 * mask
    masks[...] = half_mask
    zero = jnp.zeros(mask.shape, jnp.float32)
    own_zero = jnp.zeros((ROWS, LANES), jnp.float32)
    mine = lane_ids((ROWS, LANES)) < LANES // 2
    tiles = depth * EDGE // LANES
    field, thin = ROWS * (depth + tiles), HALO * depth + ROWS * tiles
    above = from_above()
    signs[0] = zero
    signs[0, OWN_ROWS] = near_signs[depth - 1]
    signs[depth + 1] = zero
    backward[levels] = zero
    upper[levels] = zero
    basis[levels] = zero
    kappa_pieces = (
        (
            (even_far_ref, thin, HALO, above),
            (own_far_ref, field, ROWS, None),
            (odd_far_ref, field, ROWS, None),
        ),
        (
            (swapped_far_ref, 0, HALO, above),
            (swapped_ref, thin, ROWS, None),
            (swapped_far_ref, thin // 2, ROWS, None),
        ),
    )
    sign_pieces = (
        (even_far_ref, 0, HALO, above),
        (own_far_ref, 0, ROWS, None),
        (odd_far_ref, 0, ROWS, None),
    )
    unpack(depth, signs, far_diag, mask, sign_pieces, kappa_pieces)

    def start_down(k, carry):
        ratio, value, from_end = carry
        ratio = mask / (far_diag[k] - ratio)
        here = signs[k + 1]
        value = ratio * (here + value)
        far_lower[k] = ratio
        forward[depth + k] = value
        other = depth - 1 - k
        from_end = mask / (far_diag[other] - from_end)
        upper[depth + other] = from_end
        image = far_diag[k] * here - (signs[k] + signs[k + 2]) - 0.5 * beside(here)
        far_signs[k] = here[OWN_ROWS]
        far_k_signs[k] = image[OWN_ROWS]
        return ratio, value, from_end

    start = (near_lower[depth - 1], near_forward[depth - 1], zero)
    carry = lax.fori_loop(0, depth, start_down, start, unroll=depth)

    def start_up_far(step, carry):
        k = depth - 1 - step
        solved, value = carry
        solved = forward[depth + k] + far_lower[k] * solved
        value = upper[depth + k] * (solved + value)
        backward[depth + k] = value
        return solved, value

    solved, value = lax.fori_loop(0, depth, start_up_far, (zero, zero), unroll=depth)

    def start_up_near(step, carry):
        k = depth - 1 - step
        ratio, solved, value = carry
        ratio = mask / (near_diag[k] - ratio)
        solved = near_forward[k] + near_lower[k] * solved
        value = ratio * (solved + value)
        upper[k] = ratio
        backward[k] = value
        return ratio, solved, value

    lax.fori_loop(0, depth, start_up_near, (carry[2], solved, value), unroll=depth)

    parts = (
        (0, near_diag, near_lower, lambda k: near_signs[k]),
        (depth, far_diag, far_lower, lambda k: signs[k + 1, OWN_ROWS]),
    )
    place = 0
    for index in range(ITERS):
        final = index + 1 == ITERS
        group_size = 2 * GROUP if final else GROUP

        def next_basis(k, previous, index=index):
            solved = backward[k] + upper[k] * previous
            if index == 0:
                value = solved
            elif SHIFTS[index - 1] == 0.0:
                value = solved
            elif SHIFTS[index - 1] == 1.0:
                value = basis[k] - solved
            elif SHIFTS[index - 1] == -1.0:
                value = basis[k] + solved
            else:
                value = SHIFTS[index - 1] * basis[k] - solved
            return solved, value

        solved, here = next_basis(0, zero)
        if not final:
            basis[0] = here
        carry = (solved, zero, here, zero)
        slots = list(range(place, place + index + 1)) + [len(PAIRS) + index]
        for offset, half_diag, lower, sign_of in parts:

            def down(group, carry):
                solved, above, here, value = carry
                added = [None] * len(slots)
                for step in range(group_size):
                    k = group * group_size + step
                    solved, below = next_basis(offset + k + 1, solved)
                    if not final:
                        basis[offset + k + 1] = below
                    side = beside(here)
                    image = half_diag[k] * here - (above + below) - masks[...] * side
                    if not final:
                        value = lower[k] * (beside(image) + value)
                        forward[offset + k] = value
                        sides[offset + k] = side
                    my_basis, my_image = here[OWN_ROWS], image[OWN_ROWS]
                    basis_ref[index, offset + k] = my_basis
                    image_ref[index, offset + k] = my_image
                    factors = [(image_ref[other, offset + k], my_image) for other in range(index)]
                    factors += [(my_image, my_image), (my_basis, sign_of(k))]
                    for slot, (a, b) in enumerate(factors):
                        product = a[:, :LANES] * b[:, :LANES] + a[:, LANES:] * b[:, LANES:]
                        added[slot] = product if step % GROUP == 0 else added[slot] + product
                        if step % GROUP == GROUP - 1:
                            at = (offset + group * group_size + step) // GROUP
                            sums[slots[slot], at] = added[slot]
                    above, here = here, below
                return solved, above, here, value

            carry = lax.fori_loop(0, depth // group_size, down, carry)
        place += index + 1
        if final:
            break
        carry = (zero, zero)
        for offset, half_diag, lower, sign_of in reversed(parts):

            def up(step, carry):
                k = depth - 1 - step
                solved, value = carry
                solved = forward[offset + k] + lower[k] * solved
                value = upper[offset + k] * ((sides[offset + k] + solved) + value)
                backward[offset + k] = value
                return solved, value

            carry = lax.fori_loop(0, depth, up, carry, unroll=4 * GROUP)

    ids = row_ids((ROWS, LANES))
    sides_of = [[], []]
    for block in range(SLOTS // ROWS):
        high, low = own_zero, own_zero
        for slot in range(block * ROWS, min((block + 1) * ROWS, COUNT)):
            pair = (sums[slot, 0], own_zero)
            for at in range(1, sums.shape[1]):
                total, rest = two_sum(pair[0], sums[slot, at])
                pair = (total, pair[1] + rest)
            pair = tuple(jnp.where(mine, part, 0.0) for part in pair)
            for shift in (4, 2, 1):
                pair = pair_add(pair, tuple(pltpu.roll(part, shift, 0) for part in pair))
            here = ids == slot - block * ROWS
            high, low = jnp.where(here, pair[0], high), jnp.where(here, pair[1], low)
        sides_of[0].append(high)
        sides_of[1].append(low)
    ones = jnp.ones((LANES, LANES), jnp.bfloat16)

    def lane_sum(part):
        return jnp.dot(part, ones, preferred_element_type=jnp.float32)

    high, low = (jnp.concatenate(blocks, axis=0) for blocks in sides_of)
    first, second, third = (lane_sum(part) for part in split_three(high))
    high, rest = two_sum(first, second)
    low = rest + (third + lane_sum(low.astype(jnp.bfloat16)))
    quarter = lane_ids((ROWS, LANES)) // (LANES // 4)
    tile = high[:ROWS]
    for place, block in enumerate((high[ROWS:], low[:ROWS], low[ROWS:])):
        tile = jnp.where(quarter == place + 1, block, tile)
    gram_ref[...] = tile


def terms_kernel(
    depth, basis_ref, image_ref, near_signs, near_k_signs, far_signs, far_k_signs, terms_ref
):
    level = lax.axis_index("level")
    half = LANES // 2
    mine = lane_ids((ROWS, LANES)) < half
    for offset, signs, k_signs in ((0, near_signs, near_k_signs), (depth, far_signs, far_k_signs)):

        def step(k, unused, offset=offset, signs=signs, k_signs=k_signs):
            z = offset + k
            target = jnp.where(level == 0, z, 2 * depth - 1 - z)
            sign, image = signs[k], k_signs[k]
            for index in range(ITERS):
                term = basis_ref[index, z] * image + image_ref[index, z] * sign
                terms_ref[index, target] = jnp.where(
                    mine, term[:, :LANES], pltpu.roll(term[:, LANES:], half, 1)
                )
            return unused

        if offset == 0:
            lax.fori_loop(0, depth - 1, step, 0, unroll=GROUP)
            sign, image = signs[depth - 1], k_signs[depth - 1] - far_signs[0]
            target = jnp.where(level == 0, depth - 1, depth)
            for index in range(ITERS):
                term = basis_ref[index, depth - 1] * image + image_ref[index, depth - 1] * sign
                terms_ref[index, target] = jnp.where(
                    mine, term[:, :LANES], pltpu.roll(term[:, LANES:], half, 1)
                )
        else:
            lax.fori_loop(0, depth, step, 0, unroll=GROUP)


def solve_small(high, low):
    def entry(index):
        return tuple(jnp.broadcast_to(part[index : index + 1], (ROWS, LANES)) for part in (high, low))

    gram = {}
    for place, (i, j) in enumerate(PAIRS):
        gram[i, j] = gram[j, i] = entry(place)
    right = [entry(len(PAIRS) + j) for j in range(ITERS)]
    work = {key: pair[0] for key, pair in gram.items()}
    ratios, inverses = {}, []
    for i in range(ITERS):
        pivot = work[i, i]
        good = pivot > 1e-7 * gram[i, i][0]
        inverses.append(jnp.where(good, 1.0 / jnp.where(good, pivot, 1.0), 0.0))
        for r in range(i + 1, ITERS):
            ratios[r, i] = work[r, i] * inverses[i]
        for r in range(i + 1, ITERS):
            for c in range(i + 1, r + 1):
                work[r, c] = work[c, r] = work[r, c] - ratios[r, i] * work[c, i]

    def solve(values):
        values = list(values)
        for i in range(ITERS):
            for r in range(i + 1, ITERS):
                values[r] = values[r] - ratios[r, i] * values[i]
        values = [value * inverse for value, inverse in zip(values, inverses)]
        for i in reversed(range(ITERS)):
            for r in range(i):
                values[r] = values[r] - ratios[i, r] * values[i]
        return values

    found = solve([pair[0] for pair in right])
    for unused in range(2):
        rest = []
        for i in range(ITERS):
            total = right[i]
            for j in range(ITERS):
                product, error = two_product(gram[i, j][0], found[j])
                total = pair_add(total, (-product, -(error + gram[i, j][1] * found[j])))
            rest.append(total[0] + total[1])
        found = [a + b for a, b in zip(found, solve(rest))]
    return found


def combine_kernel(depth, terms_ref, *refs):
    gram_refs, (keep_ref, send_ref) = refs[:-2], refs[-2:]
    half, width = LANES // 2, LANES // 4
    pairs = []
    for ref in gram_refs:
        for start in range(0, ref.shape[0], ROWS):
            tile = ref[start : start + ROWS]
            pairs.append((tile, pltpu.roll(tile, half, 1)))
    while len(pairs) > 1:
        merged = [pair_add(pairs[i], pairs[i + 1]) for i in range(0, len(pairs) - 1, 2)]
        pairs = merged + pairs[2 * len(merged) :]
    lanes = lane_ids((ROWS, LANES))

    def spread(part, block):
        part = jnp.where(lanes // width == block, part, 0.0)
        part = part + pltpu.roll(part, width, 1)
        return part + pltpu.roll(part, half, 1)

    found = solve_small(
        *(jnp.concatenate([spread(part, 0), spread(part, 1)], axis=0) for part in pairs[0])
    )
    core = lax.rem(lax.axis_index("probe"), 2)
    first_lanes = lanes % half < width
    pairs_deep = depth // 2

    def step(z, unused):
        for which in range(2):
            def total(k):
                value = found[0] * terms_ref[0, k]
                for j in range(1, ITERS):
                    value = value + found[j] * terms_ref[j, k]
                return value

            one = total(which * depth + z)
            two = total(which * depth + pairs_deep + z)
            low = jnp.where(first_lanes, one, pltpu.roll(two, width, 1))
            high = jnp.where(first_lanes, pltpu.roll(one, LANES - width, 1), two)
            keep_ref[which, z] = jnp.where(core == 0, low, high)
            send_ref[which, z] = jnp.where(core == 0, high, low)
        return unused

    lax.fori_loop(0, pairs_deep, step, 0, unroll=GROUP)


def observed_kernel(
    depth, probes, kappa_ref, observed_ref, even_ref, odd_ref, far_ref, factor_ref, data_ref
):
    level = lax.axis_index("level")
    tile = lax.axis_index("tile")
    last_tile = lax.axis_size("tile") - 1
    probe = lax.axis_index("probe")
    in_low = probe < probes // 2
    even = lax.rem(probe, 2) == 0
    width = LANES // 2
    lanes = lane_ids((ROWS, 2 * LANES))
    ids = row_ids((ROWS, LANES))
    base = even_ref.shape[0] - depth
    from_even = lax.rem(tile, 2) == 1

    def half(value):
        return jnp.where(in_low, value[..., :LANES], value[..., LANES:])

    def take(value):
        return jnp.where(even, value, pltpu.roll(value, width, 1))

    far_edge = far_ref[far_ref.shape[0] - ROWS :]
    factors, parts = [], []
    for z in range(depth):
        value = observed_ref[z]
        mine = half(value)
        y_sides = jnp.where(lanes > 0, pltpu.roll(value, 1, 1), 0.0) + jnp.where(
            lanes < 2 * LANES - 1, pltpu.roll(value, 2 * LANES - 1, 1), 0.0
        )
        first = even_ref[base + z : base + z + 1]
        second = odd_ref[base + z : base + z + 1]
        left, right = jnp.where(from_even, first, second), jnp.where(from_even, second, first)
        before = jnp.where(ids > 0, pltpu.roll(mine, 1, 0), jnp.where(tile > 0, left, 0.0))
        after = jnp.where(
            ids < ROWS - 1, pltpu.roll(mine, ROWS - 1, 0), jnp.where(tile < last_tile, right, 0.0)
        )
        above = half(observed_ref[z - 1]) if z > 0 else jnp.where(level > 0, far_edge, 0.0)
        below = half(observed_ref[z + 1]) if z < depth - 1 else jnp.where(level == 0, far_edge, 0.0)
        kappa = half(kappa_ref[z])
        k_observed = (
            (kappa + (4.0 + 2.0 * VERTICAL)) * mine
            - (before + after)
            - half(y_sides)
            - VERTICAL * (above + below)
        )
        factors.append(take(kappa * (0.5 / probes)))
        parts.append(take(kappa * (2.0 * mine * k_observed)))
    first_lanes = lane_ids((ROWS, LANES)) < width
    for ref, values in ((factor_ref, factors), (data_ref, parts)):
        for z in range(depth // 2):
            ref[z] = jnp.where(first_lanes, values[z], pltpu.roll(values[depth // 2 + z], width, 1))


def gradient_kernel(
    depth, trace_b_ref, trace_a_ref, straight_ref, factor_ref, data_ref, out_ref
):
    width = LANES // 2
    square = (LANES, LANES)
    lane = lane_ids(square)
    source = (width // 2) * (lane // width) + (lane % width) // 2 + width * (lane % 2)
    chosen = jnp.where(row_ids(square) == source, 1.0, 0.0).astype(jnp.bfloat16)
    stays = lax.axis_index("level") == 0
    traces = trace_a_ref[...] + jnp.where(stays, straight_ref[...], trace_b_ref[...])
    traces = pick(traces.reshape(-1, LANES), chosen).reshape(traces.shape)
    values = factor_ref[...] * traces - data_ref[...]
    for z in range(depth // 2):
        out_ref[z] = values[z, :, :width]
        out_ref[depth // 2 + z] = pltpu.roll(values[z], width, 1)[:, :width]


def whole(count):
    return [pl.BlockSpec(memory_space=pltpu.VMEM)] * count


def body(probe_bits, kappa_sq, observed):
    probes, tile_count = lax.axis_size("probe"), lax.axis_size("tile")
    unused, depth, rows, columns = probe_bits.shape
    assert probe_bits.shape[0] == 1 and lax.axis_size("level") == 2 and probes == 4
    assert rows == ROWS and columns == 2 * LANES and depth % (2 * LANES // EDGE) == 0
    params = pltpu.CompilerParams(vmem_limit_bytes=24 * 1024 * 1024)
    f32 = jnp.float32
    tiles = depth * EDGE // LANES
    field, thin = ROWS * (depth + tiles), HALO * depth + ROWS * tiles

    def block(count):
        return jax.ShapeDtypeStruct((count, LANES), f32)

    near_shape = block(thin + thin // 2 + depth)
    far_shape = block(field + field // 2 + ROWS)

    own_block, even_block, odd_block, cross_block, diagonal_block = pl.pallas_call(
        functools.partial(pack_kernel, depth),
        out_shape=(block(2 * field), near_shape, near_shape, far_shape, block(thin + thin // 2)),
        in_specs=[pl.BlockSpec(memory_space=pltpu.HBM)] * 3,
        out_specs=tuple(whole(5)),
        scratch_shapes=[
            pltpu.VMEM((depth, rows, columns), jnp.int32),
            pltpu.VMEM((depth, rows, columns), f32),
            pltpu.VMEM((depth, rows, columns), f32),
            pltpu.SemaphoreType.DMA((3,)),
        ],
        compiler_params=params,
        name="pack",
    )(
        *(
            pltpu.with_memory_space_constraint(value, pltpu.HBM)
            for value in (probe_bits[0], kappa_sq, observed)
        )
    )

    def swaps(pairs):
        return [way for a, b in pairs for way in ((a, b), (b, a))]

    def tile_swap(block, first, flip):
        partner = dict(swaps([(i, i + 1) for i in range(first, tile_count - 1, 2)]))

        def device(probe, tile, level):
            return (probe * tile_count + tile) * 2 + level

        ways = []
        for probe in range(probes):
            for tile in range(tile_count):
                for level in range(2):
                    if tile in partner:
                        target = device(probe, partner[tile], level ^ flip)
                    else:
                        target = device(probe ^ 1, tile, level)
                    ways.append((device(probe, tile, level), target))
        return lax.ppermute(block, ("probe", "tile", "level"), ways)

    own_far = lax.ppermute(cross_block, "level", swaps([(0, 1)]))
    even = tile_swap(even_block, 0, 0)
    odd = tile_swap(odd_block, 1, 0)
    odd_far = tile_swap(own_far, 1, 0)
    even_far = tile_swap(diagonal_block, 0, 1)

    quarter = jax.ShapeDtypeStruct((depth, ROWS, columns // probes), f32)
    paired = jax.ShapeDtypeStruct((depth // 2, ROWS, LANES), f32)
    factor, data = pl.pallas_call(
        functools.partial(observed_kernel, depth, probes),
        out_shape=(paired, paired),
        in_specs=whole(5),
        out_specs=tuple(whole(2)),
        compiler_params=params,
        name="observed",
    )(kappa_sq, observed, even, odd, own_far)

    def core_swap(*pieces):
        kappa = jnp.concatenate([piece[first : first + first // 2] for piece, first in pieces], axis=0)
        return lax.ppermute(kappa, "probe", swaps([(0, 1), (2, 3)]))

    swapped = core_swap((even, thin), (odd, thin), (own_far, field))
    levels = 2 * depth
    part = jax.ShapeDtypeStruct((depth, 3 * ROWS, 2 * LANES), f32)
    own_part = jax.ShapeDtypeStruct((depth, ROWS, 2 * LANES), f32)
    near_diag, near_lower, near_forward, near_signs, near_k_signs = pl.pallas_call(
        functools.partial(near_kernel, depth),
        out_shape=(part, part, part, own_part, own_part),
        in_specs=whole(4),
        out_specs=tuple(whole(5)),
        scratch_shapes=[pltpu.VMEM((depth + 2, 3 * ROWS, 2 * LANES), f32)],
        compiler_params=params,
        name="near",
    )(own_block, even, odd, swapped)

    swapped_far = core_swap((even_far, thin), (odd_far, field))
    padded = pltpu.VMEM((levels + 1, 3 * ROWS, 2 * LANES), f32)
    plain = pltpu.VMEM((levels, 3 * ROWS, 2 * LANES), f32)
    short = pltpu.VMEM((depth, 3 * ROWS, 2 * LANES), f32)
    fields = jax.ShapeDtypeStruct((ITERS, levels, ROWS, 2 * LANES), f32)
    basis, images, far_signs, far_k_signs, gram = pl.pallas_call(
        functools.partial(basis_kernel, depth),
        out_shape=(
            fields,
            fields,
            own_part,
            own_part,
            jax.ShapeDtypeStruct((ROWS, LANES), f32),
        ),
        in_specs=whole(9),
        out_specs=tuple(whole(5)),
        scratch_shapes=[
            pltpu.VMEM((depth + 2, 3 * ROWS, 2 * LANES), f32),
            short,
            short,
            padded,
            padded,
            plain,
            plain,
            padded,
            pltpu.VMEM((SLOTS, levels // GROUP, ROWS, LANES), f32),
            pltpu.VMEM((3 * ROWS, 2 * LANES), f32),
        ],
        compiler_params=params,
        name="basis",
    )(
        near_diag,
        near_lower,
        near_forward,
        near_signs,
        own_far,
        even_far,
        odd_far,
        swapped,
        swapped_far,
    )
    terms = pl.pallas_call(
        functools.partial(terms_kernel, depth),
        out_shape=jax.ShapeDtypeStruct((ITERS, levels, ROWS, LANES), f32),
        in_specs=whole(6),
        out_specs=pl.BlockSpec(memory_space=pltpu.VMEM),
        compiler_params=params,
        name="terms",
    )(basis, images, near_signs, near_k_signs, far_signs, far_k_signs)

    if tile_count in (2, 4):
        group = [gram] + [
            lax.ppermute(
                gram,
                ("tile", "level"),
                swaps([(i, i ^ k) for i in range(2 * tile_count) if i < i ^ k]),
            )
            for k in (1, 2, 3)
        ]
        partials = [jnp.concatenate(group, axis=0)]
        if tile_count == 4:
            partials.append(lax.ppermute(partials[0], "tile", swaps([(0, 2), (1, 3)])))
    else:
        partials = [lax.all_gather(gram, ("tile", "level"), axis=0, tiled=True)]
    piece = jax.ShapeDtypeStruct((2, depth // 2, ROWS, LANES), f32)
    keep, send = pl.pallas_call(
        functools.partial(combine_kernel, depth),
        out_shape=(piece, piece),
        in_specs=whole(1 + len(partials)),
        out_specs=tuple(whole(2)),
        compiler_params=params,
        name="combine",
    )(terms, *partials)

    summed = keep + lax.ppermute(send, "probe", swaps([(0, 1), (2, 3)]))
    level = lax.axis_index("level")
    turned = lax.dynamic_index_in_dim(summed, 1 - level, 0, keepdims=False)
    straight = lax.dynamic_index_in_dim(summed, level, 0, keepdims=False)

    def device(x, core, level):
        return (2 * x + core) * 2 + level

    chips = [(x, core) for x in range(2) for core in range(2)]
    trace_a = lax.ppermute(
        turned,
        ("probe", "level"),
        [(device(x, core, 0), device(x, core, 1)) for x, core in chips]
        + [(device(x, core, 1), device(1 - x, core, 0)) for x, core in chips],
    )
    trace_b = lax.ppermute(
        straight,
        ("probe", "level"),
        [(device(x, core, 1), device(1 - x, core, 1)) for x, core in chips]
        + [(device(x, core, 0), device(x, 1 - core, 0)) for x, core in chips],
    )
    return pl.pallas_call(
        functools.partial(gradient_kernel, depth),
        out_shape=quarter,
        in_specs=whole(5),
        out_specs=pl.BlockSpec(memory_space=pltpu.VMEM),
        compiler_params=params,
        name="gradient",
    )(trace_b, trace_a, straight, factor, data)


def solution(mesh):
    in_specs = (
        P("probe", "level", "tile", None),
        P("level", "tile", None),
        P("level", "tile", None),
    )
    out_specs = P("level", "tile", "probe")
    return jax.shard_map(body, mesh=mesh, in_specs=in_specs, out_specs=out_specs, check_vma=False)
```

```python
import functools

import jax
import jax.numpy as jnp
from jax import lax
from jax.experimental import pallas as pl
from jax.experimental.pallas import tpu as pltpu
from jax.sharding import PartitionSpec as P

ITERS = 4
VERTICAL = 2.0
LANES = 128
ROWS = 8
HALO = ROWS - 1
EDGE = 8
GROUP = 8
SHIFTS = (1.0, -1.0, 0.0)
PAIRS = [(i, j) for j in range(ITERS) for i in range(j + 1)]
COUNT = len(PAIRS) + ITERS
SLOTS = 16


def two_sum(a, b):
    total = a + b
    part = total - a
    return total, (a - (total - part)) + (b - part)


def two_product(a, b):
    def split(v):
        big = v * 4097.0
        high = big - (big - v)
        return high, v - high

    product = a * b
    a_high, a_low = split(a)
    b_high, b_low = split(b)
    return product, ((a_high * b_high - product) + a_high * b_low + a_low * b_high) + a_low * b_low


def pair_add(first, second):
    total, rest = two_sum(first[0], second[0])
    rest = rest + (first[1] + second[1])
    high = total + rest
    return high, rest - (high - total)


def lane_ids(shape):
    return lax.broadcasted_iota(jnp.int32, shape, len(shape) - 1)


def row_ids(shape):
    return lax.broadcasted_iota(jnp.int32, shape, len(shape) - 2)


def split_three(values):
    high = values.astype(jnp.bfloat16)
    rest = values - high.astype(jnp.float32)
    middle = rest.astype(jnp.bfloat16)
    low = (rest - middle.astype(jnp.float32)).astype(jnp.bfloat16)
    return high, middle, low


def pick(values, chosen):
    high, middle, low = (
        jnp.dot(part, chosen, preferred_element_type=jnp.float32) for part in split_three(values)
    )
    return high + (middle + low)


def y_half():
    return lax.rem(lax.axis_index("level") + lax.axis_index("probe") // 2, 2)


def columns_of(half):
    shape = (2 * LANES, 2 * LANES)
    ids, lane = row_ids(shape), lane_ids(shape)
    odd = (lane // (LANES // 2)) % 2
    main = LANES * half + 2 * (lane % (LANES // 2)) + odd
    edge = LANES - EDGE * half + 2 * (lane % (EDGE // 2)) + odd
    wanted = jnp.where(lane < LANES, main, edge)
    return jnp.where(ids == wanted, 1.0, 0.0).astype(jnp.bfloat16)


def pack_kernel(
    depth,
    bits_hbm,
    kappa_hbm,
    observed_hbm,
    own_ref,
    even_ref,
    odd_ref,
    cross_ref,
    diagonal_ref,
    bits_ref,
    kappa_ref,
    observed_ref,
    arrived,
):
    copies = [
        pltpu.make_async_copy(source, target, arrived.at[place])
        for place, (source, target) in enumerate(
            ((bits_hbm, bits_ref), (kappa_hbm, kappa_ref), (observed_hbm, observed_ref))
        )
    ]
    for copy in copies:
        copy.start()
    level = lax.axis_index("level")
    first = level == 0
    in_first_core = lax.rem(lax.axis_index("probe"), 2) == 0
    per_tile = LANES // EDGE
    tiles = depth // per_tile
    slot_ids = (lane_ids((ROWS, LANES)) % (LANES // 2)) // (EDGE // 2)
    same_columns, cross_columns = columns_of(y_half()), columns_of(1 - y_half())

    def blocks(picked):
        picked = picked.reshape(depth, ROWS, 2 * LANES)
        edges = []
        for tile in range(tiles):
            packed = picked[tile * per_tile, :, LANES:]
            for slot in range(1, per_tile):
                packed = jnp.where(slot_ids == slot, picked[tile * per_tile + slot, :, LANES:], packed)
            edges.append(packed)
        return [picked[z, :, :LANES] for z in range(depth)], edges

    goes_up = lax.rem(lax.axis_index("tile"), 2) == 0

    def write(ref, base, main, edges, up=None):
        if up is not None:
            main = [jnp.where(up, pltpu.roll(tile, HALO, 0), tile)[:HALO] for tile in main]
        for tile in main + edges:
            ref[base : base + tile.shape[0]] = tile
            base += tile.shape[0]
        return base

    def halves(main, edges):
        low = main[: depth // 2] + edges[: tiles // 2]
        high = main[depth // 2 :] + edges[tiles // 2 :]
        both = [jnp.where(in_first_core, a, b) for a, b in zip(low, high)]
        return both[: depth // 2], both[depth // 2 :]

    copies[0].wait()
    signs = (2 * bits_ref[...] - 1).astype(jnp.float32).reshape(depth * ROWS, 2 * LANES)
    signs = signs.astype(jnp.bfloat16)
    same = blocks(jnp.dot(signs, same_columns, preferred_element_type=jnp.float32))
    cross = blocks(jnp.dot(signs, cross_columns, preferred_element_type=jnp.float32))
    own_base = write(own_ref, 0, *same)
    even_base = write(even_ref, 0, *same, goes_up)
    write(odd_ref, 0, *same, ~goes_up)
    cross_base = write(cross_ref, 0, *cross)
    write(diagonal_ref, 0, *cross, goes_up)
    copies[1].wait()
    kappa = kappa_ref[...].reshape(depth * ROWS, 2 * LANES)
    same = blocks(pick(kappa, same_columns))
    write(own_ref, own_base, *same)
    same, cross = halves(*same), halves(*blocks(pick(kappa, cross_columns)))
    write(odd_ref, even_base, *same, ~goes_up)
    cross_base = write(cross_ref, cross_base, *cross)
    write(diagonal_ref, even_base, *cross, goes_up)
    even_base = write(even_ref, even_base, *same, goes_up)
    copies[2].wait()
    in_low = lax.axis_index("probe") < lax.axis_size("probe") // 2

    def half(value):
        return jnp.where(in_low, value[..., :LANES], value[..., LANES:])

    top = half(observed_ref[:, ROWS - 1, :])
    bottom = half(observed_ref[:, 0, :])
    width = LANES // 2
    first_lanes = lane_ids((depth // 2, LANES)) < width

    def quarters(value):
        value = jnp.where(in_first_core, value, pltpu.roll(value, width, 1))
        return jnp.where(first_lanes, value[: depth // 2], pltpu.roll(value[depth // 2 :], width, 1))

    top, bottom = quarters(top), quarters(bottom)
    even_ref[even_base:] = jnp.where(goes_up, top, bottom)
    odd_ref[even_base:] = jnp.where(goes_up, bottom, top)
    cross_ref[cross_base:] = jnp.where(first, half(observed_ref[depth - 1]), half(observed_ref[0]))


def beside(values):
    rows = values.shape[0]
    even, odd = values[:, :LANES], values[:, LANES:]
    y_sides = jnp.concatenate(
        [odd + pltpu.roll(odd, 1, 1), even + pltpu.roll(even, LANES - 1, 1)], axis=1
    )
    return (pltpu.roll(values, 1, 0) + pltpu.roll(values, rows - 1, 0)) + y_sides


def inside_mask():
    shape = (3 * ROWS, 2 * LANES)
    tile = lax.axis_index("tile")
    half = LANES // 2
    lanes, ids = lane_ids(shape) % LANES, row_ids(shape)
    near = jnp.where(y_half() == 0, half, LANES - EDGE // 2)
    inside = (lanes < half) | ((lanes >= near) & (lanes < near + EDGE // 2))
    inside = inside & (ids >= jnp.where(tile > 0, 0, ROWS))
    inside = inside & (ids < jnp.where(tile < lax.axis_size("tile") - 1, 3 * ROWS, 2 * ROWS))
    return jnp.where(inside, 1.0, 0.0)


def join(z, even, own, odd):
    half, short = LANES // 2, EDGE // 2
    from_even = lax.rem(lax.axis_index("tile"), 2) == 1
    mine = lane_ids((ROWS, LANES)) < half
    shift = half + (half - short) * y_half() - short * lax.rem(z, LANES // EDGE)
    shift = lax.rem(shift + LANES, LANES)
    left = [jnp.where(from_even, a, b) for a, b in zip(even, odd)]
    right = [jnp.where(from_even, b, a) for a, b in zip(even, odd)]
    evens, odds = [], []
    for main, edge in (left, own, right):
        edge = pltpu.roll(edge, shift, 1)
        evens.append(jnp.where(mine, main, edge))
        odds.append(pltpu.roll(jnp.where(mine, edge, main), half, 1))
    return jnp.concatenate([jnp.concatenate(evens, axis=0), jnp.concatenate(odds, axis=0)], axis=1)


def unpack(depth, signs, half_diag, mask, sign_pieces, kappa_pieces):
    level = lax.axis_index("level")
    per_tile = LANES // EDGE

    def place(z):
        return jnp.where(level == 0, z, depth - 1 - z)

    def load(piece, count, z):
        ref, base, height, side = piece
        edge = base + height * count + ROWS * (z // per_tile)
        main = ref[base + height * z : base + height * z + ROWS]
        if side is not None:
            main = jnp.where(side, pltpu.roll(main, 1, 0), main)
        return main, ref[edge : edge + ROWS]

    for z in range(depth):
        signs[place(z) + 1] = join(z, *(load(piece, depth, z) for piece in sign_pieces)) * mask
    core = lax.rem(lax.axis_index("probe"), 2)
    short = depth // 2
    for start, pieces in zip((core, 1 - core), kappa_pieces):
        for step in range(short):
            z = start * short + step
            tiles = []
            for piece in pieces:
                if len(piece) == 2:
                    ref, base = piece
                    main = pl.multiple_of(base + ROWS * z, ROWS)
                    edge = base + ROWS * (depth + start * (short // per_tile) + step // per_tile)
                    edge = pl.multiple_of(edge, ROWS)
                    tiles.append((ref[pl.ds(main, ROWS)], ref[pl.ds(edge, ROWS)]))
                else:
                    tiles.append(load(piece, short, step))
            half_diag[place(z)] = 0.5 * join(step, *tiles) + (2.0 + VERTICAL)


def from_above():
    return lax.rem(lax.axis_index("tile"), 2) == 1


OWN_ROWS = slice(ROWS, 2 * ROWS)


def near_kernel(
    depth,
    own_ref,
    even_ref,
    odd_ref,
    swapped_ref,
    half_diag,
    lower,
    forward,
    own_signs,
    k_signs,
    signs,
):
    tiles = depth * EDGE // LANES
    field, thin = ROWS * (depth + tiles), HALO * depth + ROWS * tiles
    mask = inside_mask()
    zero = jnp.zeros(mask.shape, jnp.float32)
    signs[0] = zero
    signs[depth + 1] = zero
    above = from_above()
    kappa_pieces = (
        ((even_ref, thin, HALO, above), (own_ref, field), (odd_ref, thin, HALO, ~above)),
        ((swapped_ref, 0, HALO, above), (own_ref, field), (swapped_ref, thin // 2, HALO, ~above)),
    )
    sign_pieces = (
        (even_ref, 0, HALO, above),
        (own_ref, 0, ROWS, None),
        (odd_ref, 0, HALO, ~above),
    )
    unpack(depth, signs, half_diag, mask, sign_pieces, kappa_pieces)

    def down(k, carry):
        ratio, value = carry
        ratio = mask / (half_diag[k] - ratio)
        here = signs[k + 1]
        value = ratio * (here + value)
        lower[k] = ratio
        forward[k] = value
        image = half_diag[k] * here - (signs[k] + signs[k + 2]) - 0.5 * beside(here)
        own_signs[k] = here[OWN_ROWS]
        k_signs[k] = image[OWN_ROWS]
        return ratio, value

    lax.fori_loop(0, depth, down, (zero, zero), unroll=GROUP)


def basis_kernel(
    depth,
    near_diag,
    near_lower,
    near_forward,
    near_signs,
    own_far_ref,
    even_far_ref,
    odd_far_ref,
    swapped_ref,
    swapped_far_ref,
    basis_ref,
    image_ref,
    far_signs,
    far_k_signs,
    gram_ref,
    signs,
    far_diag,
    far_lower,
    upper,
    basis,
    forward,
    sides,
    backward,
    sums,
    masks,
):
    levels = 2 * depth
    mask = inside_mask()
    half_mask = 0.5 * mask
    masks[...] = half_mask
    zero = jnp.zeros(mask.shape, jnp.float32)
    own_zero = jnp.zeros((ROWS, LANES), jnp.float32)
    mine = lane_ids((ROWS, LANES)) < LANES // 2
    tiles = depth * EDGE // LANES
    field, thin = ROWS * (depth + tiles), HALO * depth + ROWS * tiles
    above = from_above()
    signs[0] = zero
    signs[0, OWN_ROWS] = near_signs[depth - 1]
    signs[depth + 1] = zero
    backward[levels] = zero
    upper[levels] = zero
    basis[levels] = zero
    kappa_pieces = (
        (
            (even_far_ref, thin, HALO, above),
            (own_far_ref, field, ROWS, None),
            (odd_far_ref, field, ROWS, None),
        ),
        (
            (swapped_far_ref, 0, HALO, above),
            (swapped_ref, thin, ROWS, None),
            (swapped_far_ref, thin // 2, ROWS, None),
        ),
    )
    sign_pieces = (
        (even_far_ref, 0, HALO, above),
        (own_far_ref, 0, ROWS, None),
        (odd_far_ref, 0, ROWS, None),
    )
    unpack(depth, signs, far_diag, mask, sign_pieces, kappa_pieces)

    def start_down(k, carry):
        ratio, value, from_end = carry
        ratio = mask / (far_diag[k] - ratio)
        here = signs[k + 1]
        value = ratio * (here + value)
        far_lower[k] = ratio
        forward[depth + k] = value
        other = depth - 1 - k
        from_end = mask / (far_diag[other] - from_end)
        upper[depth + other] = from_end
        image = far_diag[k] * here - (signs[k] + signs[k + 2]) - 0.5 * beside(here)
        far_signs[k] = here[OWN_ROWS]
        far_k_signs[k] = image[OWN_ROWS]
        return ratio, value, from_end

    start = (near_lower[depth - 1], near_forward[depth - 1], zero)
    carry = lax.fori_loop(0, depth, start_down, start, unroll=depth)

    def start_up_far(step, carry):
        k = depth - 1 - step
        solved, value = carry
        solved = forward[depth + k] + far_lower[k] * solved
        value = upper[depth + k] * (solved + value)
        backward[depth + k] = value
        return solved, value

    solved, value = lax.fori_loop(0, depth, start_up_far, (zero, zero), unroll=depth)

    def start_up_near(step, carry):
        k = depth - 1 - step
        ratio, solved, value = carry
        ratio = mask / (near_diag[k] - ratio)
        solved = near_forward[k] + near_lower[k] * solved
        value = ratio * (solved + value)
        upper[k] = ratio
        backward[k] = value
        return ratio, solved, value

    lax.fori_loop(0, depth, start_up_near, (carry[2], solved, value), unroll=depth)

    parts = (
        (0, near_diag, near_lower, lambda k: near_signs[k]),
        (depth, far_diag, far_lower, lambda k: signs[k + 1, OWN_ROWS]),
    )
    place = 0
    for index in range(ITERS):
        final = index + 1 == ITERS
        group_size = 2 * GROUP if final else GROUP

        def next_basis(k, previous, index=index):
            solved = backward[k] + upper[k] * previous
            if index == 0:
                value = solved
            elif SHIFTS[index - 1] == 0.0:
                value = solved
            elif SHIFTS[index - 1] == 1.0:
                value = basis[k] - solved
            elif SHIFTS[index - 1] == -1.0:
                value = basis[k] + solved
            else:
                value = SHIFTS[index - 1] * basis[k] - solved
            return solved, value

        solved, here = next_basis(0, zero)
        if not final:
            basis[0] = here
        carry = (solved, zero, here, zero)
        slots = list(range(place, place + index + 1)) + [len(PAIRS) + index]
        for offset, half_diag, lower, sign_of in parts:

            def down(group, carry):
                solved, above, here, value = carry
                added = [None] * len(slots)
                for step in range(group_size):
                    k = group * group_size + step
                    solved, below = next_basis(offset + k + 1, solved)
                    if not final:
                        basis[offset + k + 1] = below
                    side = beside(here)
                    image = half_diag[k] * here - (above + below) - masks[...] * side
                    if not final:
                        value = lower[k] * (beside(image) + value)
                        forward[offset + k] = value
                        sides[offset + k] = side
                    my_basis, my_image = here[OWN_ROWS], image[OWN_ROWS]
                    basis_ref[index, offset + k] = my_basis
                    image_ref[index, offset + k] = my_image
                    factors = [(image_ref[other, offset + k], my_image) for other in range(index)]
                    factors += [(my_image, my_image), (my_basis, sign_of(k))]
                    for slot, (a, b) in enumerate(factors):
                        product = a[:, :LANES] * b[:, :LANES] + a[:, LANES:] * b[:, LANES:]
                        added[slot] = product if step % GROUP == 0 else added[slot] + product
                        if step % GROUP == GROUP - 1:
                            at = (offset + group * group_size + step) // GROUP
                            sums[slots[slot], at] = added[slot]
                    above, here = here, below
                return solved, above, here, value

            carry = lax.fori_loop(0, depth // group_size, down, carry)
        place += index + 1
        if final:
            break
        carry = (zero, zero)
        for offset, half_diag, lower, sign_of in reversed(parts):

            def up(step, carry):
                k = depth - 1 - step
                solved, value = carry
                solved = forward[offset + k] + lower[k] * solved
                value = upper[offset + k] * ((sides[offset + k] + solved) + value)
                backward[offset + k] = value
                return solved, value

            carry = lax.fori_loop(0, depth, up, carry, unroll=4 * GROUP)

    ids = row_ids((ROWS, LANES))
    sides_of = [[], []]
    for block in range(SLOTS // ROWS):
        high, low = own_zero, own_zero
        for slot in range(block * ROWS, min((block + 1) * ROWS, COUNT)):
            pair = (sums[slot, 0], own_zero)
            for at in range(1, sums.shape[1]):
                total, rest = two_sum(pair[0], sums[slot, at])
                pair = (total, pair[1] + rest)
            pair = tuple(jnp.where(mine, part, 0.0) for part in pair)
            for shift in (4, 2, 1):
                pair = pair_add(pair, tuple(pltpu.roll(part, shift, 0) for part in pair))
            here = ids == slot - block * ROWS
            high, low = jnp.where(here, pair[0], high), jnp.where(here, pair[1], low)
        sides_of[0].append(high)
        sides_of[1].append(low)
    ones = jnp.ones((LANES, LANES), jnp.bfloat16)

    def lane_sum(part):
        return jnp.dot(part, ones, preferred_element_type=jnp.float32)

    high, low = (jnp.concatenate(blocks, axis=0) for blocks in sides_of)
    first, second, third = (lane_sum(part) for part in split_three(high))
    high, rest = two_sum(first, second)
    low = rest + (third + lane_sum(low.astype(jnp.bfloat16)))
    quarter = lane_ids((ROWS, LANES)) // (LANES // 4)
    tile = high[:ROWS]
    for place, block in enumerate((high[ROWS:], low[:ROWS], low[ROWS:])):
        tile = jnp.where(quarter == place + 1, block, tile)
    gram_ref[...] = tile


def terms_kernel(
    depth, basis_ref, image_ref, near_signs, near_k_signs, far_signs, far_k_signs, terms_ref
):
    level = lax.axis_index("level")
    half = LANES // 2
    mine = lane_ids((ROWS, LANES)) < half
    for offset, signs, k_signs in ((0, near_signs, near_k_signs), (depth, far_signs, far_k_signs)):

        def step(k, unused, offset=offset, signs=signs, k_signs=k_signs):
            z = offset + k
            target = jnp.where(level == 0, z, 2 * depth - 1 - z)
            sign, image = signs[k], k_signs[k]
            for index in range(ITERS):
                term = basis_ref[index, z] * image + image_ref[index, z] * sign
                terms_ref[index, target] = jnp.where(
                    mine, term[:, :LANES], pltpu.roll(term[:, LANES:], half, 1)
                )
            return unused

        if offset == 0:
            lax.fori_loop(0, depth - 1, step, 0, unroll=GROUP)
            sign, image = signs[depth - 1], k_signs[depth - 1] - far_signs[0]
            target = jnp.where(level == 0, depth - 1, depth)
            for index in range(ITERS):
                term = basis_ref[index, depth - 1] * image + image_ref[index, depth - 1] * sign
                terms_ref[index, target] = jnp.where(
                    mine, term[:, :LANES], pltpu.roll(term[:, LANES:], half, 1)
                )
        else:
            lax.fori_loop(0, depth, step, 0, unroll=GROUP)


def solve_small(high, low):
    def entry(index):
        return tuple(jnp.broadcast_to(part[index : index + 1], (ROWS, LANES)) for part in (high, low))

    gram = {}
    for place, (i, j) in enumerate(PAIRS):
        gram[i, j] = gram[j, i] = entry(place)
    right = [entry(len(PAIRS) + j) for j in range(ITERS)]
    work = {key: pair[0] for key, pair in gram.items()}
    ratios, inverses = {}, []
    for i in range(ITERS):
        pivot = work[i, i]
        good = pivot > 1e-7 * gram[i, i][0]
        inverses.append(jnp.where(good, 1.0 / jnp.where(good, pivot, 1.0), 0.0))
        for r in range(i + 1, ITERS):
            ratios[r, i] = work[r, i] * inverses[i]
        for r in range(i + 1, ITERS):
            for c in range(i + 1, r + 1):
                work[r, c] = work[c, r] = work[r, c] - ratios[r, i] * work[c, i]

    def solve(values):
        values = list(values)
        for i in range(ITERS):
            for r in range(i + 1, ITERS):
                values[r] = values[r] - ratios[r, i] * values[i]
        values = [value * inverse for value, inverse in zip(values, inverses)]
        for i in reversed(range(ITERS)):
            for r in range(i):
                values[r] = values[r] - ratios[i, r] * values[i]
        return values

    found = solve([pair[0] for pair in right])
    for unused in range(2):
        rest = []
        for i in range(ITERS):
            total = right[i]
            for j in range(ITERS):
                product, error = two_product(gram[i, j][0], found[j])
                total = pair_add(total, (-product, -(error + gram[i, j][1] * found[j])))
            rest.append(total[0] + total[1])
        found = [a + b for a, b in zip(found, solve(rest))]
    return found


def combine_kernel(depth, terms_ref, *refs):
    gram_refs, (keep_ref, send_ref) = refs[:-2], refs[-2:]
    half, width = LANES // 2, LANES // 4
    pairs = []
    for ref in gram_refs:
        for start in range(0, ref.shape[0], ROWS):
            tile = ref[start : start + ROWS]
            pairs.append((tile, pltpu.roll(tile, half, 1)))
    while len(pairs) > 1:
        merged = [pair_add(pairs[i], pairs[i + 1]) for i in range(0, len(pairs) - 1, 2)]
        pairs = merged + pairs[2 * len(merged) :]
    lanes = lane_ids((ROWS, LANES))

    def spread(part, block):
        part = jnp.where(lanes // width == block, part, 0.0)
        part = part + pltpu.roll(part, width, 1)
        return part + pltpu.roll(part, half, 1)

    found = solve_small(
        *(jnp.concatenate([spread(part, 0), spread(part, 1)], axis=0) for part in pairs[0])
    )
    core = lax.rem(lax.axis_index("probe"), 2)
    first_lanes = lanes % half < width
    pairs_deep = depth // 2

    def step(z, unused):
        for which in range(2):
            def total(k):
                value = found[0] * terms_ref[0, k]
                for j in range(1, ITERS):
                    value = value + found[j] * terms_ref[j, k]
                return value

            one = total(which * depth + z)
            two = total(which * depth + pairs_deep + z)
            low = jnp.where(first_lanes, one, pltpu.roll(two, width, 1))
            high = jnp.where(first_lanes, pltpu.roll(one, LANES - width, 1), two)
            keep_ref[which, z] = jnp.where(core == 0, low, high)
            send_ref[which, z] = jnp.where(core == 0, high, low)
        return unused

    lax.fori_loop(0, pairs_deep, step, 0, unroll=GROUP)


def observed_kernel(
    depth, probes, kappa_ref, observed_ref, even_ref, odd_ref, far_ref, factor_ref, data_ref
):
    level = lax.axis_index("level")
    tile = lax.axis_index("tile")
    last_tile = lax.axis_size("tile") - 1
    probe = lax.axis_index("probe")
    in_low = probe < probes // 2
    even = lax.rem(probe, 2) == 0
    width = LANES // 2
    lanes = lane_ids((ROWS, 2 * LANES))
    ids = row_ids((ROWS, LANES))
    base = even_ref.shape[0] - depth // 2

    def rows_beside(ref):
        packed = ref[base : base + depth // 2]
        turned = pltpu.roll(packed, width, 1)
        first_lanes = lane_ids(packed.shape) < width
        return jnp.concatenate(
            [jnp.where(first_lanes, packed, turned), jnp.where(first_lanes, turned, packed)], axis=0
        )

    even_rows, odd_rows = rows_beside(even_ref), rows_beside(odd_ref)
    from_even = lax.rem(tile, 2) == 1

    def half(value):
        return jnp.where(in_low, value[..., :LANES], value[..., LANES:])

    def take(value):
        return jnp.where(even, value, pltpu.roll(value, width, 1))

    far_edge = far_ref[far_ref.shape[0] - ROWS :]
    factors, parts = [], []
    for z in range(depth):
        value = observed_ref[z]
        mine = half(value)
        y_sides = jnp.where(lanes > 0, pltpu.roll(value, 1, 1), 0.0) + jnp.where(
            lanes < 2 * LANES - 1, pltpu.roll(value, 2 * LANES - 1, 1), 0.0
        )
        first, second = even_rows[z : z + 1], odd_rows[z : z + 1]
        left, right = jnp.where(from_even, first, second), jnp.where(from_even, second, first)
        before = jnp.where(ids > 0, pltpu.roll(mine, 1, 0), jnp.where(tile > 0, left, 0.0))
        after = jnp.where(
            ids < ROWS - 1, pltpu.roll(mine, ROWS - 1, 0), jnp.where(tile < last_tile, right, 0.0)
        )
        above = half(observed_ref[z - 1]) if z > 0 else jnp.where(level > 0, far_edge, 0.0)
        below = half(observed_ref[z + 1]) if z < depth - 1 else jnp.where(level == 0, far_edge, 0.0)
        kappa = half(kappa_ref[z])
        k_observed = (
            (kappa + (4.0 + 2.0 * VERTICAL)) * mine
            - (before + after)
            - half(y_sides)
            - VERTICAL * (above + below)
        )
        factors.append(take(kappa * (0.5 / probes)))
        parts.append(take(kappa * (2.0 * mine * k_observed)))
    first_lanes = lane_ids((ROWS, LANES)) < width
    for ref, values in ((factor_ref, factors), (data_ref, parts)):
        for z in range(depth // 2):
            ref[z] = jnp.where(first_lanes, values[z], pltpu.roll(values[depth // 2 + z], width, 1))


def gradient_kernel(
    depth, trace_b_ref, trace_a_ref, straight_ref, factor_ref, data_ref, out_ref
):
    width = LANES // 2
    square = (LANES, LANES)
    lane = lane_ids(square)
    source = (width // 2) * (lane // width) + (lane % width) // 2 + width * (lane % 2)
    chosen = jnp.where(row_ids(square) == source, 1.0, 0.0).astype(jnp.bfloat16)
    stays = lax.axis_index("level") == 0
    traces = trace_a_ref[...] + jnp.where(stays, straight_ref[...], trace_b_ref[...])
    traces = pick(traces.reshape(-1, LANES), chosen).reshape(traces.shape)
    values = factor_ref[...] * traces - data_ref[...]
    for z in range(depth // 2):
        out_ref[z] = values[z, :, :width]
        out_ref[depth // 2 + z] = pltpu.roll(values[z], width, 1)[:, :width]


def whole(count):
    return [pl.BlockSpec(memory_space=pltpu.VMEM)] * count


def body(probe_bits, kappa_sq, observed):
    probes, tile_count = lax.axis_size("probe"), lax.axis_size("tile")
    unused, depth, rows, columns = probe_bits.shape
    assert probe_bits.shape[0] == 1 and lax.axis_size("level") == 2 and probes == 4
    assert rows == ROWS and columns == 2 * LANES and depth % (2 * LANES // EDGE) == 0
    params = pltpu.CompilerParams(vmem_limit_bytes=24 * 1024 * 1024)
    f32 = jnp.float32
    tiles = depth * EDGE // LANES
    field, thin = ROWS * (depth + tiles), HALO * depth + ROWS * tiles

    def block(count):
        return jax.ShapeDtypeStruct((count, LANES), f32)

    near_shape = block(thin + thin // 2 + depth // 2)
    far_shape = block(field + field // 2 + ROWS)

    own_block, even_block, odd_block, cross_block, diagonal_block = pl.pallas_call(
        functools.partial(pack_kernel, depth),
        out_shape=(block(2 * field), near_shape, near_shape, far_shape, block(thin + thin // 2)),
        in_specs=[pl.BlockSpec(memory_space=pltpu.HBM)] * 3,
        out_specs=tuple(whole(5)),
        scratch_shapes=[
            pltpu.VMEM((depth, rows, columns), jnp.int32),
            pltpu.VMEM((depth, rows, columns), f32),
            pltpu.VMEM((depth, rows, columns), f32),
            pltpu.SemaphoreType.DMA((3,)),
        ],
        compiler_params=params,
        name="pack",
    )(
        *(
            pltpu.with_memory_space_constraint(value, pltpu.HBM)
            for value in (probe_bits[0], kappa_sq, observed)
        )
    )

    def swaps(pairs):
        return [way for a, b in pairs for way in ((a, b), (b, a))]

    def tile_swap(block, first, flip):
        partner = dict(swaps([(i, i + 1) for i in range(first, tile_count - 1, 2)]))

        def device(probe, tile, level):
            return (probe * tile_count + tile) * 2 + level

        ways = []
        for probe in range(probes):
            for tile in range(tile_count):
                for level in range(2):
                    if tile in partner:
                        target = device(probe, partner[tile], level ^ flip)
                    else:
                        target = device(probe ^ 1, tile, level)
                    ways.append((device(probe, tile, level), target))
        return lax.ppermute(block, ("probe", "tile", "level"), ways)

    own_far = lax.ppermute(cross_block, "level", swaps([(0, 1)]))
    even = tile_swap(even_block, 0, 0)
    odd = tile_swap(odd_block, 1, 0)
    odd_far = tile_swap(own_far, 1, 0)
    even_far = tile_swap(diagonal_block, 0, 1)

    quarter = jax.ShapeDtypeStruct((depth, ROWS, columns // probes), f32)
    paired = jax.ShapeDtypeStruct((depth // 2, ROWS, LANES), f32)
    factor, data = pl.pallas_call(
        functools.partial(observed_kernel, depth, probes),
        out_shape=(paired, paired),
        in_specs=whole(5),
        out_specs=tuple(whole(2)),
        compiler_params=params,
        name="observed",
    )(kappa_sq, observed, even, odd, own_far)

    def core_swap(*pieces):
        kappa = jnp.concatenate([piece[first : first + first // 2] for piece, first in pieces], axis=0)
        return lax.ppermute(kappa, "probe", swaps([(0, 1), (2, 3)]))

    swapped = core_swap((even, thin), (odd, thin), (own_far, field))
    levels = 2 * depth
    part = jax.ShapeDtypeStruct((depth, 3 * ROWS, 2 * LANES), f32)
    own_part = jax.ShapeDtypeStruct((depth, ROWS, 2 * LANES), f32)
    near_diag, near_lower, near_forward, near_signs, near_k_signs = pl.pallas_call(
        functools.partial(near_kernel, depth),
        out_shape=(part, part, part, own_part, own_part),
        in_specs=whole(4),
        out_specs=tuple(whole(5)),
        scratch_shapes=[pltpu.VMEM((depth + 2, 3 * ROWS, 2 * LANES), f32)],
        compiler_params=params,
        name="near",
    )(own_block, even, odd, swapped)

    swapped_far = core_swap((even_far, thin), (odd_far, field))
    padded = pltpu.VMEM((levels + 1, 3 * ROWS, 2 * LANES), f32)
    plain = pltpu.VMEM((levels, 3 * ROWS, 2 * LANES), f32)
    short = pltpu.VMEM((depth, 3 * ROWS, 2 * LANES), f32)
    fields = jax.ShapeDtypeStruct((ITERS, levels, ROWS, 2 * LANES), f32)
    basis, images, far_signs, far_k_signs, gram = pl.pallas_call(
        functools.partial(basis_kernel, depth),
        out_shape=(
            fields,
            fields,
            own_part,
            own_part,
            jax.ShapeDtypeStruct((ROWS, LANES), f32),
        ),
        in_specs=whole(9),
        out_specs=tuple(whole(5)),
        scratch_shapes=[
            pltpu.VMEM((depth + 2, 3 * ROWS, 2 * LANES), f32),
            short,
            short,
            padded,
            padded,
            plain,
            plain,
            padded,
            pltpu.VMEM((SLOTS, levels // GROUP, ROWS, LANES), f32),
            pltpu.VMEM((3 * ROWS, 2 * LANES), f32),
        ],
        compiler_params=params,
        name="basis",
    )(
        near_diag,
        near_lower,
        near_forward,
        near_signs,
        own_far,
        even_far,
        odd_far,
        swapped,
        swapped_far,
    )
    terms = pl.pallas_call(
        functools.partial(terms_kernel, depth),
        out_shape=jax.ShapeDtypeStruct((ITERS, levels, ROWS, LANES), f32),
        in_specs=whole(6),
        out_specs=pl.BlockSpec(memory_space=pltpu.VMEM),
        compiler_params=params,
        name="terms",
    )(basis, images, near_signs, near_k_signs, far_signs, far_k_signs)

    if tile_count in (2, 4):
        group = [gram] + [
            lax.ppermute(
                gram,
                ("tile", "level"),
                swaps([(i, i ^ k) for i in range(2 * tile_count) if i < i ^ k]),
            )
            for k in (1, 2, 3)
        ]
        partials = [jnp.concatenate(group, axis=0)]
        if tile_count == 4:
            partials.append(lax.ppermute(partials[0], "tile", swaps([(0, 2), (1, 3)])))
    else:
        partials = [lax.all_gather(gram, ("tile", "level"), axis=0, tiled=True)]
    piece = jax.ShapeDtypeStruct((2, depth // 2, ROWS, LANES), f32)
    keep, send = pl.pallas_call(
        functools.partial(combine_kernel, depth),
        out_shape=(piece, piece),
        in_specs=whole(1 + len(partials)),
        out_specs=tuple(whole(2)),
        compiler_params=params,
        name="combine",
    )(terms, *partials)

    summed = keep + lax.ppermute(send, "probe", swaps([(0, 1), (2, 3)]))
    level = lax.axis_index("level")
    turned = lax.dynamic_index_in_dim(summed, 1 - level, 0, keepdims=False)
    straight = lax.dynamic_index_in_dim(summed, level, 0, keepdims=False)

    def device(x, core, level):
        return (2 * x + core) * 2 + level

    chips = [(x, core) for x in range(2) for core in range(2)]
    trace_a = lax.ppermute(
        turned,
        ("probe", "level"),
        [(device(x, core, 0), device(x, core, 1)) for x, core in chips]
        + [(device(x, core, 1), device(1 - x, core, 0)) for x, core in chips],
    )
    trace_b = lax.ppermute(
        straight,
        ("probe", "level"),
        [(device(x, core, 1), device(1 - x, core, 1)) for x, core in chips]
        + [(device(x, core, 0), device(x, 1 - core, 0)) for x, core in chips],
    )
    return pl.pallas_call(
        functools.partial(gradient_kernel, depth),
        out_shape=quarter,
        in_specs=whole(5),
        out_specs=pl.BlockSpec(memory_space=pltpu.VMEM),
        compiler_params=params,
        name="gradient",
    )(trace_b, trace_a, straight, factor, data)


def solution(mesh):
    in_specs = (
        P("probe", "level", "tile", None),
        P("level", "tile", None),
        P("level", "tile", None),
    )
    out_specs = P("level", "tile", "probe")
    return jax.shard_map(body, mesh=mesh, in_specs=in_specs, out_specs=out_specs, check_vma=False)
```

```python
import functools

import jax
import jax.numpy as jnp
from jax import lax
from jax.experimental import pallas as pl
from jax.experimental.pallas import tpu as pltpu
from jax.sharding import PartitionSpec as P

ITERS = 4
VERTICAL = 2.0
LANES = 128
ROWS = 8
HALO = ROWS - 1
EDGE = 8
GROUP = 8
SHIFTS = (1.0, -1.0, 0.0)
PAIRS = [(i, j) for j in range(ITERS) for i in range(j + 1)]
COUNT = len(PAIRS) + ITERS
SLOTS = 16


def two_sum(a, b):
    total = a + b
    part = total - a
    return total, (a - (total - part)) + (b - part)


def two_product(a, b):
    def split(v):
        big = v * 4097.0
        high = big - (big - v)
        return high, v - high

    product = a * b
    a_high, a_low = split(a)
    b_high, b_low = split(b)
    return product, ((a_high * b_high - product) + a_high * b_low + a_low * b_high) + a_low * b_low


def pair_add(first, second):
    total, rest = two_sum(first[0], second[0])
    rest = rest + (first[1] + second[1])
    high = total + rest
    return high, rest - (high - total)


def lane_ids(shape):
    return lax.broadcasted_iota(jnp.int32, shape, len(shape) - 1)


def row_ids(shape):
    return lax.broadcasted_iota(jnp.int32, shape, len(shape) - 2)


def split_three(values):
    high = values.astype(jnp.bfloat16)
    rest = values - high.astype(jnp.float32)
    middle = rest.astype(jnp.bfloat16)
    low = (rest - middle.astype(jnp.float32)).astype(jnp.bfloat16)
    return high, middle, low


def pick(values, chosen):
    high, middle, low = (
        jnp.dot(part, chosen, preferred_element_type=jnp.float32) for part in split_three(values)
    )
    return high + (middle + low)


def y_half():
    return lax.rem(lax.axis_index("level") + lax.axis_index("probe") // 2, 2)


def columns_of(half):
    shape = (2 * LANES, 2 * LANES)
    ids, lane = row_ids(shape), lane_ids(shape)
    odd = (lane // (LANES // 2)) % 2
    main = LANES * half + 2 * (lane % (LANES // 2)) + odd
    edge = LANES - EDGE * half + 2 * (lane % (EDGE // 2)) + odd
    wanted = jnp.where(lane < LANES, main, edge)
    return jnp.where(ids == wanted, 1.0, 0.0).astype(jnp.bfloat16)


def pack_kernel(
    depth,
    bits_hbm,
    kappa_hbm,
    observed_hbm,
    own_ref,
    even_ref,
    odd_ref,
    cross_ref,
    diagonal_ref,
    bits_ref,
    kappa_ref,
    observed_ref,
    arrived,
):
    copies = [
        pltpu.make_async_copy(source, target, arrived.at[place])
        for place, (source, target) in enumerate(
            ((bits_hbm, bits_ref), (kappa_hbm, kappa_ref), (observed_hbm, observed_ref))
        )
    ]
    for copy in copies:
        copy.start()
    level = lax.axis_index("level")
    first = level == 0
    in_first_core = lax.rem(lax.axis_index("probe"), 2) == 0
    per_tile = LANES // EDGE
    tiles = depth // per_tile
    slot_ids = (lane_ids((ROWS, LANES)) % (LANES // 2)) // (EDGE // 2)
    same_columns, cross_columns = columns_of(y_half()), columns_of(1 - y_half())

    def blocks(picked):
        picked = picked.reshape(depth, ROWS, 2 * LANES)
        edges = []
        for tile in range(tiles):
            packed = picked[tile * per_tile, :, LANES:]
            for slot in range(1, per_tile):
                packed = jnp.where(slot_ids == slot, picked[tile * per_tile + slot, :, LANES:], packed)
            edges.append(packed)
        return [picked[z, :, :LANES] for z in range(depth)], edges

    goes_up = lax.rem(lax.axis_index("tile"), 2) == 0

    def write(ref, base, main, edges, up=None):
        if up is not None:
            main = [jnp.where(up, pltpu.roll(tile, HALO, 0), tile)[:HALO] for tile in main]
        for tile in main + edges:
            ref[base : base + tile.shape[0]] = tile
            base += tile.shape[0]
        return base

    def halves(main, edges):
        low = main[: depth // 2] + edges[: tiles // 2]
        high = main[depth // 2 :] + edges[tiles // 2 :]
        both = [jnp.where(in_first_core, a, b) for a, b in zip(low, high)]
        return both[: depth // 2], both[depth // 2 :]

    copies[0].wait()
    signs = (2 * bits_ref[...] - 1).astype(jnp.float32).reshape(depth * ROWS, 2 * LANES)
    signs = signs.astype(jnp.bfloat16)
    same = blocks(jnp.dot(signs, same_columns, preferred_element_type=jnp.float32))
    cross = blocks(jnp.dot(signs, cross_columns, preferred_element_type=jnp.float32))
    own_base = write(own_ref, 0, *same)
    even_base = write(even_ref, 0, *same, goes_up)
    write(odd_ref, 0, *same, ~goes_up)
    cross_base = write(cross_ref, 0, *cross)
    write(diagonal_ref, 0, *cross, goes_up)
    copies[1].wait()
    kappa = kappa_ref[...].reshape(depth * ROWS, 2 * LANES)
    same = blocks(pick(kappa, same_columns))
    write(own_ref, own_base, *same)
    same, cross = halves(*same), halves(*blocks(pick(kappa, cross_columns)))
    write(odd_ref, even_base, *same, ~goes_up)
    cross_base = write(cross_ref, cross_base, *cross)
    write(diagonal_ref, even_base, *cross, goes_up)
    even_base = write(even_ref, even_base, *same, goes_up)
    copies[2].wait()
    in_low = lax.axis_index("probe") < lax.axis_size("probe") // 2

    def half(value):
        return jnp.where(in_low, value[..., :LANES], value[..., LANES:])

    top = half(observed_ref[:, ROWS - 1, :])
    bottom = half(observed_ref[:, 0, :])
    even_ref[even_base:] = jnp.where(goes_up, top, bottom)
    odd_ref[even_base:] = jnp.where(goes_up, bottom, top)
    cross_ref[cross_base:] = jnp.where(first, half(observed_ref[depth - 1]), half(observed_ref[0]))


def beside(values):
    rows = values.shape[0]
    even, odd = values[:, :LANES], values[:, LANES:]
    y_sides = jnp.concatenate(
        [odd + pltpu.roll(odd, 1, 1), even + pltpu.roll(even, LANES - 1, 1)], axis=1
    )
    return (pltpu.roll(values, 1, 0) + pltpu.roll(values, rows - 1, 0)) + y_sides


def inside_mask():
    shape = (3 * ROWS, 2 * LANES)
    tile = lax.axis_index("tile")
    half = LANES // 2
    lanes, ids = lane_ids(shape) % LANES, row_ids(shape)
    near = jnp.where(y_half() == 0, half, LANES - EDGE // 2)
    inside = (lanes < half) | ((lanes >= near) & (lanes < near + EDGE // 2))
    inside = inside & (ids >= jnp.where(tile > 0, 0, ROWS))
    inside = inside & (ids < jnp.where(tile < lax.axis_size("tile") - 1, 3 * ROWS, 2 * ROWS))
    return jnp.where(inside, 1.0, 0.0)


def join(z, even, own, odd):
    half, short = LANES // 2, EDGE // 2
    from_even = lax.rem(lax.axis_index("tile"), 2) == 1
    mine = lane_ids((ROWS, LANES)) < half
    shift = half + (half - short) * y_half() - short * lax.rem(z, LANES // EDGE)
    shift = lax.rem(shift + LANES, LANES)
    left = [jnp.where(from_even, a, b) for a, b in zip(even, odd)]
    right = [jnp.where(from_even, b, a) for a, b in zip(even, odd)]
    evens, odds = [], []
    for main, edge in (left, own, right):
        edge = pltpu.roll(edge, shift, 1)
        evens.append(jnp.where(mine, main, edge))
        odds.append(pltpu.roll(jnp.where(mine, edge, main), half, 1))
    return jnp.concatenate([jnp.concatenate(evens, axis=0), jnp.concatenate(odds, axis=0)], axis=1)


def unpack(depth, signs, half_diag, mask, sign_pieces, kappa_pieces):
    level = lax.axis_index("level")
    per_tile = LANES // EDGE

    def place(z):
        return jnp.where(level == 0, z, depth - 1 - z)

    def load(piece, count, z):
        ref, base, height, side = piece
        edge = base + height * count + ROWS * (z // per_tile)
        main = ref[base + height * z : base + height * z + ROWS]
        if side is not None:
            main = jnp.where(side, pltpu.roll(main, 1, 0), main)
        return main, ref[edge : edge + ROWS]

    for z in range(depth):
        signs[place(z) + 1] = join(z, *(load(piece, depth, z) for piece in sign_pieces)) * mask
    core = lax.rem(lax.axis_index("probe"), 2)
    short = depth // 2
    for start, pieces in zip((core, 1 - core), kappa_pieces):
        for step in range(short):
            z = start * short + step
            tiles = []
            for piece in pieces:
                if len(piece) == 2:
                    ref, base = piece
                    main = pl.multiple_of(base + ROWS * z, ROWS)
                    edge = base + ROWS * (depth + start * (short // per_tile) + step // per_tile)
                    edge = pl.multiple_of(edge, ROWS)
                    tiles.append((ref[pl.ds(main, ROWS)], ref[pl.ds(edge, ROWS)]))
                else:
                    tiles.append(load(piece, short, step))
            half_diag[place(z)] = 0.5 * join(step, *tiles) + (2.0 + VERTICAL)


def from_above():
    return lax.rem(lax.axis_index("tile"), 2) == 1


OWN_ROWS = slice(ROWS, 2 * ROWS)


def near_kernel(
    depth,
    own_ref,
    even_ref,
    odd_ref,
    swapped_ref,
    half_diag,
    lower,
    forward,
    own_signs,
    k_signs,
    signs,
):
    tiles = depth * EDGE // LANES
    field, thin = ROWS * (depth + tiles), HALO * depth + ROWS * tiles
    mask = inside_mask()
    zero = jnp.zeros(mask.shape, jnp.float32)
    signs[0] = zero
    signs[depth + 1] = zero
    above = from_above()
    kappa_pieces = (
        ((even_ref, thin, HALO, above), (own_ref, field), (odd_ref, thin, HALO, ~above)),
        ((swapped_ref, 0, HALO, above), (own_ref, field), (swapped_ref, thin // 2, HALO, ~above)),
    )
    sign_pieces = (
        (even_ref, 0, HALO, above),
        (own_ref, 0, ROWS, None),
        (odd_ref, 0, HALO, ~above),
    )
    unpack(depth, signs, half_diag, mask, sign_pieces, kappa_pieces)

    def down(k, carry):
        ratio, value = carry
        ratio = mask / (half_diag[k] - ratio)
        here = signs[k + 1]
        value = ratio * (here + value)
        lower[k] = ratio
        forward[k] = value
        image = half_diag[k] * here - (signs[k] + signs[k + 2]) - 0.5 * beside(here)
        own_signs[k] = here[OWN_ROWS]
        k_signs[k] = image[OWN_ROWS]
        return ratio, value

    lax.fori_loop(0, depth, down, (zero, zero), unroll=depth)


def basis_kernel(
    depth,
    near_diag,
    near_lower,
    near_forward,
    near_signs,
    own_far_ref,
    even_far_ref,
    odd_far_ref,
    swapped_ref,
    swapped_far_ref,
    basis_ref,
    image_ref,
    far_signs,
    far_k_signs,
    gram_ref,
    signs,
    far_diag,
    far_lower,
    upper,
    basis,
    forward,
    sides,
    backward,
    sums,
    masks,
):
    levels = 2 * depth
    mask = inside_mask()
    half_mask = 0.5 * mask
    masks[...] = half_mask
    zero = jnp.zeros(mask.shape, jnp.float32)
    own_zero = jnp.zeros((ROWS, LANES), jnp.float32)
    mine = lane_ids((ROWS, LANES)) < LANES // 2
    tiles = depth * EDGE // LANES
    field, thin = ROWS * (depth + tiles), HALO * depth + ROWS * tiles
    above = from_above()
    signs[0] = zero
    signs[0, OWN_ROWS] = near_signs[depth - 1]
    signs[depth + 1] = zero
    backward[levels] = zero
    upper[levels] = zero
    basis[levels] = zero
    kappa_pieces = (
        (
            (even_far_ref, thin, HALO, above),
            (own_far_ref, field, ROWS, None),
            (odd_far_ref, field, ROWS, None),
        ),
        (
            (swapped_far_ref, 0, HALO, above),
            (swapped_ref, thin, ROWS, None),
            (swapped_far_ref, thin // 2, ROWS, None),
        ),
    )
    sign_pieces = (
        (even_far_ref, 0, HALO, above),
        (own_far_ref, 0, ROWS, None),
        (odd_far_ref, 0, ROWS, None),
    )
    unpack(depth, signs, far_diag, mask, sign_pieces, kappa_pieces)

    def start_down(k, carry):
        ratio, value, from_end = carry
        ratio = mask / (far_diag[k] - ratio)
        here = signs[k + 1]
        value = ratio * (here + value)
        far_lower[k] = ratio
        forward[depth + k] = value
        other = depth - 1 - k
        from_end = mask / (far_diag[other] - from_end)
        upper[depth + other] = from_end
        image = far_diag[k] * here - (signs[k] + signs[k + 2]) - 0.5 * beside(here)
        far_signs[k] = here[OWN_ROWS]
        far_k_signs[k] = image[OWN_ROWS]
        return ratio, value, from_end

    start = (near_lower[depth - 1], near_forward[depth - 1], zero)
    carry = lax.fori_loop(0, depth, start_down, start, unroll=depth)

    def start_up_far(step, carry):
        k = depth - 1 - step
        solved, value = carry
        solved = forward[depth + k] + far_lower[k] * solved
        value = upper[depth + k] * (solved + value)
        backward[depth + k] = value
        return solved, value

    solved, value = lax.fori_loop(0, depth, start_up_far, (zero, zero), unroll=depth)

    def start_up_near(step, carry):
        k = depth - 1 - step
        ratio, solved, value = carry
        ratio = mask / (near_diag[k] - ratio)
        solved = near_forward[k] + near_lower[k] * solved
        value = ratio * (solved + value)
        upper[k] = ratio
        backward[k] = value
        return ratio, solved, value

    lax.fori_loop(0, depth, start_up_near, (carry[2], solved, value), unroll=depth)

    parts = (
        (0, near_diag, near_lower, lambda k: near_signs[k]),
        (depth, far_diag, far_lower, lambda k: signs[k + 1, OWN_ROWS]),
    )
    place = 0
    for index in range(ITERS):
        final = index + 1 == ITERS
        group_size = 2 * GROUP if final else GROUP

        def next_basis(k, previous, index=index):
            solved = backward[k] + upper[k] * previous
            if index == 0:
                value = solved
            elif SHIFTS[index - 1] == 0.0:
                value = solved
            elif SHIFTS[index - 1] == 1.0:
                value = basis[k] - solved
            elif SHIFTS[index - 1] == -1.0:
                value = basis[k] + solved
            else:
                value = SHIFTS[index - 1] * basis[k] - solved
            return solved, value

        solved, here = next_basis(0, zero)
        if not final:
            basis[0] = here
        carry = (solved, zero, here, zero)
        slots = list(range(place, place + index + 1)) + [len(PAIRS) + index]
        for offset, half_diag, lower, sign_of in parts:

            def down(group, carry):
                solved, above, here, value = carry
                added = [None] * len(slots)
                for step in range(group_size):
                    k = group * group_size + step
                    solved, below = next_basis(offset + k + 1, solved)
                    if not final:
                        basis[offset + k + 1] = below
                    side = beside(here)
                    image = half_diag[k] * here - (above + below) - masks[...] * side
                    if not final:
                        value = lower[k] * (beside(image) + value)
                        forward[offset + k] = value
                        sides[offset + k] = side
                    my_basis, my_image = here[OWN_ROWS], image[OWN_ROWS]
                    basis_ref[index, offset + k] = my_basis
                    image_ref[index, offset + k] = my_image
                    factors = [(image_ref[other, offset + k], my_image) for other in range(index)]
                    factors += [(my_image, my_image), (my_basis, sign_of(k))]
                    for slot, (a, b) in enumerate(factors):
                        product = a[:, :LANES] * b[:, :LANES] + a[:, LANES:] * b[:, LANES:]
                        added[slot] = product if step % GROUP == 0 else added[slot] + product
                        if step % GROUP == GROUP - 1:
                            at = (offset + group * group_size + step) // GROUP
                            sums[slots[slot], at] = added[slot]
                    above, here = here, below
                return solved, above, here, value

            carry = lax.fori_loop(0, depth // group_size, down, carry)
        place += index + 1
        if final:
            break
        carry = (zero, zero)
        for offset, half_diag, lower, sign_of in reversed(parts):

            def up(step, carry):
                k = depth - 1 - step
                solved, value = carry
                solved = forward[offset + k] + lower[k] * solved
                value = upper[offset + k] * ((sides[offset + k] + solved) + value)
                backward[offset + k] = value
                return solved, value

            carry = lax.fori_loop(0, depth, up, carry, unroll=4 * GROUP)

    ids = row_ids((ROWS, LANES))
    sides_of = [[], []]
    for block in range(SLOTS // ROWS):
        high, low = own_zero, own_zero
        for slot in range(block * ROWS, min((block + 1) * ROWS, COUNT)):
            pair = (sums[slot, 0], own_zero)
            for at in range(1, sums.shape[1]):
                total, rest = two_sum(pair[0], sums[slot, at])
                pair = (total, pair[1] + rest)
            pair = tuple(jnp.where(mine, part, 0.0) for part in pair)
            for shift in (4, 2, 1):
                pair = pair_add(pair, tuple(pltpu.roll(part, shift, 0) for part in pair))
            here = ids == slot - block * ROWS
            high, low = jnp.where(here, pair[0], high), jnp.where(here, pair[1], low)
        sides_of[0].append(high)
        sides_of[1].append(low)
    ones = jnp.ones((LANES, LANES), jnp.bfloat16)

    def lane_sum(part):
        return jnp.dot(part, ones, preferred_element_type=jnp.float32)

    high, low = (jnp.concatenate(blocks, axis=0) for blocks in sides_of)
    first, second, third = (lane_sum(part) for part in split_three(high))
    high, rest = two_sum(first, second)
    low = rest + (third + lane_sum(low.astype(jnp.bfloat16)))
    quarter = lane_ids((ROWS, LANES)) // (LANES // 4)
    tile = high[:ROWS]
    for place, block in enumerate((high[ROWS:], low[:ROWS], low[ROWS:])):
        tile = jnp.where(quarter == place + 1, block, tile)
    gram_ref[...] = tile


def terms_kernel(
    depth, basis_ref, image_ref, near_signs, near_k_signs, far_signs, far_k_signs, terms_ref
):
    level = lax.axis_index("level")
    half = LANES // 2
    mine = lane_ids((ROWS, LANES)) < half
    for offset, signs, k_signs in ((0, near_signs, near_k_signs), (depth, far_signs, far_k_signs)):

        def step(k, unused, offset=offset, signs=signs, k_signs=k_signs):
            z = offset + k
            target = jnp.where(level == 0, z, 2 * depth - 1 - z)
            sign, image = signs[k], k_signs[k]
            for index in range(ITERS):
                term = basis_ref[index, z] * image + image_ref[index, z] * sign
                terms_ref[index, target] = jnp.where(
                    mine, term[:, :LANES], pltpu.roll(term[:, LANES:], half, 1)
                )
            return unused

        if offset == 0:
            lax.fori_loop(0, depth - 1, step, 0, unroll=GROUP)
            sign, image = signs[depth - 1], k_signs[depth - 1] - far_signs[0]
            target = jnp.where(level == 0, depth - 1, depth)
            for index in range(ITERS):
                term = basis_ref[index, depth - 1] * image + image_ref[index, depth - 1] * sign
                terms_ref[index, target] = jnp.where(
                    mine, term[:, :LANES], pltpu.roll(term[:, LANES:], half, 1)
                )
        else:
            lax.fori_loop(0, depth, step, 0, unroll=GROUP)


def solve_small(high, low):
    def entry(index):
        return tuple(jnp.broadcast_to(part[index : index + 1], (ROWS, LANES)) for part in (high, low))

    gram = {}
    for place, (i, j) in enumerate(PAIRS):
        gram[i, j] = gram[j, i] = entry(place)
    right = [entry(len(PAIRS) + j) for j in range(ITERS)]
    work = {key: pair[0] for key, pair in gram.items()}
    ratios, inverses = {}, []
    for i in range(ITERS):
        pivot = work[i, i]
        good = pivot > 1e-7 * gram[i, i][0]
        inverses.append(jnp.where(good, 1.0 / jnp.where(good, pivot, 1.0), 0.0))
        for r in range(i + 1, ITERS):
            ratios[r, i] = work[r, i] * inverses[i]
        for r in range(i + 1, ITERS):
            for c in range(i + 1, r + 1):
                work[r, c] = work[c, r] = work[r, c] - ratios[r, i] * work[c, i]

    def solve(values):
        values = list(values)
        for i in range(ITERS):
            for r in range(i + 1, ITERS):
                values[r] = values[r] - ratios[r, i] * values[i]
        values = [value * inverse for value, inverse in zip(values, inverses)]
        for i in reversed(range(ITERS)):
            for r in range(i):
                values[r] = values[r] - ratios[i, r] * values[i]
        return values

    found = solve([pair[0] for pair in right])
    for unused in range(2):
        rest = []
        for i in range(ITERS):
            total = right[i]
            for j in range(ITERS):
                product, error = two_product(gram[i, j][0], found[j])
                total = pair_add(total, (-product, -(error + gram[i, j][1] * found[j])))
            rest.append(total[0] + total[1])
        found = [a + b for a, b in zip(found, solve(rest))]
    return found


def combine_kernel(depth, terms_ref, *refs):
    gram_refs, (keep_ref, send_ref) = refs[:-2], refs[-2:]
    half, width = LANES // 2, LANES // 4
    pairs = []
    for ref in gram_refs:
        for start in range(0, ref.shape[0], ROWS):
            tile = ref[start : start + ROWS]
            pairs.append((tile, pltpu.roll(tile, half, 1)))
    while len(pairs) > 1:
        merged = [pair_add(pairs[i], pairs[i + 1]) for i in range(0, len(pairs) - 1, 2)]
        pairs = merged + pairs[2 * len(merged) :]
    lanes = lane_ids((ROWS, LANES))

    def spread(part, block):
        part = jnp.where(lanes // width == block, part, 0.0)
        part = part + pltpu.roll(part, width, 1)
        return part + pltpu.roll(part, half, 1)

    found = solve_small(
        *(jnp.concatenate([spread(part, 0), spread(part, 1)], axis=0) for part in pairs[0])
    )
    core = lax.rem(lax.axis_index("probe"), 2)
    first_lanes = lanes % half < width
    pairs_deep = depth // 2

    def step(z, unused):
        for which in range(2):
            def total(k):
                value = found[0] * terms_ref[0, k]
                for j in range(1, ITERS):
                    value = value + found[j] * terms_ref[j, k]
                return value

            one = total(which * depth + z)
            two = total(which * depth + pairs_deep + z)
            low = jnp.where(first_lanes, one, pltpu.roll(two, width, 1))
            high = jnp.where(first_lanes, pltpu.roll(one, LANES - width, 1), two)
            keep_ref[which, z] = jnp.where(core == 0, low, high)
            send_ref[which, z] = jnp.where(core == 0, high, low)
        return unused

    lax.fori_loop(0, pairs_deep, step, 0, unroll=pairs_deep)


def observed_kernel(
    depth, probes, kappa_ref, observed_ref, even_ref, odd_ref, far_ref, factor_ref, data_ref
):
    level = lax.axis_index("level")
    tile = lax.axis_index("tile")
    last_tile = lax.axis_size("tile") - 1
    probe = lax.axis_index("probe")
    in_low = probe < probes // 2
    even = lax.rem(probe, 2) == 0
    width = LANES // 2
    lanes = lane_ids((ROWS, 2 * LANES))
    ids = row_ids((ROWS, LANES))
    base = even_ref.shape[0] - depth
    from_even = lax.rem(tile, 2) == 1

    def half(value):
        return jnp.where(in_low, value[..., :LANES], value[..., LANES:])

    def take(value):
        return jnp.where(even, value, pltpu.roll(value, width, 1))

    far_edge = far_ref[far_ref.shape[0] - ROWS :]
    factors, parts = [], []
    for z in range(depth):
        value = observed_ref[z]
        mine = half(value)
        y_sides = jnp.where(lanes > 0, pltpu.roll(value, 1, 1), 0.0) + jnp.where(
            lanes < 2 * LANES - 1, pltpu.roll(value, 2 * LANES - 1, 1), 0.0
        )
        first = even_ref[base + z : base + z + 1]
        second = odd_ref[base + z : base + z + 1]
        left, right = jnp.where(from_even, first, second), jnp.where(from_even, second, first)
        before = jnp.where(ids > 0, pltpu.roll(mine, 1, 0), jnp.where(tile > 0, left, 0.0))
        after = jnp.where(
            ids < ROWS - 1, pltpu.roll(mine, ROWS - 1, 0), jnp.where(tile < last_tile, right, 0.0)
        )
        above = half(observed_ref[z - 1]) if z > 0 else jnp.where(level > 0, far_edge, 0.0)
        below = half(observed_ref[z + 1]) if z < depth - 1 else jnp.where(level == 0, far_edge, 0.0)
        kappa = half(kappa_ref[z])
        k_observed = (
            (kappa + (4.0 + 2.0 * VERTICAL)) * mine
            - (before + after)
            - half(y_sides)
            - VERTICAL * (above + below)
        )
        factors.append(take(kappa * (0.5 / probes)))
        parts.append(take(kappa * (2.0 * mine * k_observed)))
    first_lanes = lane_ids((ROWS, LANES)) < width
    for ref, values in ((factor_ref, factors), (data_ref, parts)):
        for z in range(depth // 2):
            ref[z] = jnp.where(first_lanes, values[z], pltpu.roll(values[depth // 2 + z], width, 1))


def gradient_kernel(
    depth, trace_b_ref, trace_a_ref, straight_ref, factor_ref, data_ref, out_ref
):
    width = LANES // 2
    square = (LANES, LANES)
    lane = lane_ids(square)
    source = (width // 2) * (lane // width) + (lane % width) // 2 + width * (lane % 2)
    chosen = jnp.where(row_ids(square) == source, 1.0, 0.0).astype(jnp.bfloat16)
    stays = lax.axis_index("level") == 0
    traces = trace_a_ref[...] + jnp.where(stays, straight_ref[...], trace_b_ref[...])
    traces = pick(traces.reshape(-1, LANES), chosen).reshape(traces.shape)
    values = factor_ref[...] * traces - data_ref[...]
    for z in range(depth // 2):
        out_ref[z] = values[z, :, :width]
        out_ref[depth // 2 + z] = pltpu.roll(values[z], width, 1)[:, :width]


def whole(count):
    return [pl.BlockSpec(memory_space=pltpu.VMEM)] * count


def body(probe_bits, kappa_sq, observed):
    probes, tile_count = lax.axis_size("probe"), lax.axis_size("tile")
    unused, depth, rows, columns = probe_bits.shape
    assert probe_bits.shape[0] == 1 and lax.axis_size("level") == 2 and probes == 4
    assert rows == ROWS and columns == 2 * LANES and depth % (2 * LANES // EDGE) == 0
    params = pltpu.CompilerParams(vmem_limit_bytes=24 * 1024 * 1024)
    f32 = jnp.float32
    tiles = depth * EDGE // LANES
    field, thin = ROWS * (depth + tiles), HALO * depth + ROWS * tiles

    def block(count):
        return jax.ShapeDtypeStruct((count, LANES), f32)

    near_shape = block(thin + thin // 2 + depth)
    far_shape = block(field + field // 2 + ROWS)

    own_block, even_block, odd_block, cross_block, diagonal_block = pl.pallas_call(
        functools.partial(pack_kernel, depth),
        out_shape=(block(2 * field), near_shape, near_shape, far_shape, block(thin + thin // 2)),
        in_specs=[pl.BlockSpec(memory_space=pltpu.HBM)] * 3,
        out_specs=tuple(whole(5)),
        scratch_shapes=[
            pltpu.VMEM((depth, rows, columns), jnp.int32),
            pltpu.VMEM((depth, rows, columns), f32),
            pltpu.VMEM((depth, rows, columns), f32),
            pltpu.SemaphoreType.DMA((3,)),
        ],
        compiler_params=params,
        name="pack",
    )(
        *(
            pltpu.with_memory_space_constraint(value, pltpu.HBM)
            for value in (probe_bits[0], kappa_sq, observed)
        )
    )

    def swaps(pairs):
        return [way for a, b in pairs for way in ((a, b), (b, a))]

    def tile_swap(block, first, flip):
        partner = dict(swaps([(i, i + 1) for i in range(first, tile_count - 1, 2)]))

        def device(probe, tile, level):
            return (probe * tile_count + tile) * 2 + level

        ways = []
        for probe in range(probes):
            for tile in range(tile_count):
                for level in range(2):
                    if tile in partner:
                        target = device(probe, partner[tile], level ^ flip)
                    else:
                        target = device(probe ^ 1, tile, level)
                    ways.append((device(probe, tile, level), target))
        return lax.ppermute(block, ("probe", "tile", "level"), ways)

    own_far = lax.ppermute(cross_block, "level", swaps([(0, 1)]))
    even = tile_swap(even_block, 0, 0)
    odd = tile_swap(odd_block, 1, 0)
    odd_far = tile_swap(own_far, 1, 0)
    even_far = tile_swap(diagonal_block, 0, 1)

    quarter = jax.ShapeDtypeStruct((depth, ROWS, columns // probes), f32)
    paired = jax.ShapeDtypeStruct((depth // 2, ROWS, LANES), f32)
    factor, data = pl.pallas_call(
        functools.partial(observed_kernel, depth, probes),
        out_shape=(paired, paired),
        in_specs=whole(5),
        out_specs=tuple(whole(2)),
        compiler_params=params,
        name="observed",
    )(kappa_sq, observed, even, odd, own_far)

    def core_swap(*pieces):
        kappa = jnp.concatenate([piece[first : first + first // 2] for piece, first in pieces], axis=0)
        return lax.ppermute(kappa, "probe", swaps([(0, 1), (2, 3)]))

    swapped = core_swap((even, thin), (odd, thin), (own_far, field))
    levels = 2 * depth
    part = jax.ShapeDtypeStruct((depth, 3 * ROWS, 2 * LANES), f32)
    own_part = jax.ShapeDtypeStruct((depth, ROWS, 2 * LANES), f32)
    near_diag, near_lower, near_forward, near_signs, near_k_signs = pl.pallas_call(
        functools.partial(near_kernel, depth),
        out_shape=(part, part, part, own_part, own_part),
        in_specs=whole(4),
        out_specs=tuple(whole(5)),
        scratch_shapes=[pltpu.VMEM((depth + 2, 3 * ROWS, 2 * LANES), f32)],
        compiler_params=params,
        name="near",
    )(own_block, even, odd, swapped)

    swapped_far = core_swap((even_far, thin), (odd_far, field))
    padded = pltpu.VMEM((levels + 1, 3 * ROWS, 2 * LANES), f32)
    plain = pltpu.VMEM((levels, 3 * ROWS, 2 * LANES), f32)
    short = pltpu.VMEM((depth, 3 * ROWS, 2 * LANES), f32)
    fields = jax.ShapeDtypeStruct((ITERS, levels, ROWS, 2 * LANES), f32)
    basis, images, far_signs, far_k_signs, gram = pl.pallas_call(
        functools.partial(basis_kernel, depth),
        out_shape=(
            fields,
            fields,
            own_part,
            own_part,
            jax.ShapeDtypeStruct((ROWS, LANES), f32),
        ),
        in_specs=whole(9),
        out_specs=tuple(whole(5)),
        scratch_shapes=[
            pltpu.VMEM((depth + 2, 3 * ROWS, 2 * LANES), f32),
            short,
            short,
            padded,
            padded,
            plain,
            plain,
            padded,
            pltpu.VMEM((SLOTS, levels // GROUP, ROWS, LANES), f32),
            pltpu.VMEM((3 * ROWS, 2 * LANES), f32),
        ],
        compiler_params=params,
        name="basis",
    )(
        near_diag,
        near_lower,
        near_forward,
        near_signs,
        own_far,
        even_far,
        odd_far,
        swapped,
        swapped_far,
    )
    terms = pl.pallas_call(
        functools.partial(terms_kernel, depth),
        out_shape=jax.ShapeDtypeStruct((ITERS, levels, ROWS, LANES), f32),
        in_specs=whole(6),
        out_specs=pl.BlockSpec(memory_space=pltpu.VMEM),
        compiler_params=params,
        name="terms",
    )(basis, images, near_signs, near_k_signs, far_signs, far_k_signs)

    if tile_count in (2, 4):
        group = [gram] + [
            lax.ppermute(
                gram,
                ("tile", "level"),
                swaps([(i, i ^ k) for i in range(2 * tile_count) if i < i ^ k]),
            )
            for k in (1, 2, 3)
        ]
        partials = [jnp.concatenate(group, axis=0)]
        if tile_count == 4:
            partials.append(lax.ppermute(partials[0], "tile", swaps([(0, 2), (1, 3)])))
    else:
        partials = [lax.all_gather(gram, ("tile", "level"), axis=0, tiled=True)]
    piece = jax.ShapeDtypeStruct((2, depth // 2, ROWS, LANES), f32)
    keep, send = pl.pallas_call(
        functools.partial(combine_kernel, depth),
        out_shape=(piece, piece),
        in_specs=whole(1 + len(partials)),
        out_specs=tuple(whole(2)),
        compiler_params=params,
        name="combine",
    )(terms, *partials)

    summed = keep + lax.ppermute(send, "probe", swaps([(0, 1), (2, 3)]))
    level = lax.axis_index("level")
    turned = lax.dynamic_index_in_dim(summed, 1 - level, 0, keepdims=False)
    straight = lax.dynamic_index_in_dim(summed, level, 0, keepdims=False)

    def device(x, core, level):
        return (2 * x + core) * 2 + level

    chips = [(x, core) for x in range(2) for core in range(2)]
    trace_a = lax.ppermute(
        turned,
        ("probe", "level"),
        [(device(x, core, 0), device(x, core, 1)) for x, core in chips]
        + [(device(x, core, 1), device(1 - x, core, 0)) for x, core in chips],
    )
    trace_b = lax.ppermute(
        straight,
        ("probe", "level"),
        [(device(x, core, 1), device(1 - x, core, 1)) for x, core in chips]
        + [(device(x, core, 0), device(x, 1 - core, 0)) for x, core in chips],
    )
    return pl.pallas_call(
        functools.partial(gradient_kernel, depth),
        out_shape=quarter,
        in_specs=whole(5),
        out_specs=pl.BlockSpec(memory_space=pltpu.VMEM),
        compiler_params=params,
        name="gradient",
    )(trace_b, trace_a, straight, factor, data)


def solution(mesh):
    in_specs = (
        P("probe", "level", "tile", None),
        P("level", "tile", None),
        P("level", "tile", None),
    )
    out_specs = P("level", "tile", "probe")
    return jax.shard_map(body, mesh=mesh, in_specs=in_specs, out_specs=out_specs, check_vma=False)
```
